32 devices in a mesh: seq: 4 (over z), head: 2 (over x), wshard: 4 (over y, core).
Axes of the slice: x: 2, y: 2, z: 4, core: 2. Of those that a mesh axis runs over, the one named last changes fastest.
Arguments:
- prompt_states: bfloat16 [4, 256, 768], P('wshard', ('seq', 'head')), may hold values from -6 to 6
- content_states: bfloat16 [4, 2048, 768], P('wshard', ('seq', 'head')), may hold values from -6 to 6
- query_states: bfloat16 [4, 2048, 768], P('wshard', ('seq', 'head')), may hold values from -6 to 6
- visible_length: int32 [4, 2], P('wshard'), may hold values from 128 to 256, as said below
- start_offsets: int32 [4, 2], P('wshard'), may hold values from 0 to 63
- prompt_segments: int32 [4, 256], P('wshard'), may hold values from 0 to 3
- token_segments: int32 [4, 2048], P('wshard'), may hold values from 0 to 3
- order_ranks: int32 [4, 2048], P('wshard'), may hold values from 0 to 1023, as said below
- query_weights: bfloat16 [768, 768], P('wshard'), may hold values from -0.21875 to 0.21875
- key_weights: bfloat16 [768, 768], P('wshard'), may hold values from -0.21875 to 0.21875
- value_weights: bfloat16 [768, 768], P('wshard'), may hold values from -0.21875 to 0.21875
- output_weights: bfloat16 [768, 768], P('wshard'), may hold values from -1.75 to 1.75
- relative_weights: bfloat16 [768, 768], P('wshard'), may hold values from -0.3125 to 0.3125
- content_bias: bfloat16 [768], P('wshard'), may hold values from -3 to 3
- position_bias: bfloat16 [768], P('wshard'), may hold values from -3 to 3
- segment_bias: bfloat16 [768], P('wshard'), may hold values from -3 to 3
- segment_vectors: bfloat16 [2, 768], P(None, 'wshard'), may hold values from -5 to 5
- attention_gain: bfloat16 [768], P('wshard'), may hold values from 0.25 to 1.75
- attention_shift: bfloat16 [768], P('wshard'), may hold values from -2 to 2
- hidden_weights: bfloat16 [768, 3072], P('wshard'), may hold values from -0.21875 to 0.21875
- hidden_bias: bfloat16 [3072], P('wshard'), may hold values from -2 to 2
- return_weights: bfloat16 [3072, 768], P('wshard'), may hold values from -0.21875 to 0.21875
- return_bias: bfloat16 [768], P('wshard'), may hold values from -2 to 2
- final_gain: bfloat16 [768], P('wshard'), may hold values from 0.25 to 1.75
- final_shift: bfloat16 [768], P('wshard'), may hold values from -2 to 2
- content_upstream: bfloat16 [4, 2048, 768], P('wshard', ('seq', 'head')), may hold values from -6 to 6
- query_upstream: bfloat16 [4, 2048, 768], P('wshard', ('seq', 'head')), may hold values from -6 to 6
Outputs:
- content_output: bfloat16 [4, 2048, 768], P('wshard', ('seq', 'head'))
- query_output: bfloat16 [4, 2048, 768], P('wshard', ('seq', 'head'))
- prompt_gradient: bfloat16 [4, 256, 768], P('wshard', ('seq', 'head'))
- content_gradient: bfloat16 [4, 2048, 768], P('wshard', ('seq', 'head'))
- queries_gradient: bfloat16 [4, 2048, 768], P('wshard', ('seq', 'head'))
- gradient_query: float32 [768, 768], P('wshard')
- gradient_key: float32 [768, 768], P('wshard')
- gradient_value: float32 [768, 768], P('wshard')
- gradient_output: float32 [768, 768], P('wshard')
- gradient_relative: float32 [768, 768], P('wshard')
- gradient_content: float32 [768], P('wshard')
- gradient_position: float32 [768], P('wshard')
- gradient_segment: float32 [768], P('wshard')
- gradient_vectors: float32 [2, 768], P(None, 'wshard')
- gradient_scale: float32 [768], P('wshard')
- gradient_offset: float32 [768], P('wshard')
- gradient_hidden: float32 [768, 3072], P('wshard')
- gradient_inner: float32 [3072], P('wshard')
- gradient_return: float32 [3072, 768], P('wshard')
- gradient_outer: float32 [768], P('wshard')
- gradient_closing: float32 [768], P('wshard')
- gradient_ending: float32 [768], P('wshard')
The draws below stay inside these ranges and needn't reach their ends.
Inputs may be any that keep to these rules, and one draw needn't show every extreme that they name: `visible_length`: in each job one continuation, drawn from the seed, sees the whole prompt; the others see a prefix of at least half of it. `order_ranks`: the 1024 ranks of each continuation are a permutation of 0 to 1023.
All inputs are finite; a program needn't handle non-finite values.
Results may differ from the reference program's by a relative error of at most 0.03.
Values may be sent and summed in bfloat16 or wider, within the bound.
No kernel may reach another device: no remote copies, remote signals or barrier semaphores. Data moves between devices by JAX's collectives and lax.ppermute only.
A program may use at most 256 MiB of HBM per device.

```python
import jax
import jax.numpy as jnp
from jax import lax

D = 768
FF = 3072
HEADS = 12
HEAD_DIM = 64
OFFS = 64
LEN = 1024
CONTS = 2
TOKENS = 2048
PROMPT = 256
JOBS = 4
RTAB = 2368


def draw_visible_length(key, part):
    first_key = jax.random.fold_in(key, 11)
    second_key = jax.random.fold_in(key, 12)
    lengths = jax.random.randint(first_key, (JOBS, CONTS), PROMPT // 2, PROMPT + 1)
    chosen = jax.random.randint(second_key, (JOBS, 1), 0, CONTS)
    whole = jnp.arange(CONTS)[None, :] == chosen
    return jnp.where(whole, PROMPT, lengths).astype(jnp.int32)


def draw_order_ranks(key, part):
    key_list = jax.random.split(jax.random.fold_in(key, 21), JOBS * CONTS)
    orders = jax.vmap(lambda single: jax.random.permutation(single, LEN))(key_list)
    return orders.reshape(JOBS, CONTS * LEN).astype(jnp.int32)


def touch_ends(array, rng, smallest, high):
    extent = array.shape
    spot = [jax.random.randint(jax.random.fold_in(rng, axis), (), 0, extent[axis]) for axis in range(len(extent))]
    array = array.at[tuple(spot)].set(smallest)
    longest = extent.index(max(extent))
    spot[longest] = (spot[longest] + 1) % extent[longest]
    return array.at[tuple(spot)].set(high)


def shard_levels(key, dims, pieces, smallest, high):
    def one(axis_at, shards_of):
        steps = jax.random.uniform(jax.random.fold_in(jax.random.fold_in(key, 6), axis_at), (shards_of,), jnp.float32, smallest / len(pieces), high / len(pieces))
        return jnp.repeat(jnp.exp(steps), dims[axis_at] // shards_of).reshape((-1,) + (1,) * (len(dims) - axis_at - 1))

    gain = one(*pieces[0])
    for cut in pieces[1:]:
        gain = gain * one(*cut)
    return gain


def centred(stream_key, shape, deviation, limit, pieces=(), kind=jnp.bfloat16):
    gain = shard_levels(stream_key, shape, pieces, -0.22, 0.18) if pieces else 1.0
    values = jax.random.normal(stream_key, shape, jnp.float32) * deviation * gain
    return jnp.minimum(jnp.maximum(values, -limit), limit).astype(kind)


def setup_inputs(seed: int = 0) -> dict:
    keys = jax.random.split(jax.random.key(seed), 28)
    return {
        "prompt_states": centred(keys[0], (JOBS, PROMPT, D), 1.0, 6.0, ((0, 4), (1, 8))),
        "content_states": centred(keys[1], (JOBS, TOKENS, D), 1.0, 6.0, ((0, 4), (1, 8))),
        "query_states": centred(keys[2], (JOBS, TOKENS, D), 1.0, 6.0, ((0, 4), (1, 8))),
        "visible_length": draw_visible_length(jax.random.fold_in(keys[27], 71), 0),
        "start_offsets": touch_ends(jax.random.randint(keys[4], (JOBS, CONTS), 0, OFFS), jax.random.fold_in(keys[4], 1), 0, OFFS - 1).astype(jnp.int32),
        "prompt_segments": touch_ends(jax.random.randint(keys[5], (JOBS, PROMPT), 0, 4), jax.random.fold_in(keys[5], 1), 0, 3).astype(jnp.int32),
        "token_segments": touch_ends(jax.random.randint(keys[6], (JOBS, TOKENS), 0, 4), jax.random.fold_in(keys[6], 1), 0, 3).astype(jnp.int32),
        "order_ranks": draw_order_ranks(jax.random.fold_in(keys[27], 71), 0),
        "query_weights": centred(keys[8], (D, D), D ** -0.5, 0.21875, ((0, 4),)),
        "key_weights": centred(keys[9], (D, D), D ** -0.5, 0.21875, ((0, 4),)),
        "value_weights": centred(keys[10], (D, D), D ** -0.5, 0.21875, ((0, 4),)),
        "output_weights": centred(keys[11], (D, D), (D // 64) ** -0.5, 1.75, ((0, 4),)),
        "relative_weights": centred(keys[12], (D, D), (D // 2) ** -0.5, 0.3125, ((0, 4),)),
        "content_bias": centred(keys[13], (D,), 0.5, 3.0, ((0, 4),)),
        "position_bias": centred(keys[14], (D,), 0.5, 3.0, ((0, 4),)),
        "segment_bias": centred(keys[15], (D,), 0.5, 3.0, ((0, 4),)),
        "segment_vectors": centred(keys[16], (2, D), 1.0, 5.0, ((1, 4),)),
        "attention_gain": jnp.clip(1.0 + 0.15 * jax.random.normal(keys[17], (D,), jnp.float32), 0.25, 1.75).astype(jnp.bfloat16),
        "attention_shift": centred(keys[18], (D,), 0.3, 2.0, ((0, 4),)),
        "hidden_weights": centred(keys[19], (D, FF), D ** -0.5, 0.21875, ((0, 4),)),
        "hidden_bias": centred(keys[20], (FF,), 0.3, 2.0, ((0, 4),)),
        "return_weights": centred(keys[21], (FF, D), (FF // 4) ** -0.5, 0.21875, ((0, 4),)),
        "return_bias": centred(keys[22], (D,), 0.3, 2.0, ((0, 4),)),
        "final_gain": jnp.clip(1.0 + 0.15 * jax.random.normal(keys[23], (D,), jnp.float32), 0.25, 1.75).astype(jnp.bfloat16),
        "final_shift": centred(keys[24], (D,), 0.3, 2.0, ((0, 4),)),
        "content_upstream": centred(keys[25], (JOBS, TOKENS, D), 1.0, 6.0, ((0, 4), (1, 8))),
        "query_upstream": centred(keys[26], (JOBS, TOKENS, D), 1.0, 6.0, ((0, 4), (1, 8))),
    }


@jax.custom_vjp
def low(v):
    return lax.optimization_barrier(v.astype(jnp.bfloat16)).astype(jnp.float32)

@jax.custom_vjp
def low_back(v):
    return v

def low_keep(v):
    return (low(v), None)

def low_pass(kept, grad):
    return (grad,)

def back_keep(v):
    return (v, None)

def back_low(kept, grad):
    return (low(grad),)
low.defvjp(low_keep, low_pass)
low_back.defvjp(back_keep, back_low)
highest = lax.Precision.HIGHEST
negative = -1e+30
epsilon = 1e-06

def matmul(former, latter):
    return jnp.dot(former, latter, precision=highest, preferred_element_type=jnp.float32)

def layer_norm(values, gain_vector, shift_vector):
    center = values - lax.optimization_barrier(jnp.mean(values, axis=-1, keepdims=True))
    spread = lax.optimization_barrier(jnp.mean(center * center, axis=-1, keepdims=True))
    return center * lax.rsqrt(spread + epsilon) * gain_vector + shift_vector

def sinusoid(row_count, width_total, length):
    distance = (jnp.arange(row_count, dtype=jnp.int32) - length).astype(jnp.float32)
    frequency = jnp.power(10000.0, -2.0 * jnp.arange(width_total // 2, dtype=jnp.float32) / width_total)
    angles = distance[:, None] * frequency[None, :]
    return jnp.concatenate([jnp.sin(angles), jnp.cos(angles)], axis=1)

def split_heads(matrix):
    return matrix.reshape(matrix.shape[:-1] + (HEADS, HEAD_DIM))

def attend(queries, key_rows, value_rows, rel_table, biases, segment_pair, visible, band_index, differ):
    content_add, position_add, segment_add = biases
    with_content = low(queries + content_add)
    with_position = low(queries + position_add)
    with_segment = queries + segment_add
    content = jnp.einsum('qhe,khe->hqk', with_content, key_rows, precision=highest)
    banded = jnp.einsum('qhe,rhe->hqr', with_position, rel_table, precision=highest)
    heads_total = banded.shape[0]
    position = jnp.take_along_axis(banded, jnp.broadcast_to(band_index[None], (heads_total,) + band_index.shape), axis=2)
    same_term = jnp.einsum('qhe,he->hq', with_segment, segment_pair[0], precision=highest)
    other_term = jnp.einsum('qhe,he->hq', with_segment, segment_pair[1], precision=highest)
    segment = jnp.where(differ[None], other_term[:, :, None], same_term[:, :, None])
    scores = low_back((content + position + segment) * HEAD_DIM ** (-0.5))
    scores = jnp.where(visible[None], scores, negative)
    largest = lax.optimization_barrier(jnp.max(scores, axis=-1, keepdims=True))
    weights = jnp.exp(scores - largest)
    shares = weights / lax.optimization_barrier(jnp.sum(weights, axis=-1, keepdims=True))
    return jnp.einsum('hqk,khe->qhe', low(shares), value_rows, precision=highest)

def job_forward(params, prompt_rows, content_rows, query_rows, visible_length, start_offsets, prompt_segments, token_segments, order_ranks):
    query_weights, key_weights, value_weights, output_weights, relative_weights, content_bias, position_bias, segment_bias, segment_vectors, attention_gain, attention_shift, hidden_weights, hidden_bias, return_weights, return_bias, final_gain, final_shift = params
    content_query = low_back(low(matmul(content_rows, query_weights)))
    query_query = low_back(low(matmul(query_rows, query_weights)))
    source_rows = jnp.concatenate([prompt_rows, content_rows], axis=0)
    key_rows = low_back(low(matmul(source_rows, key_weights)))
    value_rows = low_back(low(matmul(source_rows, value_weights)))
    rel_table = split_heads(low(matmul(low(sinusoid(RTAB, D, LEN)), relative_weights)))
    biases = (content_bias.reshape(HEADS, HEAD_DIM), position_bias.reshape(HEADS, HEAD_DIM), segment_bias.reshape(HEADS, HEAD_DIM))
    segment_pair = segment_vectors.reshape(2, HEADS, HEAD_DIM)
    prompt_keys = split_heads(key_rows[:PROMPT])
    prompt_values = split_heads(value_rows[:PROMPT])
    token_keys = split_heads(key_rows[PROMPT:]).reshape(CONTS, LEN, HEADS, HEAD_DIM)
    token_values = split_heads(value_rows[PROMPT:]).reshape(CONTS, LEN, HEADS, HEAD_DIM)
    prompt_places = jnp.arange(PROMPT, dtype=jnp.int32)

    def one_sequence(entries):
        content_block, query_block, key_block, value_block, seen_length, offset_value, segment_block, rank_block = entries
        places = seen_length + offset_value + jnp.arange(LEN, dtype=jnp.int32)
        key_places = jnp.concatenate([prompt_places, places])
        band_index = jnp.clip(places[:, None] - key_places[None, :] + LEN, 0, RTAB - 1).astype(jnp.int32)
        prompt_seen = jnp.broadcast_to((prompt_places < seen_length)[None, :], (LEN, PROMPT))
        content_seen = jnp.concatenate([prompt_seen, rank_block[None, :] <= rank_block[:, None]], axis=1)
        query_seen = jnp.concatenate([prompt_seen, rank_block[None, :] < rank_block[:, None]], axis=1)
        differ = jnp.concatenate([prompt_segments[None, :] != segment_block[:, None], segment_block[None, :] != segment_block[:, None]], axis=1)
        all_keys = jnp.concatenate([prompt_keys, key_block], axis=0)
        all_values = jnp.concatenate([prompt_values, value_block], axis=0)
        content_mix = attend(content_block, all_keys, all_values, rel_table, biases, segment_pair, content_seen, band_index, differ)
        query_mix = attend(query_block, all_keys, all_values, rel_table, biases, segment_pair, query_seen, band_index, differ)
        return (content_mix.reshape(LEN, D), query_mix.reshape(LEN, D))
    mixtures = lax.map(jax.checkpoint(one_sequence), (split_heads(content_query).reshape(CONTS, LEN, HEADS, HEAD_DIM), split_heads(query_query).reshape(CONTS, LEN, HEADS, HEAD_DIM), token_keys, token_values, visible_length, start_offsets, token_segments.reshape(CONTS, LEN), order_ranks.reshape(CONTS, LEN)))
    content_mix = low_back(low(mixtures[0].reshape(TOKENS, D)))
    query_mix = low_back(low(mixtures[1].reshape(TOKENS, D)))
    outputs = []
    for stream_rows, mixture in ((content_rows, content_mix), (query_rows, query_mix)):
        branch = low_back(matmul(mixture, output_weights))
        middle = layer_norm(stream_rows + branch, attention_gain, attention_shift)
        inner_sum = low_back(matmul(low(middle), hidden_weights) + hidden_bias)
        active = low(jax.nn.gelu(inner_sum, approximate=True))
        returned = low_back(matmul(active, return_weights) + return_bias)
        outputs.append(layer_norm(middle + returned, final_gain, final_shift))
    return (outputs[0], outputs[1])

def reference(prompt_states, content_states, query_states, visible_length, start_offsets, prompt_segments, token_segments, order_ranks, query_weights, key_weights, value_weights, output_weights, relative_weights, content_bias, position_bias, segment_bias, segment_vectors, attention_gain, attention_shift, hidden_weights, hidden_bias, return_weights, return_bias, final_gain, final_shift, content_upstream, query_upstream):
    params = tuple((weight.astype(jnp.float32) for weight in (query_weights, key_weights, value_weights, output_weights, relative_weights, content_bias, position_bias, segment_bias, segment_vectors, attention_gain, attention_shift, hidden_weights, hidden_bias, return_weights, return_bias, final_gain, final_shift)))
    inputs = (prompt_states.astype(jnp.float32), content_states.astype(jnp.float32), query_states.astype(jnp.float32))

    def forward(params, inputs):
        content_list = []
        query_list = []
        for job_index in range(JOBS):
            content_out, query_out = job_forward(params, inputs[0][job_index], inputs[1][job_index], inputs[2][job_index], visible_length[job_index], start_offsets[job_index], prompt_segments[job_index], token_segments[job_index], order_ranks[job_index])
            content_list.append(content_out)
            query_list.append(query_out)
        return (jnp.stack(content_list), jnp.stack(query_list))
    (content_output, query_output), pullback = jax.vjp(forward, params, inputs)
    param_grads, input_grads = pullback((content_upstream.astype(jnp.float32), query_upstream.astype(jnp.float32)))
    grad_query, grad_key, grad_value, grad_output, grad_relative, grad_content, grad_position, grad_segment, grad_vectors, grad_scale, grad_offset, grad_hidden, grad_inner, grad_return, grad_outer, grad_closing, grad_ending = param_grads
    return (content_output.astype(jnp.bfloat16), query_output.astype(jnp.bfloat16), input_grads[0].astype(jnp.bfloat16), input_grads[1].astype(jnp.bfloat16), input_grads[2].astype(jnp.bfloat16), grad_query, grad_key, grad_value, grad_output, grad_relative, grad_content, grad_position, grad_segment, grad_vectors, grad_scale, grad_offset, grad_hidden, grad_inner, grad_return, grad_outer, grad_closing, grad_ending)
```

```python
from functools import partial

import jax
import jax.numpy as jnp
import numpy as np
from jax import lax
from jax.experimental import pallas as pl
from jax.experimental.pallas import tpu as pltpu
from jax.sharding import Mesh, PartitionSpec as P

D = 768
HEADS = 12
HEAD_DIM = 64
LEN = 1024
SEGMENTS = 4
TQ = 128

negative = -1e30
epsilon = 1e-06
scale_factor = HEAD_DIM ** (-0.5)
NT = (((1,), (1,)), ((), ()))
NN = (((1,), (0,)), ((), ()))
TN = (((0,), (0,)), ((), ()))

COL_HIGH = HEAD_DIM
COL_LOW = HEAD_DIM + SEGMENTS
COL_ONE = HEAD_DIM + 2 * SEGMENTS
COL_ONE_LOW = COL_ONE + 1
COL_MASK = COL_ONE + 2


def mm(a, b, dims=NN):
    return lax.dot_general(a, b, dims, preferred_element_type=jnp.float32)


def reverse_rows(x):
    groups = x.shape[0] // 8
    index = 7 - lax.broadcasted_iota(jnp.int32, (8, x.shape[1]), 0)
    return jnp.concatenate(
        [
            jnp.take_along_axis(x[8 * (groups - 1 - g) : 8 * (groups - g)], index, axis=0)
            for g in range(groups)
        ],
        axis=0,
    )


def prepare_keys(head, k_ref, v_ref, rt_ref, kinfo_ref, kaug, vaug, rt):
    cols = slice(head * HEAD_DIM, (head + 1) * HEAD_DIM)
    rows = k_ref.shape[0]
    lane = lax.broadcasted_iota(jnp.int32, (rows, HEAD_DIM), 1)
    segment = kinfo_ref[:, 0:1]
    hidden = kinfo_ref[:, 1:2]
    one_hot = ((lane == segment) | (lane - SEGMENTS == segment)) & (lane < 2 * SEGMENTS)
    ones = (lane == COL_ONE - HEAD_DIM) | (lane == COL_ONE_LOW - HEAD_DIM)
    extra = jnp.where(one_hot | ones, 1.0, 0.0)
    extra = jnp.where((lane == COL_MASK - HEAD_DIM) & (hidden > 0), negative, extra)
    kaug[:, :HEAD_DIM] = k_ref[:, cols]
    kaug[:, HEAD_DIM:] = extra.astype(jnp.bfloat16)
    vaug[:, :HEAD_DIM] = v_ref[:, cols]
    vaug[:, HEAD_DIM:] = jnp.where(lane < 2, 1.0, 0.0).astype(jnp.bfloat16)
    rt[...] = rt_ref[:, cols]


def query_terms(head, s, q_ref, bias_ref):
    cols = slice(head * HEAD_DIM, (head + 1) * HEAD_DIM)
    q = q_ref[s, :, cols].astype(jnp.float32)
    content = (q + bias_ref[0:1, cols]).astype(jnp.bfloat16).astype(jnp.float32)
    position = (q + bias_ref[1:2, cols]).astype(jnp.bfloat16).astype(jnp.float32)
    segment = q + bias_ref[2:3, cols]
    return content, position, segment


def forward_kernel(
    head, q_ref, k_ref, v_ref, rt_ref, bias_ref, qinfo_ref, kinfo_ref, rank_ref,
    p_ref, a_ref, kaug, vaug, rt, qaug,
):
    step = pl.program_id(0)
    keys = k_ref.shape[0]
    prompt = keys - LEN
    cols = slice(head * HEAD_DIM, (head + 1) * HEAD_DIM)

    @pl.when(step == 0)
    def _():
        prepare_keys(head, k_ref, v_ref, rt_ref, kinfo_ref, kaug, vaug, rt)

    start = pl.multiple_of(LEN - TQ - step * TQ, TQ)
    lane = lax.broadcasted_iota(jnp.int32, (TQ, HEAD_DIM), 1)
    segment_id = qinfo_ref[:, 0:1]
    rank = qinfo_ref[:, 1:2]
    table_p = rt[pl.ds(start, TQ + prompt), :]
    table_c = rt[pl.ds(pl.multiple_of(LEN + prompt + start, TQ), TQ + LEN), :]
    for s in range(2):
        content, position, with_segment = query_terms(head, s, q_ref, bias_ref)
        same = jnp.sum(with_segment * bias_ref[3:4, cols], axis=1, keepdims=True) * scale_factor
        other = jnp.sum(with_segment * bias_ref[4:5, cols], axis=1, keepdims=True) * scale_factor
        differ = same - other
        differ_high = differ.astype(jnp.bfloat16).astype(jnp.float32)
        other_high = other.astype(jnp.bfloat16).astype(jnp.float32)
        extra = jnp.where(lane == segment_id, differ_high, 0.0)
        extra = jnp.where(lane - SEGMENTS == segment_id, differ - differ_high, extra)
        extra = jnp.where(lane == COL_ONE - HEAD_DIM, other_high, extra)
        extra = jnp.where(lane == COL_ONE_LOW - HEAD_DIM, other - other_high, extra)
        extra = jnp.where(lane == COL_MASK - HEAD_DIM, 1.0, extra)
        qaug[:, :HEAD_DIM] = (content * scale_factor).astype(jnp.bfloat16)
        qaug[:, HEAD_DIM:] = extra.astype(jnp.bfloat16)
        scores = mm(qaug[...], kaug[...], NT)
        position = (position * scale_factor).astype(jnp.bfloat16)
        band_p = pltpu.roll(
            mm(position, table_p, NT), prompt + 1, axis=1, stride=1, stride_axis=0
        )
        band_c = pltpu.roll(mm(position, table_c, NT), LEN + 1, axis=1, stride=1, stride_axis=0)
        scores_p = scores[:, :prompt] + band_p[:, :prompt]
        scores_c = scores[:, prompt:] + band_c[:, :LEN]
        scores_c = jnp.where(rank_ref[0:1, :] <= rank - s, scores_c, negative)
        largest = jnp.maximum(
            jnp.max(scores_p, axis=1, keepdims=True), jnp.max(scores_c, axis=1, keepdims=True)
        )
        weights_p = jnp.exp(scores_p - largest)
        weights_c = jnp.exp(scores_c - largest)
        mixed = mm(weights_p.astype(jnp.bfloat16), vaug[:prompt, :])
        mixed += mm(weights_c.astype(jnp.bfloat16), vaug[prompt:, :])
        inverse = 1.0 / mixed[:, HEAD_DIM : HEAD_DIM + 1]
        wide = lax.broadcasted_iota(jnp.int32, (TQ, 2 * HEAD_DIM), 1)
        a_ref[s] = jnp.where(wide < HEAD_DIM, mixed * inverse, inverse)
        rows = slice(s * TQ, (s + 1) * TQ)
        p_ref[0, rows, :prompt] = reverse_rows(weights_p).astype(jnp.bfloat16)
        p_ref[0, rows, prompt:] = reverse_rows(weights_c).astype(jnp.bfloat16)


def backward_kernel(
    head, q_ref, k_ref, v_ref, rt_ref, bias_ref, qinfo_ref, kinfo_ref, p_ref, a_ref, ag_ref,
    dq_ref, dk_ref, dv_ref, dt_ref, sum_ref,
    kaug, vaug, rt, agaug, cw, cr, g_all, band_p, band_c, dk_acc, dv_acc, dt_acc,
):
    step = pl.program_id(0)
    keys = k_ref.shape[0]
    prompt = keys - LEN
    cols = slice(head * HEAD_DIM, (head + 1) * HEAD_DIM)

    @pl.when(step == 0)
    def _():
        prepare_keys(head, k_ref, v_ref, rt_ref, kinfo_ref, kaug, vaug, rt)
        dk_acc[...] = jnp.zeros_like(dk_acc)
        dv_acc[...] = jnp.zeros_like(dv_acc)
        dt_acc[...] = jnp.zeros_like(dt_acc)
        sum_ref[...] = jnp.zeros_like(sum_ref)

    start = pl.multiple_of(LEN - TQ - step * TQ, TQ)
    start_c = pl.multiple_of(LEN + prompt + start, TQ)
    lane = lax.broadcasted_iota(jnp.int32, (TQ, HEAD_DIM), 1)
    segment_id = qinfo_ref[:, 2:3]
    segments = []
    for s in range(2):
        rows = slice(s * TQ, (s + 1) * TQ)
        content, position, with_segment = query_terms(head, s, q_ref, bias_ref)
        cw[rows, :] = reverse_rows(content).astype(jnp.bfloat16)
        cr[rows, :] = reverse_rows(position).astype(jnp.bfloat16)
        segments.append(reverse_rows(with_segment))
        grad = ag_ref[0, s, :, cols].astype(jnp.float32)
        inverse = a_ref[s, :, HEAD_DIM : HEAD_DIM + 1] * scale_factor
        delta = jnp.sum(grad * a_ref[s, :, :HEAD_DIM], axis=1, keepdims=True) * inverse
        delta_high = delta.astype(jnp.bfloat16).astype(jnp.float32)
        extra = jnp.where(lane == 0, -delta_high, jnp.where(lane == 1, delta_high - delta, 0.0))
        agaug[rows, :HEAD_DIM] = reverse_rows(grad * inverse).astype(jnp.bfloat16)
        agaug[rows, HEAD_DIM:] = reverse_rows(extra).astype(jnp.bfloat16)
    share_grad = mm(agaug[...], vaug[...], NT)
    g_all[...] = (p_ref[0].astype(jnp.float32) * share_grad).astype(jnp.bfloat16)
    for s in range(2):
        rows = slice(s * TQ, (s + 1) * TQ)
        blank = jnp.zeros((TQ, TQ), jnp.bfloat16)
        wide_p = jnp.concatenate([g_all[rows, :prompt], blank], axis=1)
        wide_c = jnp.concatenate([g_all[rows, prompt:], blank], axis=1)
        band_p[rows, :] = pltpu.roll(wide_p, 0, axis=1, stride=1, stride_axis=0)
        band_c[rows, :] = pltpu.roll(wide_c, 0, axis=1, stride=1, stride_axis=0)
    dv_acc[...] += mm(agaug[:, :HEAD_DIM], p_ref[0], TN)
    dk_acc[...] += mm(cw[...], g_all[...], TN)
    dt_acc[:, pl.ds(start, TQ + prompt)] += mm(cr[...], band_p[...], TN)
    dt_acc[:, pl.ds(start_c, TQ + LEN)] += mm(cr[...], band_c[...], TN)
    query_content = mm(g_all[...], kaug[...])
    query_position = mm(band_p[...], rt[pl.ds(start, TQ + prompt), :])
    query_position += mm(band_c[...], rt[pl.ds(start_c, TQ + LEN), :])
    same_vector = bias_ref[3:4, cols]
    other_vector = bias_ref[4:5, cols]

    def add_row(row, value):
        sum_ref[row : row + 1, :] += jnp.sum(value, axis=0, keepdims=True)

    for s in range(2):
        rows = slice(s * TQ, (s + 1) * TQ)
        from_content = query_content[rows, :HEAD_DIM]
        extra = query_content[rows, HEAD_DIM:]
        hit = (lane == segment_id) & (lane < SEGMENTS)
        same = jnp.sum(jnp.where(hit, extra, 0.0), axis=1, keepdims=True)
        other = extra[:, COL_ONE - HEAD_DIM : COL_ONE - HEAD_DIM + 1] - same
        from_segment = same * same_vector + other * other_vector
        from_position = query_position[rows, :]
        total = reverse_rows(from_content + from_position + from_segment)
        dq_ref[0, s] = total.astype(jnp.bfloat16)
        add_row(0, from_content)
        add_row(1, from_position)
        add_row(2, from_segment)
        add_row(3, same * segments[s])
        add_row(4, other * segments[s])

    @pl.when(step == pl.num_programs(0) - 1)
    def _():
        dk_ref[...] = dk_acc[...].T.astype(jnp.bfloat16)
        dv_ref[...] = (dv_acc[...].T * HEAD_DIM**0.5).astype(jnp.bfloat16)
        dt_ref[...] = dt_acc[...].T.astype(jnp.bfloat16)


def whole(shape):
    return pl.BlockSpec(shape, lambda i: (0,) * len(shape))


def attend_forward(head, q, k, v, rt, bias, qinfo, kinfo, ranks):
    keys, width = k.shape
    table = rt.shape[0]
    steps = LEN // TQ
    return pl.pallas_call(
        partial(forward_kernel, head),
        grid=(steps,),
        in_specs=[
            pl.BlockSpec((2, TQ, width), lambda i: (0, i, 0)),
            whole((keys, width)),
            whole((keys, width)),
            whole((table, width)),
            whole(bias.shape),
            pl.BlockSpec((TQ, qinfo.shape[1]), lambda i: (i, 0)),
            whole(kinfo.shape),
            whole(ranks.shape),
        ],
        out_specs=[
            pl.BlockSpec((1, 2 * TQ, keys), lambda i: (i, 0, 0)),
            pl.BlockSpec((2, TQ, 2 * HEAD_DIM), lambda i: (0, i, 0)),
        ],
        out_shape=[
            jax.ShapeDtypeStruct((steps, 2 * TQ, keys), jnp.bfloat16),
            jax.ShapeDtypeStruct((2, LEN, 2 * HEAD_DIM), jnp.float32),
        ],
        scratch_shapes=[
            pltpu.VMEM((keys, 2 * HEAD_DIM), jnp.bfloat16),
            pltpu.VMEM((keys, 2 * HEAD_DIM), jnp.bfloat16),
            pltpu.VMEM((table, HEAD_DIM), jnp.bfloat16),
            pltpu.VMEM((TQ, 2 * HEAD_DIM), jnp.bfloat16),
        ],
        compiler_params=pltpu.CompilerParams(vmem_limit_bytes=48 * 2**20),
        cost_estimate=pl.CostEstimate(
            flops=6 * 2 * LEN * keys * 256, bytes_accessed=2 * LEN * keys * 2, transcendentals=2 * LEN * keys
        ),
        name="attend_forward",
    )(q, k, v, rt, bias, qinfo, kinfo, ranks)


def attend_backward(head, q, k, v, rt, bias, qinfo, kinfo, p, a, ag):
    keys, width = k.shape
    table = rt.shape[0]
    steps = LEN // TQ
    prompt = keys - LEN
    per = ag.shape[2] // TQ
    return pl.pallas_call(
        partial(backward_kernel, head),
        grid=(steps,),
        in_specs=[
            pl.BlockSpec((2, TQ, width), lambda i: (0, i, 0)),
            whole((keys, width)),
            whole((keys, width)),
            whole((table, width)),
            whole(bias.shape),
            pl.BlockSpec((TQ, qinfo.shape[1]), lambda i: (i, 0)),
            whole(kinfo.shape),
            pl.BlockSpec((1, 2 * TQ, keys), lambda i: (i, 0, 0)),
            pl.BlockSpec((2, TQ, 2 * HEAD_DIM), lambda i: (0, i, 0)),
            pl.BlockSpec((1, 2, TQ, width), lambda i: (i // per, 0, i % per, 0)),
        ],
        out_specs=[
            pl.BlockSpec((1, 2, TQ, HEAD_DIM), lambda i: (i // per, 0, i % per, 0)),
            whole((keys, HEAD_DIM)),
            whole((keys, HEAD_DIM)),
            whole((table, HEAD_DIM)),
            whole((8, HEAD_DIM)),
        ],
        out_shape=[
            jax.ShapeDtypeStruct(ag.shape[:3] + (HEAD_DIM,), jnp.bfloat16),
            jax.ShapeDtypeStruct((keys, HEAD_DIM), jnp.bfloat16),
            jax.ShapeDtypeStruct((keys, HEAD_DIM), jnp.bfloat16),
            jax.ShapeDtypeStruct((table, HEAD_DIM), jnp.bfloat16),
            jax.ShapeDtypeStruct((8, HEAD_DIM), jnp.float32),
        ],
        scratch_shapes=[
            pltpu.VMEM((keys, 2 * HEAD_DIM), jnp.bfloat16),
            pltpu.VMEM((keys, 2 * HEAD_DIM), jnp.bfloat16),
            pltpu.VMEM((table, HEAD_DIM), jnp.bfloat16),
            pltpu.VMEM((2 * TQ, 2 * HEAD_DIM), jnp.bfloat16),
            pltpu.VMEM((2 * TQ, HEAD_DIM), jnp.bfloat16),
            pltpu.VMEM((2 * TQ, HEAD_DIM), jnp.bfloat16),
            pltpu.VMEM((2 * TQ, keys), jnp.bfloat16),
            pltpu.VMEM((2 * TQ, TQ + prompt), jnp.bfloat16),
            pltpu.VMEM((2 * TQ, TQ + LEN), jnp.bfloat16),
            pltpu.VMEM((HEAD_DIM, keys), jnp.float32),
            pltpu.VMEM((HEAD_DIM, keys), jnp.float32),
            pltpu.VMEM((HEAD_DIM, table), jnp.float32),
        ],
        compiler_params=pltpu.CompilerParams(vmem_limit_bytes=48 * 2**20),
        cost_estimate=pl.CostEstimate(
            flops=12 * 2 * LEN * keys * 256, bytes_accessed=2 * LEN * keys * 2, transcendentals=0
        ),
        name="attend_backward",
    )(q, k, v, rt, bias, qinfo, kinfo, p, a, ag)


def axes_size(axes):
    size = 1
    for name in axes:
        size *= lax.axis_size(name)
    return size


def flat_index(axes):
    index = 0
    for name in axes:
        index = index * lax.axis_size(name) + lax.axis_index(name)
    return index


def swap(x, axes, mask):
    return lax.ppermute(x, axes, [(i, i ^ mask) for i in range(axes_size(axes))])


def gather(x, axes, order=None):
    count = axes_size(axes)
    index = flat_index(axes)
    pieces = {0: x}
    bits = list(range(count.bit_length() - 1))
    for bit in reversed(bits) if order is None else order:
        for mask in list(pieces):
            pieces[mask | 1 << bit] = swap(pieces[mask], axes, 1 << bit)
    result = jnp.zeros((count,) + x.shape, x.dtype)
    for mask, piece in pieces.items():
        result = lax.dynamic_update_slice(
            result, piece[None], (index ^ mask,) + (0,) * x.ndim
        )
    return result


def pick(x, index):
    return lax.dynamic_index_in_dim(x, index, 0, keepdims=False)


def scatter_sum(x, axes):
    count = axes_size(axes)
    index = flat_index(axes)
    for bit in range(count.bit_length() - 1):
        x = x.reshape((x.shape[0] // 2, 2) + x.shape[1:])
        own = index >> bit & 1
        kept = lax.dynamic_index_in_dim(x, own, 1, keepdims=False)
        sent = lax.dynamic_index_in_dim(x, 1 - own, 1, keepdims=False)
        x = kept.astype(jnp.float32) + swap(sent.astype(jnp.bfloat16), axes, 1 << bit).astype(
            jnp.float32
        )
    return x[0]


def total_sum(x, stages):
    taken = []
    for axes, mask in stages:
        bit = mask.bit_length() - 1
        own = flat_index(axes) >> bit & 1
        x = x.reshape((2, x.shape[0] // 2) + x.shape[1:])
        sent = pick(x, 1 - own).astype(jnp.bfloat16)
        x = pick(x, own).astype(jnp.float32) + swap(sent, axes, mask).astype(jnp.float32)
        taken.append((axes, mask, own))
    x = x.astype(jnp.bfloat16)
    for axes, mask, own in reversed(taken):
        other = swap(x, axes, mask)
        pair = jnp.zeros((2,) + x.shape, x.dtype)
        pair = lax.dynamic_update_slice(pair, x[None], (own,) + (0,) * x.ndim)
        pair = lax.dynamic_update_slice(pair, other[None], (1 - own,) + (0,) * x.ndim)
        x = pair.reshape((2 * x.shape[0],) + x.shape[1:])
    return x


def bit_stages(axes):
    return [((name,), 1 << bit) for name in axes for bit in range(lax.axis_size(name).bit_length() - 1)]


def layer_norm(values, gain_vector, shift_vector):
    center = values - jnp.mean(values, axis=-1, keepdims=True)
    spread = jnp.mean(center * center, axis=-1, keepdims=True)
    return center * lax.rsqrt(spread + epsilon) * gain_vector + shift_vector


def project(rows_in, weight):
    return jnp.dot(rows_in, weight, preferred_element_type=jnp.float32)


def back_through(grad_rows, weight):
    return jnp.einsum("rc,dc->rd", grad_rows, weight, preferred_element_type=jnp.float32)


def outer_sum(rows_in, grad_rows):
    return jnp.einsum("rd,rc->dc", rows_in, grad_rows, preferred_element_type=jnp.float32)


def sinusoid_rows(first, rows):
    frequency = jnp.asarray(
        np.power(10000.0, -2.0 * np.arange(D // 2) / D).astype(np.float32)
    )
    fine = jnp.arange(64, dtype=jnp.float32)[:, None] * frequency
    coarse = (first - 64 * jnp.arange(rows // 64, dtype=jnp.int32)).astype(jnp.float32)
    coarse = coarse[:, None] * frequency
    fs, fc = jnp.sin(fine)[None], jnp.cos(fine)[None]
    cs, cc = jnp.sin(coarse)[:, None], jnp.cos(coarse)[:, None]
    both = jnp.concatenate([cs * fc - cc * fs, cc * fc + cs * fs], axis=-1)
    return both.reshape(rows, D).astype(jnp.bfloat16)


GROUP = ("half", "head")
JOB = ("cont", "half", "head")


def per_device(
    prompt_states, content_states, query_states, visible_length, start_offsets,
    prompt_segments, token_segments, order_ranks,
    query_weights, key_weights, value_weights, output_weights, relative_weights,
    content_bias, position_bias, segment_bias, segment_vectors,
    attention_gain, attention_shift, hidden_weights, hidden_bias, return_weights, return_bias,
    final_gain, final_shift, content_upstream, query_upstream,
):
    members = axes_size(GROUP)
    member = flat_index(GROUP)
    shards = lax.axis_size("wshard")
    shard = lax.axis_index("wshard")
    chapter = lax.axis_index("cont")
    width = D // members
    local_heads = HEADS // members
    prompt_rows = prompt_states[0]
    content_rows = content_states[0]
    query_rows = query_states[0]
    tokens = content_rows.shape[0]
    prompt_part = prompt_rows.shape[0]
    prompt_total = prompt_segments.shape[1]
    keys = prompt_total + LEN
    rows_w = query_weights.shape[0]

    def columns(x):
        return lax.dynamic_slice_in_dim(x, member * width, width, x.ndim - 1)

    first_weights = jnp.stack(
        [columns(w) for w in (query_weights, key_weights, value_weights, relative_weights)], axis=0
    )
    small = jnp.concatenate(
        [
            jnp.stack([content_bias, position_bias, segment_bias]),
            segment_vectors,
            jnp.stack([attention_gain, attention_shift, return_bias, final_gain, final_shift]),
            hidden_bias.reshape(-1, rows_w),
        ],
        axis=0,
    )
    first_full = gather(first_weights, ("wshard",))
    small_full = gather(small, ("wshard",))
    content_all = gather(content_rows, GROUP, (1, 0)).reshape(LEN, D)
    query_all = gather(query_rows, GROUP, (0, 1)).reshape(LEN, D)
    prompt_all = gather(prompt_rows, JOB).reshape(prompt_total, D)
    output_full = gather(output_weights, ("wshard",)).reshape(D, D)
    hidden_full = gather(hidden_weights, ("wshard",)).reshape(D, -1)
    return_full = gather(return_weights, ("wshard",)).reshape(-1, D)
    query_full = gather(query_weights, ("wshard",)).reshape(D, D)
    key_full = gather(key_weights, ("wshard",)).reshape(D, D)
    value_full = gather(value_weights, ("wshard",)).reshape(D, D)

    vectors = jnp.transpose(small_full, (1, 0, 2))
    inner_full = small_full[:, 10:].reshape(-1).astype(jnp.float32)
    vectors = vectors[:10].reshape(10, D).astype(jnp.float32)
    head_bias = jnp.concatenate([columns(vectors[:5]), jnp.zeros((3, width), jnp.float32)])
    attention_scale, attention_offset, outer_full, final_scale, final_offset = vectors[5:]

    seen = pick(visible_length[0], chapter)
    base = seen + pick(start_offsets[0], chapter)
    segments = lax.dynamic_slice_in_dim(token_segments[0], chapter * LEN, LEN)
    ranks = lax.dynamic_slice_in_dim(order_ranks[0], chapter * LEN, LEN)
    reversed_segments = jnp.flip(segments.reshape(-1, TQ), 1).reshape(-1)
    qinfo = jnp.stack([segments, ranks, reversed_segments, segments], axis=1)
    key_segments = jnp.concatenate([prompt_segments[0], segments])
    hidden_keys = (jnp.arange(keys, dtype=jnp.int32) < prompt_total) & (
        jnp.arange(keys, dtype=jnp.int32) >= seen
    )
    kinfo = jnp.stack([key_segments, hidden_keys.astype(jnp.int32)], axis=1)
    rank_row = ranks[None]
    positions = jnp.concatenate(
        [
            sinusoid_rows(base + LEN - 1, LEN + prompt_total),
            sinusoid_rows(jnp.int32(LEN - 1), 2 * LEN),
        ]
    )

    first_full = jnp.transpose(first_full, (1, 0, 2, 3)).reshape(4, D, width)
    streams_all = jnp.concatenate([content_all, query_all])
    sources_all = jnp.concatenate([prompt_all, content_all])
    q = project(streams_all, first_full[0]).astype(jnp.bfloat16).reshape(2, LEN, width)
    k = project(sources_all, first_full[1]).astype(jnp.bfloat16)
    v = project(sources_all, first_full[2]).astype(jnp.bfloat16)
    rt = project(positions, first_full[3]).astype(jnp.bfloat16)

    forward = [
        attend_forward(h, q, k, v, rt, head_bias, qinfo, kinfo, rank_row)
        for h in range(local_heads)
    ]
    mixture = jnp.concatenate([a[:, :, :HEAD_DIM] for _, a in forward], axis=-1)
    mixture = jnp.transpose(
        mixture.astype(jnp.bfloat16).reshape(2, members, tokens, width), (1, 0, 2, 3)
    )
    mixture = lax.all_to_all(mixture, GROUP, 0, 0, tiled=True)
    mixed_flat = jnp.transpose(mixture, (1, 2, 0, 3)).reshape(2 * tokens, D)

    streams_in = jnp.concatenate([content_rows, query_rows], axis=0).astype(jnp.float32)
    branch = project(mixed_flat, output_full)
    middle, norm_back = jax.vjp(
        layer_norm, streams_in + branch, attention_scale, attention_offset
    )
    inner_in = middle.astype(jnp.bfloat16)
    inner_sum = project(inner_in, hidden_full) + inner_full
    active, gelu_back = jax.vjp(partial(jax.nn.gelu, approximate=True), inner_sum)
    active_low = active.astype(jnp.bfloat16)
    returned = project(active_low, return_full) + outer_full
    normed, final_back = jax.vjp(layer_norm, middle + returned, final_scale, final_offset)
    upstream = jnp.concatenate([content_upstream[0], query_upstream[0]], axis=0).astype(jnp.float32)
    sum_grad, closing_grad, ending_grad = final_back(upstream)
    returned_grad = sum_grad.astype(jnp.bfloat16)
    outer_grad = jnp.sum(returned_grad.astype(jnp.float32), axis=0)
    active_grad = back_through(returned_grad, return_full)
    inner_grad = gelu_back(active_grad)[0].astype(jnp.bfloat16)
    inner_bias_grad = jnp.sum(inner_grad.astype(jnp.float32), axis=0)
    middle_grad = sum_grad + back_through(inner_grad, hidden_full)
    residual_grad, scale_grad, offset_grad = norm_back(middle_grad)
    branch_grad = residual_grad.astype(jnp.bfloat16)
    mixed_grad = back_through(branch_grad, output_full).astype(jnp.bfloat16)
    grad_out = jnp.transpose(mixed_grad.reshape(2, tokens, members, width), (2, 0, 1, 3))
    grad_out = lax.all_to_all(grad_out, GROUP, 0, 0, tiled=True)

    return_grad = outer_sum(active_low, returned_grad)
    hidden_grad = outer_sum(inner_in, inner_grad)
    output_grad = outer_sum(mixed_flat, branch_grad)
    stages = bit_stages(("head", "half", "cont"))
    return_part = scatter_sum(return_grad.reshape(shards, -1, D), ("wshard",))
    hidden_part = scatter_sum(hidden_grad.reshape(shards, rows_w, -1), ("wshard",))
    output_part = scatter_sum(output_grad.reshape(shards, rows_w, D), ("wshard",))
    return_total = total_sum(return_part, stages).astype(jnp.float32)
    hidden_total = total_sum(hidden_part, stages).astype(jnp.float32)
    output_total = total_sum(output_part, stages).astype(jnp.float32)

    backward = [
        attend_backward(
            h, q, k, v, rt, head_bias, qinfo, kinfo, forward[h][0], forward[h][1], grad_out
        )
        for h in range(local_heads)
    ]
    dq = jnp.concatenate([b[0] for b in backward], axis=-1)
    dk = jnp.concatenate([b[1] for b in backward], axis=-1)
    dv = jnp.concatenate([b[2] for b in backward], axis=-1)
    dt = jnp.concatenate([b[3] for b in backward], axis=-1)
    sums = jnp.concatenate([b[4] for b in backward], axis=-1)

    token_back = jnp.concatenate(
        [
            dq,
            dk[prompt_total:].reshape(members, 1, tokens, width),
            dv[prompt_total:].reshape(members, 1, tokens, width),
        ],
        axis=1,
    )
    token_back = lax.all_to_all(token_back, GROUP, 0, 0, tiled=True)
    token_back = jnp.transpose(token_back, (1, 2, 0, 3)).reshape(4, tokens, D)
    chapters = lax.axis_size("cont")
    prompt_back = jnp.stack([dk[:prompt_total], dv[:prompt_total]]).reshape(
        2, chapters * members, prompt_part, width
    )
    prompt_back = lax.all_to_all(jnp.transpose(prompt_back, (1, 0, 2, 3)), JOB, 0, 0, tiled=True)
    prompt_back = jnp.sum(
        prompt_back.reshape(chapters, members, 2, prompt_part, width).astype(jnp.float32), axis=0
    ).astype(jnp.bfloat16)
    prompt_back = jnp.transpose(prompt_back, (1, 2, 0, 3)).reshape(2, prompt_part, D)

    dq_rows = jnp.transpose(dq, (1, 0, 2, 3)).reshape(2 * LEN, width)
    head_grads = jnp.concatenate(
        [
            outer_sum(streams_all, dq_rows),
            outer_sum(sources_all, dk),
            outer_sum(sources_all, dv),
            outer_sum(positions, dt),
        ],
        axis=1,
    ).reshape(shards, rows_w, 4 * width)

    placed = lax.dynamic_update_slice_in_dim(
        jnp.zeros((5, D), jnp.float32), sums[:5], member * width, 1
    )
    token_sums = jnp.stack([scale_grad, offset_grad, outer_grad, closing_grad, ending_grad])
    small_grads = jnp.concatenate([placed, token_sums]).reshape(10, shards, rows_w)
    small_grads = jnp.transpose(small_grads, (1, 0, 2)).reshape(shards, -1)
    small_grads = jnp.concatenate([small_grads, inner_bias_grad.reshape(shards, -1)], axis=1)
    unit = 8 * lax.axis_size("cont")
    small_rows = rows_w - (-small_grads.shape[1] // (4 * width))
    small_rows = -(-small_rows // unit) * unit - rows_w
    small_grads = jnp.pad(
        small_grads, ((0, 0), (0, small_rows * 4 * width - small_grads.shape[1]))
    ).reshape(shards, small_rows, 4 * width)
    head_part = scatter_sum(jnp.concatenate([head_grads, small_grads], axis=1), ("wshard",))
    head_part = total_sum(head_part, bit_stages(("cont",)))
    head_total = gather(head_part, GROUP).astype(jnp.float32)
    weights_total = jnp.transpose(
        head_total[:, :rows_w].reshape(members, rows_w, 4, width), (2, 1, 0, 3)
    ).reshape(4, rows_w, D)
    small_total = jnp.sum(head_total[:, rows_w:], axis=0).reshape(-1)
    vector_total = small_total[: 10 * rows_w].reshape(10, rows_w)
    inner_total = small_total[10 * rows_w : 10 * rows_w + inner_bias_grad.shape[0] // shards]

    content_grad = (
        residual_grad[:tokens]
        + back_through(token_back[0], query_full)
        + back_through(token_back[2], key_full)
        + back_through(token_back[3], value_full)
    )
    queries_grad = residual_grad[tokens:] + back_through(token_back[1], query_full)
    prompt_grad = back_through(prompt_back[0], key_full) + back_through(prompt_back[1], value_full)
    return (
        normed[:tokens].astype(jnp.bfloat16)[None],
        normed[tokens:].astype(jnp.bfloat16)[None],
        prompt_grad.astype(jnp.bfloat16)[None],
        content_grad.astype(jnp.bfloat16)[None],
        queries_grad.astype(jnp.bfloat16)[None],
        weights_total[0],
        weights_total[1],
        weights_total[2],
        output_total,
        weights_total[3],
        vector_total[0],
        vector_total[1],
        vector_total[2],
        vector_total[3:5],
        vector_total[5],
        vector_total[6],
        hidden_total,
        inner_total,
        return_total,
        vector_total[7],
        vector_total[8],
        vector_total[9],
    )


def solution(mesh):
    rows = P("wshard", JOB, None)
    job = P("wshard", None)
    matrix = P("wshard", None)
    vector = P("wshard")
    pair = P(None, "wshard")
    in_specs = (
        (rows,) * 3 + (job,) * 5 + (matrix,) * 5 + (vector,) * 3 + (pair,)
        + (vector, vector, matrix, vector, matrix, vector, vector, vector, rows, rows)
    )
    out_specs = (
        (rows,) * 5 + (matrix,) * 5 + (vector,) * 3 + (pair,)
        + (vector, vector, matrix, vector, matrix, vector, vector, vector)
    )

    def run(*arguments):
        seq_count, head_count, shard_count = mesh.devices.shape
        tokens = arguments[1].shape[1] // (seq_count * head_count)
        halves = LEN // (tokens * head_count)
        split = Mesh(
            mesh.devices.reshape(seq_count // halves, halves, head_count, shard_count),
            ("cont", "half", "head", "wshard"),
        )
        return jax.shard_map(
            per_device, mesh=split, in_specs=in_specs, out_specs=out_specs, check_vma=False
        )(*arguments)

    return run
```

```python
from functools import partial

import jax
import jax.numpy as jnp
import numpy as np
from jax import lax
from jax.experimental import pallas as pl
from jax.experimental.pallas import tpu as pltpu
from jax.sharding import Mesh, PartitionSpec as P

D = 768
HEADS = 12
HEAD_DIM = 64
LEN = 1024
SEGMENTS = 4
TQ = 128

negative = -1e30
epsilon = 1e-06
scale_factor = HEAD_DIM ** (-0.5)
NT = (((1,), (1,)), ((), ()))
NN = (((1,), (0,)), ((), ()))
TN = (((0,), (0,)), ((), ()))

COL_HIGH = HEAD_DIM
COL_LOW = HEAD_DIM + SEGMENTS
COL_ONE = HEAD_DIM + 2 * SEGMENTS
COL_ONE_LOW = COL_ONE + 1
COL_MASK = COL_ONE + 2


def mm(a, b, dims=NN):
    return lax.dot_general(a, b, dims, preferred_element_type=jnp.float32)


def reverse_rows(x):
    groups = x.shape[0] // 8
    index = 7 - lax.broadcasted_iota(jnp.int32, (8, x.shape[1]), 0)
    return jnp.concatenate(
        [
            jnp.take_along_axis(x[8 * (groups - 1 - g) : 8 * (groups - g)], index, axis=0)
            for g in range(groups)
        ],
        axis=0,
    )


def prepare_keys(head, k_ref, v_ref, rt_ref, kinfo_ref, kaug, vaug, rt):
    cols = slice(head * HEAD_DIM, (head + 1) * HEAD_DIM)
    rows = k_ref.shape[0]
    lane = lax.broadcasted_iota(jnp.int32, (rows, HEAD_DIM), 1)
    segment = kinfo_ref[:, 0:1]
    hidden = kinfo_ref[:, 1:2]
    one_hot = ((lane == segment) | (lane - SEGMENTS == segment)) & (lane < 2 * SEGMENTS)
    ones = (lane == COL_ONE - HEAD_DIM) | (lane == COL_ONE_LOW - HEAD_DIM)
    extra = jnp.where(one_hot | ones, 1.0, 0.0)
    extra = jnp.where((lane == COL_MASK - HEAD_DIM) & (hidden > 0), negative, extra)
    kaug[:, :HEAD_DIM] = k_ref[:, cols]
    kaug[:, HEAD_DIM:] = extra.astype(jnp.bfloat16)
    vaug[:, :HEAD_DIM] = v_ref[:, cols]
    vaug[:, HEAD_DIM:] = jnp.where(lane < 2, 1.0, 0.0).astype(jnp.bfloat16)
    rt[...] = rt_ref[:, cols]


def query_terms(head, s, q_ref, bias_ref):
    cols = slice(head * HEAD_DIM, (head + 1) * HEAD_DIM)
    q = q_ref[s, :, cols].astype(jnp.float32)
    content = (q + bias_ref[0:1, cols]).astype(jnp.bfloat16).astype(jnp.float32)
    position = (q + bias_ref[1:2, cols]).astype(jnp.bfloat16).astype(jnp.float32)
    segment = q + bias_ref[2:3, cols]
    return content, position, segment


def forward_kernel(
    q_ref, k_ref, v_ref, rt_ref, bias_ref, qinfo_ref, kinfo_ref, rank_ref,
    p_ref, a_ref, mix_ref, kaug_ref, vaug_ref, table_ref, qaug,
):
    step = pl.program_id(0)
    keys = k_ref.shape[0]
    prompt = keys - LEN
    heads = p_ref.shape[0]

    @pl.when(step == 0)
    def _():
        for head in range(heads):
            prepare_keys(
                head, k_ref, v_ref, rt_ref, kinfo_ref,
                kaug_ref.at[head], vaug_ref.at[head], table_ref.at[head],
            )

    start = pl.multiple_of(LEN - TQ - step * TQ, TQ)
    lane = lax.broadcasted_iota(jnp.int32, (TQ, HEAD_DIM), 1)
    segment_id = qinfo_ref[:, 0:1]
    rank = qinfo_ref[:, 1:2]
    wide = lax.broadcasted_iota(jnp.int32, (TQ, 2 * HEAD_DIM), 1)
    for head, s in [(head, s) for head in range(heads) for s in range(2)]:
        cols = slice(head * HEAD_DIM, (head + 1) * HEAD_DIM)
        table_p = table_ref[head, pl.ds(start, TQ + prompt), :]
        table_c = table_ref[head, pl.ds(pl.multiple_of(LEN + prompt + start, TQ), TQ + LEN), :]
        content, position, with_segment = query_terms(head, s, q_ref, bias_ref)
        same = jnp.sum(with_segment * bias_ref[3:4, cols], axis=1, keepdims=True) * scale_factor
        other = jnp.sum(with_segment * bias_ref[4:5, cols], axis=1, keepdims=True) * scale_factor
        differ = same - other
        differ_high = differ.astype(jnp.bfloat16).astype(jnp.float32)
        other_high = other.astype(jnp.bfloat16).astype(jnp.float32)
        extra = jnp.where(lane == segment_id, differ_high, 0.0)
        extra = jnp.where(lane - SEGMENTS == segment_id, differ - differ_high, extra)
        extra = jnp.where(lane == COL_ONE - HEAD_DIM, other_high, extra)
        extra = jnp.where(lane == COL_ONE_LOW - HEAD_DIM, other - other_high, extra)
        extra = jnp.where(lane == COL_MASK - HEAD_DIM, 1.0, extra)
        qaug[:, :HEAD_DIM] = (content * scale_factor).astype(jnp.bfloat16)
        qaug[:, HEAD_DIM:] = extra.astype(jnp.bfloat16)
        scores = mm(qaug[...], kaug_ref[head], NT)
        position = (position * scale_factor).astype(jnp.bfloat16)
        band_p = pltpu.roll(
            mm(position, table_p, NT), prompt + 1, axis=1, stride=1, stride_axis=0
        )
        band_c = pltpu.roll(mm(position, table_c, NT), LEN + 1, axis=1, stride=1, stride_axis=0)
        scores_p = scores[:, :prompt] + band_p[:, :prompt]
        scores_c = scores[:, prompt:] + band_c[:, :LEN]
        scores_c = jnp.where(rank_ref[0:1, :] <= rank - s, scores_c, negative)
        largest = jnp.maximum(
            jnp.max(scores_p, axis=1, keepdims=True), jnp.max(scores_c, axis=1, keepdims=True)
        )
        weights_p = jnp.exp(scores_p - largest)
        weights_c = jnp.exp(scores_c - largest)
        mixed = mm(weights_p.astype(jnp.bfloat16), vaug_ref[head, :prompt, :])
        mixed += mm(weights_c.astype(jnp.bfloat16), vaug_ref[head, prompt:, :])
        inverse = 1.0 / mixed[:, HEAD_DIM : HEAD_DIM + 1]
        mixed = mixed * inverse
        a_ref[head, s] = jnp.where(wide < HEAD_DIM, mixed, inverse)
        mix_ref[0, head, :, s * HEAD_DIM : (s + 1) * HEAD_DIM] = mixed[:, :HEAD_DIM].astype(
            jnp.bfloat16
        )
        rows = slice(s * TQ, (s + 1) * TQ)
        p_ref[head, 0, rows, :prompt] = reverse_rows(weights_p).astype(jnp.bfloat16)
        p_ref[head, 0, rows, prompt:] = reverse_rows(weights_c).astype(jnp.bfloat16)


def backward_kernel(
    head, q_ref, bias_ref, qinfo_ref, kaug_ref, vaug_ref, table_ref, p_ref, a_ref, ag_ref,
    dq_ref, dkv_ref, dt_ref, sum_ref,
    agaug, cw, cr, g_all, band_p, band_c, dk_acc, dv_acc, dt_acc,
):
    step = pl.program_id(0)
    keys = kaug_ref.shape[1]
    prompt = keys - LEN
    cols = slice(head * HEAD_DIM, (head + 1) * HEAD_DIM)

    @pl.when(step == 0)
    def _():
        dk_acc[...] = jnp.zeros_like(dk_acc)
        dv_acc[...] = jnp.zeros_like(dv_acc)
        dt_acc[...] = jnp.zeros_like(dt_acc)
        sum_ref[...] = jnp.zeros_like(sum_ref)

    start = pl.multiple_of(LEN - TQ - step * TQ, TQ)
    start_c = pl.multiple_of(LEN + prompt + start, TQ)
    lane = lax.broadcasted_iota(jnp.int32, (TQ, HEAD_DIM), 1)
    segment_id = qinfo_ref[:, 2:3]
    segments = []
    for s in range(2):
        rows = slice(s * TQ, (s + 1) * TQ)
        content, position, with_segment = query_terms(head, s, q_ref, bias_ref)
        cw[rows, :] = reverse_rows(content).astype(jnp.bfloat16)
        cr[rows, :] = reverse_rows(position).astype(jnp.bfloat16)
        segments.append(reverse_rows(with_segment))
        grad = ag_ref[0, 0, :, s * HEAD_DIM : (s + 1) * HEAD_DIM].astype(jnp.float32)
        inverse = a_ref[0, s, :, HEAD_DIM : HEAD_DIM + 1] * scale_factor
        delta = jnp.sum(grad * a_ref[0, s, :, :HEAD_DIM], axis=1, keepdims=True) * inverse
        delta_high = delta.astype(jnp.bfloat16).astype(jnp.float32)
        extra = jnp.where(lane == 0, -delta_high, jnp.where(lane == 1, delta_high - delta, 0.0))
        agaug[rows, :HEAD_DIM] = reverse_rows(grad * inverse).astype(jnp.bfloat16)
        agaug[rows, HEAD_DIM:] = reverse_rows(extra).astype(jnp.bfloat16)
    share_grad = mm(agaug[...], vaug_ref[0], NT)
    g_all[...] = (p_ref[0, 0].astype(jnp.float32) * share_grad).astype(jnp.bfloat16)
    for s in range(2):
        rows = slice(s * TQ, (s + 1) * TQ)
        blank = jnp.zeros((TQ, TQ), jnp.bfloat16)
        wide_p = jnp.concatenate([g_all[rows, :prompt], blank], axis=1)
        wide_c = jnp.concatenate([g_all[rows, prompt:], blank], axis=1)
        band_p[rows, :] = pltpu.roll(wide_p, 0, axis=1, stride=1, stride_axis=0)
        band_c[rows, :] = pltpu.roll(wide_c, 0, axis=1, stride=1, stride_axis=0)
    dv_acc[...] += mm(agaug[:, :HEAD_DIM], p_ref[0, 0], TN)
    dk_acc[...] += mm(cw[...], g_all[...], TN)
    dt_acc[:, pl.ds(start, TQ + prompt)] += mm(cr[...], band_p[...], TN)
    dt_acc[:, pl.ds(start_c, TQ + LEN)] += mm(cr[...], band_c[...], TN)
    query_content = mm(g_all[...], kaug_ref[0])
    query_position = mm(band_p[...], table_ref[0, pl.ds(start, TQ + prompt), :])
    query_position += mm(band_c[...], table_ref[0, pl.ds(start_c, TQ + LEN), :])
    same_vector = bias_ref[3:4, cols]
    other_vector = bias_ref[4:5, cols]

    def add_row(row, value):
        sum_ref[row : row + 1, :] += jnp.sum(value, axis=0, keepdims=True)

    for s in range(2):
        rows = slice(s * TQ, (s + 1) * TQ)
        from_content = query_content[rows, :HEAD_DIM]
        extra = query_content[rows, HEAD_DIM:]
        hit = (lane == segment_id) & (lane < SEGMENTS)
        same = jnp.sum(jnp.where(hit, extra, 0.0), axis=1, keepdims=True)
        other = extra[:, COL_ONE - HEAD_DIM : COL_ONE - HEAD_DIM + 1] - same
        from_segment = same * same_vector + other * other_vector
        from_position = query_position[rows, :]
        total = reverse_rows(from_content + from_position + from_segment)
        dq_ref[0, :, s * HEAD_DIM : (s + 1) * HEAD_DIM] = total.astype(jnp.bfloat16)
        add_row(0, from_content)
        add_row(1, from_position)
        add_row(2, from_segment)
        add_row(3, same * segments[s])
        add_row(4, other * segments[s])

    @pl.when(step == pl.num_programs(0) - 1)
    def _():
        dkv_ref[:, :HEAD_DIM] = dk_acc[...].T.astype(jnp.bfloat16)
        dkv_ref[:, HEAD_DIM:] = (dv_acc[...].T * HEAD_DIM**0.5).astype(jnp.bfloat16)
        dt_ref[...] = dt_acc[...].T.astype(jnp.bfloat16)


def whole(shape):
    return pl.BlockSpec(shape, lambda i: (0,) * len(shape))


def attend_forward(q, k, v, rt, bias, qinfo, kinfo, ranks, tokens):
    keys, width = k.shape
    table = rt.shape[0]
    steps = LEN // TQ
    heads = width // HEAD_DIM
    per = tokens // TQ
    return pl.pallas_call(
        forward_kernel,
        grid=(steps,),
        in_specs=[
            pl.BlockSpec((2, TQ, width), lambda i: (0, i, 0)),
            whole((keys, width)),
            whole((keys, width)),
            whole((table, width)),
            whole(bias.shape),
            pl.BlockSpec((TQ, qinfo.shape[1]), lambda i: (i, 0)),
            whole(kinfo.shape),
            whole(ranks.shape),
        ],
        out_specs=[
            pl.BlockSpec((heads, 1, 2 * TQ, keys), lambda i: (0, i, 0, 0)),
            pl.BlockSpec((heads, 2, TQ, 2 * HEAD_DIM), lambda i: (0, 0, i, 0)),
            pl.BlockSpec((1, heads, TQ, 2 * HEAD_DIM), lambda i: (i // per, 0, i % per, 0)),
            whole((heads, keys, 2 * HEAD_DIM)),
            whole((heads, keys, 2 * HEAD_DIM)),
            whole((heads, table, HEAD_DIM)),
        ],
        out_shape=[
            jax.ShapeDtypeStruct((heads, steps, 2 * TQ, keys), jnp.bfloat16),
            jax.ShapeDtypeStruct((heads, 2, LEN, 2 * HEAD_DIM), jnp.float32),
            jax.ShapeDtypeStruct((LEN // tokens, heads, tokens, 2 * HEAD_DIM), jnp.bfloat16),
            jax.ShapeDtypeStruct((heads, keys, 2 * HEAD_DIM), jnp.bfloat16),
            jax.ShapeDtypeStruct((heads, keys, 2 * HEAD_DIM), jnp.bfloat16),
            jax.ShapeDtypeStruct((heads, table, HEAD_DIM), jnp.bfloat16),
        ],
        scratch_shapes=[pltpu.VMEM((TQ, 2 * HEAD_DIM), jnp.bfloat16)],
        compiler_params=pltpu.CompilerParams(vmem_limit_bytes=56 * 2**20),
        cost_estimate=pl.CostEstimate(
            flops=heads * 6 * 2 * LEN * keys * 256,
            bytes_accessed=heads * 2 * LEN * keys * 2,
            transcendentals=heads * 2 * LEN * keys,
        ),
        name="attend_forward",
    )(q, k, v, rt, bias, qinfo, kinfo, ranks)


def attend_backward(head, q, bias, qinfo, kaug, vaug, rows_of, p, a, ag):
    _, keys, wide = kaug.shape
    table = rows_of.shape[1]
    width = q.shape[2]
    steps = LEN // TQ
    prompt = keys - LEN
    members, heads, tokens, _ = ag.shape
    per = tokens // TQ

    def one(shape):
        return pl.BlockSpec((1,) + shape, lambda i: (head,) + (0,) * len(shape))

    return pl.pallas_call(
        partial(backward_kernel, head),
        grid=(steps,),
        in_specs=[
            pl.BlockSpec((2, TQ, width), lambda i: (0, i, 0)),
            whole(bias.shape),
            pl.BlockSpec((TQ, qinfo.shape[1]), lambda i: (i, 0)),
            one((keys, wide)),
            one((keys, wide)),
            one((table, HEAD_DIM)),
            pl.BlockSpec((1, 1, 2 * TQ, keys), lambda i: (head, i, 0, 0)),
            pl.BlockSpec((1, 2, TQ, wide), lambda i: (head, 0, i, 0)),
            pl.BlockSpec((1, 1, TQ, wide), lambda i: (i // per, head, i % per, 0)),
        ],
        out_specs=[
            pl.BlockSpec((1, TQ, wide), lambda i: (i // per, i % per, 0)),
            whole((keys, wide)),
            whole((table, HEAD_DIM)),
            whole((8, HEAD_DIM)),
        ],
        out_shape=[
            jax.ShapeDtypeStruct((members, tokens, wide), jnp.bfloat16),
            jax.ShapeDtypeStruct((keys, wide), jnp.bfloat16),
            jax.ShapeDtypeStruct((table, HEAD_DIM), jnp.bfloat16),
            jax.ShapeDtypeStruct((8, HEAD_DIM), jnp.float32),
        ],
        scratch_shapes=[
            pltpu.VMEM((2 * TQ, wide), jnp.bfloat16),
            pltpu.VMEM((2 * TQ, HEAD_DIM), jnp.bfloat16),
            pltpu.VMEM((2 * TQ, HEAD_DIM), jnp.bfloat16),
            pltpu.VMEM((2 * TQ, keys), jnp.bfloat16),
            pltpu.VMEM((2 * TQ, TQ + prompt), jnp.bfloat16),
            pltpu.VMEM((2 * TQ, TQ + LEN), jnp.bfloat16),
            pltpu.VMEM((HEAD_DIM, keys), jnp.float32),
            pltpu.VMEM((HEAD_DIM, keys), jnp.float32),
            pltpu.VMEM((HEAD_DIM, table), jnp.float32),
        ],
        compiler_params=pltpu.CompilerParams(vmem_limit_bytes=56 * 2**20),
        cost_estimate=pl.CostEstimate(
            flops=12 * 2 * LEN * keys * 256, bytes_accessed=2 * LEN * keys * 2, transcendentals=0
        ),
        name="attend_backward",
    )(q, bias, qinfo, kaug, vaug, rows_of, p, a, ag)


def table_kernel(shards, place_ref, *refs):
    pieces, small, rest = refs[:shards], refs[shards : 2 * shards], refs[2 * shards :]
    (
        coarse_ref, fine_ref, weight_ref, rt_ref, position_ref, vector_ref, inner_ref, bias_ref,
        held, sem,
    ) = rest
    _, rows, width = pieces[0].shape
    shard, member = place_ref[0], place_ref[1]
    copies = []
    for m in range(shards):
        spot = pl.multiple_of((shard ^ m) * rows, rows)
        copies.append(
            pltpu.make_async_copy(pieces[m], weight_ref.at[:, pl.ds(spot, rows), :], sem.at[m])
        )
    for copy in copies:
        copy.start()
    for m in range(shards):
        held[m] = small[m][...].astype(jnp.float32)
    bias_ref[...] = held[shard ^ member][0:8, :]
    for w in range(shards):
        block = held[shard ^ w]
        at = slice(w * width, (w + 1) * width)
        vector_ref[0:5, at] = block[5:10, :]
        for j in range(4):
            spot = (w * 4 + j) * width
            inner_ref[0:1, spot : spot + width] = block[10 + j : 11 + j, :]
    half = fine_ref.shape[2]
    fine_sin, fine_cos = fine_ref[0], fine_ref[1]
    step = 64

    def build(i, carry):
        at = pl.ds(pl.multiple_of(i * step, step), step)
        coarse_sin, coarse_cos = coarse_ref[0, pl.ds(i, 1), :], coarse_ref[1, pl.ds(i, 1), :]
        position_ref[at, :half] = (coarse_sin * fine_cos - coarse_cos * fine_sin).astype(
            jnp.bfloat16
        )
        position_ref[at, half:] = (coarse_cos * fine_cos + coarse_sin * fine_sin).astype(
            jnp.bfloat16
        )
        return carry

    lax.fori_loop(0, position_ref.shape[0] // step, build, 0)
    for copy in copies:
        copy.wait()
    block = 256
    relative = weight_ref[3]

    def body(i, carry):
        at = pl.ds(pl.multiple_of(i * block, block), block)
        rt_ref[at, :] = mm(position_ref[at, :], relative).astype(jnp.bfloat16)
        return carry

    lax.fori_loop(0, position_ref.shape[0] // block, body, 0)


def project_table(place, pieces, small, coarse, fine):
    _, rows, width = pieces[0].shape
    shards = len(pieces)
    table = coarse.shape[1] * fine.shape[1]
    vmem = pl.BlockSpec(memory_space=pltpu.VMEM)
    return pl.pallas_call(
        partial(table_kernel, shards),
        in_specs=[pl.BlockSpec(memory_space=pltpu.SMEM)]
        + [pl.BlockSpec(memory_space=pl.ANY)] * shards
        + [vmem] * (shards + 2),
        out_specs=[vmem] * 6,
        out_shape=[
            jax.ShapeDtypeStruct((4, shards * rows, width), jnp.bfloat16),
            jax.ShapeDtypeStruct((table, width), jnp.bfloat16),
            jax.ShapeDtypeStruct((table, D), jnp.bfloat16),
            jax.ShapeDtypeStruct((8, D), jnp.float32),
            jax.ShapeDtypeStruct((1, 4 * D), jnp.float32),
            jax.ShapeDtypeStruct((8, width), jnp.float32),
        ],
        scratch_shapes=[
            pltpu.VMEM((shards,) + small[0].shape, jnp.float32),
            pltpu.SemaphoreType.DMA((shards,)),
        ],
        compiler_params=pltpu.CompilerParams(vmem_limit_bytes=48 * 2**20),
        name="project_table",
    )(place, *pieces, *small, coarse, fine)


def states_kernel(members, place_ref, *refs):
    pieces, (prompt_ref, weight_ref, q_ref, k_ref, v_ref, states_ref, sem) = (
        (refs[:members], refs[members : 2 * members]),
        refs[2 * members :],
    )
    tokens = pieces[0][0].shape[0]
    prompt = prompt_ref.shape[0]
    copies = [pltpu.make_async_copy(prompt_ref, states_ref.at[pl.ds(0, prompt)], sem.at[0])]
    for s in range(2):
        for m, piece in enumerate(pieces[s]):
            spot = prompt + s * LEN + pl.multiple_of((place_ref[1] ^ m) * tokens, tokens)
            copies.append(
                pltpu.make_async_copy(
                    piece, states_ref.at[pl.ds(spot, tokens)], sem.at[1 + 2 * m + s]
                )
            )
    for copy in copies:
        copy.start()
    for copy in copies:
        copy.wait()
    step = 256
    query, key, value = weight_ref[0], weight_ref[1], weight_ref[2]
    for i in range(2 * LEN // step):
        rows = states_ref[prompt + i * step : prompt + (i + 1) * step, :]
        stream, at = divmod(i * step, LEN)
        q_ref[stream, at : at + step, :] = mm(rows, query).astype(jnp.bfloat16)
    for i in range((prompt + LEN) // step):
        rows = states_ref[i * step : (i + 1) * step, :]
        k_ref[i * step : (i + 1) * step, :] = mm(rows, key).astype(jnp.bfloat16)
        v_ref[i * step : (i + 1) * step, :] = mm(rows, value).astype(jnp.bfloat16)


def project_states(place, content, query, prompt_all, weights):
    members = len(content)
    width = weights.shape[2]
    prompt = prompt_all.shape[0]
    return pl.pallas_call(
        partial(states_kernel, members),
        in_specs=[pl.BlockSpec(memory_space=pltpu.SMEM)]
        + [pl.BlockSpec(memory_space=pl.ANY)] * (2 * members + 1)
        + [pl.BlockSpec(memory_space=pltpu.VMEM)],
        out_specs=[pl.BlockSpec(memory_space=pltpu.VMEM)] * 4,
        out_shape=[
            jax.ShapeDtypeStruct((2, LEN, width), jnp.bfloat16),
            jax.ShapeDtypeStruct((prompt + LEN, width), jnp.bfloat16),
            jax.ShapeDtypeStruct((prompt + LEN, width), jnp.bfloat16),
            jax.ShapeDtypeStruct((prompt + 2 * LEN, D), jnp.bfloat16),
        ],
        scratch_shapes=[pltpu.SemaphoreType.DMA((1 + 2 * members,))],
        compiler_params=pltpu.CompilerParams(vmem_limit_bytes=48 * 2**20),
        name="project_states",
    )(place, *content, *query, prompt_all, weights)


def normalise(x):
    center = x - jnp.mean(x, axis=1, keepdims=True)
    inverse = lax.rsqrt(jnp.mean(center * center, axis=1, keepdims=True) + epsilon)
    return center * inverse, inverse


def norm_backward(grad, unit, inverse, gain):
    scaled = grad * gain
    mean = jnp.mean(scaled, axis=1, keepdims=True)
    along = jnp.mean(scaled * unit, axis=1, keepdims=True)
    return (scaled - mean - unit * along) * inverse


def layer_kernel(
    a_ref, content_ref, query_ref, up_content_ref, up_query_ref, vector_ref, inner_ref,
    output_hbm, hidden_hbm, return_hbm,
    out_content_ref, out_query_ref, flat_ref, inner_in_ref, active_ref, returned_ref, zgrad_ref,
    residual_ref, branch_ref, ag_ref, sum_ref, inner_sum_ref,
    output_w, hidden_w, return_w, flat, inner_in, slope, acc, unit, sem,
):
    members, heads, tokens, _ = a_ref.shape
    shards, _, rows_w = flat_ref.shape
    copies = [
        pltpu.make_async_copy(output_hbm, output_w, sem.at[0]),
        pltpu.make_async_copy(hidden_hbm, hidden_w, sem.at[1]),
        pltpu.make_async_copy(return_hbm, return_w, sem.at[2]),
    ]
    for copy in copies:
        copy.start()
    for g in range(members):
        for h in range(heads):
            spot = (g * heads + h) * HEAD_DIM
            for s in range(2):
                flat[s * tokens : (s + 1) * tokens, spot : spot + HEAD_DIM] = a_ref[
                    g, h, :, s * HEAD_DIM : (s + 1) * HEAD_DIM
                ]
    for w in range(shards):
        flat_ref[w] = flat[:, w * rows_w : (w + 1) * rows_w]
    gain, shift, outer, final_gain, final_shift = (vector_ref[i : i + 1, :] for i in range(5))
    copies[0].wait()
    inverses = []
    for s, source in enumerate((content_ref, query_ref)):
        at = slice(s * tokens, (s + 1) * tokens)
        mixed = mm(flat[at, :], output_w[...])
        normal, inverse = normalise(source[...].astype(jnp.float32) + mixed)
        inverses.append(inverse)
        unit[at, :] = normal
        middle = normal * gain + shift
        low = middle.astype(jnp.bfloat16)
        inner_in[at, :] = low
        for w in range(shards):
            inner_in_ref[w, at, :] = low[:, w * rows_w : (w + 1) * rows_w]
        acc[at, :] = middle + outer
    copies[1].wait()
    copies[2].wait()
    step = 512
    chunks = hidden_w.shape[1] // step
    root = 0.7978845608028654

    def forward(i, carry):
        at = pl.ds(pl.multiple_of(i * step, step), step)
        for s in range(2):
            part = slice(s * tokens, (s + 1) * tokens)
            z = mm(inner_in[part, :], hidden_w[:, at]) + inner_ref[:, at]
            square = z * z
            curve = jnp.tanh(root * (z + 0.044715 * (z * square)))
            half = 0.5 + 0.5 * curve
            active = (z * half).astype(jnp.bfloat16)
            slope[part, at] = half + (0.5 * root) * z * (1.0 - curve * curve) * (
                1.0 + (3 * 0.044715) * square
            )
            active_ref[part, at] = active
            acc[part, :] += mm(active, return_w[at, :])
        return carry

    lax.fori_loop(0, chunks, forward, 0)
    sums = []
    for s, (upstream, result) in enumerate(
        ((up_content_ref, out_content_ref), (up_query_ref, out_query_ref))
    ):
        at = slice(s * tokens, (s + 1) * tokens)
        normal, inverse = normalise(acc[at, :])
        result[...] = (normal * final_gain + final_shift).astype(jnp.bfloat16)
        grad = upstream[...].astype(jnp.float32)
        back = norm_backward(grad, normal, inverse, final_gain)
        low = back.astype(jnp.bfloat16)
        returned_ref[at, :] = low
        acc[at, :] = back
        sums.append(
            [
                jnp.sum(low.astype(jnp.float32), axis=0, keepdims=True),
                jnp.sum(grad * normal, axis=0, keepdims=True),
                jnp.sum(grad, axis=0, keepdims=True),
            ]
        )
    for i in range(3):
        sum_ref[2 + i : 3 + i, :] = sums[0][i] + sums[1][i]

    def backward(i, carry):
        at = pl.ds(pl.multiple_of(i * step, step), step)
        total = jnp.zeros((1, step), jnp.float32)
        for s in range(2):
            part = slice(s * tokens, (s + 1) * tokens)
            grad = mm(returned_ref[part, :], return_w[at, :], NT) * slope[part, at]
            low = grad.astype(jnp.bfloat16)
            zgrad_ref[part, at] = low
            total += jnp.sum(low.astype(jnp.float32), axis=0, keepdims=True)
            acc[part, :] += mm(low, hidden_w[:, at], NT)
        inner_sum_ref[:, at] = total
        return carry

    lax.fori_loop(0, chunks, backward, 0)
    sums = []
    for s in range(2):
        at = slice(s * tokens, (s + 1) * tokens)
        grad = acc[at, :]
        normal = unit[at, :]
        back = norm_backward(grad, normal, inverses[s], gain)
        residual_ref[at, :] = back
        low = back.astype(jnp.bfloat16)
        branch_ref[at, :] = low
        sums.append(
            [
                jnp.sum(grad * normal, axis=0, keepdims=True),
                jnp.sum(grad, axis=0, keepdims=True),
            ]
        )
        mixed = mm(low, output_w[...], NT).astype(jnp.bfloat16)
        for g in range(members):
            for h in range(heads):
                spot = (g * heads + h) * HEAD_DIM
                ag_ref[g, h, :, s * HEAD_DIM : (s + 1) * HEAD_DIM] = mixed[
                    :, spot : spot + HEAD_DIM
                ]
    for i in range(2):
        sum_ref[i : i + 1, :] = sums[0][i] + sums[1][i]


def layer(shards, a, content, query, up_content, up_query, vectors, inner, output_w, hidden_w, return_w):
    tokens = content.shape[0]
    rows = 2 * tokens
    hidden = hidden_w.shape[1]
    vmem = pl.BlockSpec(memory_space=pltpu.VMEM)
    low = partial(jax.ShapeDtypeStruct, dtype=jnp.bfloat16)
    wide = partial(jax.ShapeDtypeStruct, dtype=jnp.float32)
    return pl.pallas_call(
        layer_kernel,
        in_specs=[vmem] * 7 + [pl.BlockSpec(memory_space=pl.ANY)] * 3,
        out_specs=[vmem] * 12,
        out_shape=[
            low((tokens, D)),
            low((tokens, D)),
            low((shards, rows, D // shards)),
            low((shards, rows, D // shards)),
            low((rows, hidden)),
            low((rows, D)),
            low((rows, hidden)),
            wide((rows, D)),
            low((rows, D)),
            low(a.shape),
            wide((5, D)),
            wide((1, hidden)),
        ],
        scratch_shapes=[
            pltpu.VMEM((D, D), jnp.bfloat16),
            pltpu.VMEM((D, hidden), jnp.bfloat16),
            pltpu.VMEM((hidden, D), jnp.bfloat16),
            pltpu.VMEM((rows, D), jnp.bfloat16),
            pltpu.VMEM((rows, D), jnp.bfloat16),
            pltpu.VMEM((rows, hidden), jnp.float32),
            pltpu.VMEM((rows, D), jnp.float32),
            pltpu.VMEM((rows, D), jnp.float32),
            pltpu.SemaphoreType.DMA((3,)),
        ],
        compiler_params=pltpu.CompilerParams(vmem_limit_bytes=60 * 2**20),
        cost_estimate=pl.CostEstimate(
            flops=8 * rows * D * hidden, bytes_accessed=24 * 2**20, transcendentals=rows * hidden
        ),
        name="layer",
    )(a, content, query, up_content, up_query, vectors, inner, output_w, hidden_w, return_w)


def token_grads_kernel(
    core_ref, active_ref, inner_ref, mixed_ref, returned_ref, zgrad_ref, branch_ref, out_ref
):
    rows_w = inner_ref.shape[2]
    low = partial(jnp.asarray, dtype=jnp.bfloat16)
    count = zgrad_ref.shape[1] // D
    block = mm(inner_ref[0], zgrad_ref[...], TN)
    spots = [0, 1, 2, 6]
    for j in range(count):
        at = spots[j] * rows_w
        out_ref[0, at : at + rows_w, :] = low(block[:, j * D : (j + 1) * D])
    block = mm(active_ref[...], returned_ref[...], TN)
    spots = [3, 4, 5, 7]
    for j in range(count):
        at = spots[j] * rows_w
        out_ref[0, at : at + rows_w, :] = low(block[j * rows_w : (j + 1) * rows_w])
    out_ref[0, 8 * rows_w :, :] = low(mm(mixed_ref[0], branch_ref[...], TN))


def token_grads(core, active, inner, mixed, returned, zgrad, branch):
    shards, rows, rows_w = inner.shape
    hidden = active.shape[1]
    per = hidden // shards
    block = (1, 9 * rows_w, D)
    return pl.pallas_call(
        token_grads_kernel,
        grid_spec=pltpu.PrefetchScalarGridSpec(
            num_scalar_prefetch=1,
            grid=(shards // 2,),
            in_specs=[
                pl.BlockSpec((rows, per), lambda i, c: (0, 2 * i + c[0])),
                pl.BlockSpec((1, rows, rows_w), lambda i, c: (2 * i + c[0], 0, 0)),
                pl.BlockSpec((1, rows, rows_w), lambda i, c: (2 * i + c[0], 0, 0)),
                pl.BlockSpec((rows, D), lambda i, c: (0, 0)),
                pl.BlockSpec((rows, hidden), lambda i, c: (0, 0)),
                pl.BlockSpec((rows, D), lambda i, c: (0, 0)),
            ],
            out_specs=pl.BlockSpec(block, lambda i, c: (i, 0, 0)),
        ),
        out_shape=jax.ShapeDtypeStruct((shards // 2,) + block[1:], jnp.bfloat16),
        compiler_params=pltpu.CompilerParams(vmem_limit_bytes=56 * 2**20),
        cost_estimate=pl.CostEstimate(
            flops=2 * rows * D * hidden, bytes_accessed=16 * 2**20, transcendentals=0
        ),
        name="token_grads",
    )(core.reshape(1), active, inner, mixed, returned, zgrad, branch)


def unpack_tokens_kernel(members, head_count, place_ref, *refs):
    pieces, (hidden_ref, return_ref, output_ref, held) = refs[:members], refs[members:]
    rows_w = hidden_ref.shape[0]
    chains, per, _ = held.shape[1:]
    for m in range(members):
        held[m] = pieces[m][...]
    member = place_ref[1]
    targets = {0: 0, 1: 1, 2: 2, 6: 3}
    for g in range(members):
        head, half = g % head_count, g // head_count
        for c in range(chains):
            if c == 2:
                spot = (half * head_count + head) * per
            else:
                spot = (head * (members // head_count) + half) * per
            row = c * members * per + spot
            done = 0
            while done < per:
                block, at = divmod(row + done, rows_w)
                count = min(per - done, rows_w - at)
                value = held[member ^ g, c, done : done + count, :].astype(jnp.float32)
                if block == 8:
                    output_ref[at : at + count, :] = value
                elif block in targets:
                    j = targets[block]
                    hidden_ref[at : at + count, j * D : (j + 1) * D] = value
                else:
                    j = {3: 0, 4: 1, 5: 2, 7: 3}[block]
                    return_ref[j * rows_w + at : j * rows_w + at + count, :] = value
                done += count


def unpack_tokens(place, rows_w, head_count, pieces):
    members = len(pieces)
    vmem = pl.BlockSpec(memory_space=pltpu.VMEM)
    return pl.pallas_call(
        partial(unpack_tokens_kernel, members, head_count),
        in_specs=[pl.BlockSpec(memory_space=pltpu.SMEM)] + [vmem] * members,
        out_specs=[vmem] * 3,
        out_shape=[
            jax.ShapeDtypeStruct((rows_w, 4 * D), jnp.float32),
            jax.ShapeDtypeStruct((4 * rows_w, D), jnp.float32),
            jax.ShapeDtypeStruct((rows_w, D), jnp.float32),
        ],
        scratch_shapes=[pltpu.VMEM((members,) + pieces[0].shape, jnp.bfloat16)],
        compiler_params=pltpu.CompilerParams(vmem_limit_bytes=48 * 2**20),
        name="unpack_tokens",
    )(place, *pieces)


def head_grads_kernel(shards, heads, place_ref, states_ref, position_ref, *rest):
    dq, dkv, dt = (rest[i * heads : (i + 1) * heads] for i in range(3))
    small, out_ref = rest[3 * heads : -1], rest[-1]
    keys = dkv[0].shape[0]
    prompt = keys - LEN
    rows_w = D // shards
    wide = 2 * HEAD_DIM
    side = partial(jnp.concatenate, axis=1)
    dq = side([ref[...].reshape(LEN, wide) for ref in dq])
    key_value = mm(side([ref[...] for ref in dkv]), states_ref[:keys, :], TN)
    content = mm(dq, states_ref[prompt:keys, :], TN)
    query = mm(dq, states_ref[keys:, :], TN)
    table = mm(side([ref[...] for ref in dt]), position_ref[...], TN)
    parts = []
    for h in range(heads):
        at = h * wide
        parts += [
            content[at : at + HEAD_DIM] + query[at + HEAD_DIM : at + wide],
            key_value[at : at + wide],
            table[h * HEAD_DIM : (h + 1) * HEAD_DIM],
        ]
    turned = jnp.concatenate(parts, axis=0).T.astype(jnp.bfloat16)
    for w in range(shards):
        out_ref[w, :rows_w, :] = turned[w * rows_w : (w + 1) * rows_w, :]
    if small:
        token_ref, inner_ref, sums = small[0], small[1], small[2:]
        member = place_ref[1]
        out_ref[:, rows_w:, :] = jnp.zeros_like(out_ref[:, rows_w:, :])
        own_sums = side([ref[0:5, :] for ref in sums])
        for w in range(shards):
            own = jnp.where(member == w, own_sums, 0.0)
            parts = [token_ref[0:5, w * rows_w : (w + 1) * rows_w], own]
            parts += [
                inner_ref[0:1, (4 * w + j) * rows_w : (4 * w + j + 1) * rows_w] for j in range(4)
            ]
            parts.append(jnp.zeros((2, rows_w), jnp.float32))
            out_ref[w, rows_w : rows_w + 16, :rows_w] = jnp.concatenate(parts, axis=0).astype(
                jnp.bfloat16
            )


def head_grads(place, shards, states, positions, dq, dkv, dt, small=()):
    vmem = pl.BlockSpec(memory_space=pltpu.VMEM)
    heads = len(dq)
    operands = (states, positions) + tuple(dq) + tuple(dkv) + tuple(dt) + tuple(small)
    rows = D // shards + (16 if small else 0)
    return pl.pallas_call(
        partial(head_grads_kernel, shards, heads),
        in_specs=[pl.BlockSpec(memory_space=pltpu.SMEM)] + [vmem] * len(operands),
        out_specs=vmem,
        out_shape=jax.ShapeDtypeStruct((shards, rows, 4 * HEAD_DIM * heads), jnp.bfloat16),
        compiler_params=pltpu.CompilerParams(vmem_limit_bytes=56 * 2**20),
        cost_estimate=pl.CostEstimate(
            flops=2 * 6656 * D * 256, bytes_accessed=12 * 2**20, transcendentals=0
        ),
        name="head_grads",
    )(place, *operands)


def unpack_kernel(members, groups, place_ref, *refs):
    pieces = [refs[i * members : (i + 1) * members] for i in range(groups)]
    outs = refs[groups * members : groups * members + 4]
    small_ref = refs[groups * members + 4]
    held = refs[groups * members + 5 : groups * members + 5 + groups]
    rows_w = outs[0].shape[0]
    for i in range(groups):
        for m in range(members):
            held[i][m] = pieces[i][m][...]
    member = place_ref[1]
    for g in range(members):
        head = 0
        for i in range(groups):
            block = held[i][member ^ g].astype(jnp.float32)
            for j in range(block.shape[1] // (4 * HEAD_DIM)):
                spot = (g * groups_heads(held) + head) * HEAD_DIM
                for kind in range(4):
                    at = (4 * j + kind) * HEAD_DIM
                    outs[kind][:, spot : spot + HEAD_DIM] = block[:rows_w, at : at + HEAD_DIM]
                head += 1
    last = held[-1]
    total = last[0, rows_w : rows_w + 16, :].astype(jnp.float32)
    for m in range(1, members):
        total += last[m, rows_w : rows_w + 16, :].astype(jnp.float32)
    small_ref[...] = total


def groups_heads(held):
    return sum(ref.shape[2] // (4 * HEAD_DIM) for ref in held)


def unpack(place, rows_w, *pieces):
    members = len(pieces[0])
    vmem = pl.BlockSpec(memory_space=pltpu.VMEM)
    flat = [x for group in pieces for x in group]
    return pl.pallas_call(
        partial(unpack_kernel, members, len(pieces)),
        in_specs=[pl.BlockSpec(memory_space=pltpu.SMEM)] + [vmem] * len(flat),
        out_specs=[vmem] * 5,
        out_shape=[jax.ShapeDtypeStruct((rows_w, D), jnp.float32)] * 4
        + [jax.ShapeDtypeStruct((16, 4 * HEAD_DIM), jnp.float32)],
        scratch_shapes=[pltpu.VMEM((members,) + group[0].shape, jnp.bfloat16) for group in pieces],
        compiler_params=pltpu.CompilerParams(vmem_limit_bytes=48 * 2**20),
        name="unpack",
    )(place, *flat)


def finish_kernel(
    token_ref, prompt_ref, residual_ref, weight_hbm, content_ref, query_ref, out_prompt_ref,
    weight, parts, prompts, sem,
):
    copy = pltpu.make_async_copy(weight_hbm, weight, sem)
    copy.start()
    members, heads, _, tokens, wide = token_ref.shape
    chapters = prompt_ref.shape[0]
    for g in range(members):
        for h in range(heads):
            spot = (g * heads + h) * HEAD_DIM
            for kind in range(4):
                at = (kind % 2) * HEAD_DIM
                parts[kind, :, spot : spot + HEAD_DIM] = token_ref[
                    g, h, kind // 2, :, at : at + HEAD_DIM
                ]
            total = prompt_ref[0, g, h].astype(jnp.float32)
            for c in range(1, chapters):
                total += prompt_ref[c, g, h].astype(jnp.float32)
            total = total.astype(jnp.bfloat16)
            for kind in range(2):
                prompts[kind, :, spot : spot + HEAD_DIM] = total[
                    :, kind * HEAD_DIM : (kind + 1) * HEAD_DIM
                ]
    copy.wait()
    query, key, value = (weight[:, i * D : (i + 1) * D] for i in range(3))
    content = residual_ref[:tokens, :] + mm(parts[0], query, NT)
    content += mm(parts[2], key, NT)
    content += mm(parts[3], value, NT)
    content_ref[...] = content.astype(jnp.bfloat16)
    query_ref[...] = (residual_ref[tokens:, :] + mm(parts[1], query, NT)).astype(jnp.bfloat16)
    out_prompt_ref[...] = (mm(prompts[0], key, NT) + mm(prompts[1], value, NT)).astype(
        jnp.bfloat16
    )


def finish(token_back, prompt_back, residual, weights):
    tokens = token_back.shape[3]
    prompt = prompt_back.shape[3]
    vmem = pl.BlockSpec(memory_space=pltpu.VMEM)
    return pl.pallas_call(
        finish_kernel,
        in_specs=[vmem] * 3 + [pl.BlockSpec(memory_space=pl.ANY)],
        out_specs=[vmem] * 3,
        out_shape=[
            jax.ShapeDtypeStruct((tokens, D), jnp.bfloat16),
            jax.ShapeDtypeStruct((tokens, D), jnp.bfloat16),
            jax.ShapeDtypeStruct((prompt, D), jnp.bfloat16),
        ],
        scratch_shapes=[
            pltpu.VMEM(weights.shape, jnp.bfloat16),
            pltpu.VMEM((4, tokens, D), jnp.bfloat16),
            pltpu.VMEM((2, prompt, D), jnp.bfloat16),
            pltpu.SemaphoreType.DMA,
        ],
        compiler_params=pltpu.CompilerParams(vmem_limit_bytes=48 * 2**20),
        cost_estimate=pl.CostEstimate(
            flops=8 * tokens * D * D, bytes_accessed=8 * 2**20, transcendentals=0
        ),
        name="finish",
    )(token_back, prompt_back, residual, weights)


def axes_size(axes):
    size = 1
    for name in axes:
        size *= lax.axis_size(name)
    return size


def flat_index(axes):
    index = 0
    for name in axes:
        index = index * lax.axis_size(name) + lax.axis_index(name)
    return index


def swap(x, axes, mask):
    return lax.ppermute(x, axes, [(i, i ^ mask) for i in range(axes_size(axes))])


def bits_of(axes):
    return range(axes_size(axes).bit_length() - 1)


def pieces_of(x, axes):
    pieces = {0: x}
    for bit in reversed(bits_of(axes)):
        for mask in list(pieces):
            pieces[mask | 1 << bit] = swap(pieces[mask], axes, 1 << bit)
    return [pieces[m] for m in range(axes_size(axes))]


def in_order(pieces, index):
    count = len(pieces)
    result = jnp.zeros((count,) + pieces[0].shape, pieces[0].dtype)
    for m, piece in enumerate(pieces):
        result = lax.dynamic_update_slice(result, piece[None], (index ^ m,) + (0,) * piece.ndim)
    return result


def pick(x, index, axis=0):
    return lax.dynamic_index_in_dim(x, index, axis, keepdims=False)


def add_low(x, y):
    return (x.astype(jnp.float32) + y.astype(jnp.float32)).astype(jnp.bfloat16)


def half_sum(x, axes, bit, axis):
    own = flat_index(axes) >> bit & 1
    return add_low(pick(x, own, axis), swap(pick(x, 1 - own, axis), axes, 1 << bit))


def split_axis(x, axis):
    return x.reshape(x.shape[:axis] + (2, x.shape[axis] // 2) + x.shape[axis + 1 :])


def stages_of(names):
    return [((name,), bit) for name in names for bit in bits_of((name,))]


def full_sum(x, stages):
    for axes, bit in stages:
        x = add_low(x, swap(x, axes, 1 << bit))
    return x


def group_pieces(x, axes):
    return [x] + [swap(x, axes, m) for m in range(1, axes_size(axes))]


def back_through(grad_rows, weight):
    return jnp.einsum("rc,dc->rd", grad_rows, weight, preferred_element_type=jnp.float32)


def outer_sum(rows_in, grad_rows):
    return jnp.einsum("rd,rc->dc", rows_in, grad_rows, preferred_element_type=jnp.float32)


def sinusoid_rows(first, rows):
    frequency = jnp.asarray(
        np.power(10000.0, -2.0 * np.arange(D // 2) / D).astype(np.float32)
    )
    fine = jnp.arange(64, dtype=jnp.float32)[:, None] * frequency
    coarse = (first - 64 * jnp.arange(rows // 64, dtype=jnp.int32)).astype(jnp.float32)
    coarse = coarse[:, None] * frequency
    fs, fc = jnp.sin(fine)[None], jnp.cos(fine)[None]
    cs, cc = jnp.sin(coarse)[:, None], jnp.cos(coarse)[:, None]
    both = jnp.concatenate([cs * fc - cc * fs, cc * fc + cs * fs], axis=-1)
    return both.reshape(rows, D).astype(jnp.bfloat16)


GROUP = ("half", "head")
JOB = ("cont", "half", "head")
SHARD = ("wshard",)


def per_device(
    prompt_states, content_states, query_states, visible_length, start_offsets,
    prompt_segments, token_segments, order_ranks,
    query_weights, key_weights, value_weights, output_weights, relative_weights,
    content_bias, position_bias, segment_bias, segment_vectors,
    attention_gain, attention_shift, hidden_weights, hidden_bias, return_weights, return_bias,
    final_gain, final_shift, content_upstream, query_upstream,
):
    members = axes_size(GROUP)
    member = flat_index(GROUP)
    shards = lax.axis_size("wshard")
    shard = lax.axis_index("wshard")
    chapters = lax.axis_size("cont")
    chapter = lax.axis_index("cont")
    width = D // members
    local_heads = HEADS // members
    content_rows = content_states[0]
    query_rows = query_states[0]
    tokens = content_rows.shape[0]
    prompt_part = prompt_states.shape[1]
    prompt_total = prompt_segments.shape[1]
    keys = prompt_total + LEN
    rows_w = query_weights.shape[0]

    def columns(x):
        return lax.dynamic_slice_in_dim(x, member * width, width, x.ndim - 1)

    content = {0: content_rows}
    query = {0: query_rows}
    content[1], query[2] = swap(content_rows, GROUP, 1), swap(query_rows, GROUP, 2)
    first_weights = jnp.stack(
        [columns(w) for w in (query_weights, key_weights, value_weights, relative_weights)], axis=0
    )
    small = jnp.concatenate(
        [
            jnp.stack([content_bias, position_bias, segment_bias]),
            segment_vectors,
            jnp.stack([attention_gain, attention_shift, return_bias, final_gain, final_shift]),
            hidden_bias.reshape(-1, rows_w),
            jnp.zeros((2, rows_w), jnp.bfloat16),
        ],
        axis=0,
    )
    first_pieces = pieces_of(first_weights, SHARD)
    small_pieces = pieces_of(small, SHARD)
    query[1], content[2] = swap(query_rows, GROUP, 1), swap(content_rows, GROUP, 2)
    content[3], query[3] = swap(content[1], GROUP, 2), swap(query[2], GROUP, 1)
    prompt_all = lax.all_to_all(
        jnp.broadcast_to(prompt_states, (chapters * members,) + prompt_states.shape[1:]),
        JOB,
        0,
        0,
        tiled=True,
    ).reshape(prompt_total, D)
    output_full = lax.all_gather(output_weights, "wshard", axis=0, tiled=True)
    hidden_full = lax.all_gather(hidden_weights, "wshard", axis=0, tiled=True)
    return_full = lax.all_gather(return_weights, "wshard", axis=0, tiled=True)
    attention_weights = jnp.concatenate([query_weights, key_weights, value_weights], axis=1)
    attention_full = lax.all_gather(attention_weights, "wshard", axis=0, tiled=True)

    seen = pick(visible_length[0], chapter)
    base = seen + pick(start_offsets[0], chapter)
    segments = lax.dynamic_slice_in_dim(token_segments[0], chapter * LEN, LEN)
    ranks = lax.dynamic_slice_in_dim(order_ranks[0], chapter * LEN, LEN)
    reversed_segments = jnp.flip(segments.reshape(-1, TQ), 1).reshape(-1)
    qinfo = jnp.stack([segments, ranks, reversed_segments, segments], axis=1)
    key_segments = jnp.concatenate([prompt_segments[0], segments])
    hidden_keys = (jnp.arange(keys, dtype=jnp.int32) < prompt_total) & (
        jnp.arange(keys, dtype=jnp.int32) >= seen
    )
    kinfo = jnp.stack([key_segments, hidden_keys.astype(jnp.int32)], axis=1)
    place = jnp.stack([shard, member])

    frequency = jnp.asarray(np.power(10000.0, -2.0 * np.arange(D // 2) / D).astype(np.float32))
    starts = jnp.concatenate(
        [
            base + LEN - 1 - 64 * jnp.arange((LEN + prompt_total) // 64, dtype=jnp.int32),
            LEN - 1 - 64 * jnp.arange(2 * LEN // 64, dtype=jnp.int32),
        ]
    )
    coarse = starts.astype(jnp.float32)[:, None] * frequency
    coarse = jnp.stack([jnp.sin(coarse), jnp.cos(coarse)])
    fine = jnp.arange(64, dtype=jnp.float32)[:, None] * frequency
    fine = jnp.stack([jnp.sin(fine), jnp.cos(fine)])

    first_full, rt, positions, vectors, inner_full, head_bias = project_table(
        place, first_pieces, small_pieces, coarse, fine
    )
    q, k, v, states = project_states(
        place,
        [content[m] for m in range(members)],
        [query[m] for m in range(members)],
        prompt_all,
        first_full,
    )
    p, a, mixture, kaug, vaug, table_rows = attend_forward(
        q, k, v, rt, head_bias, qinfo, kinfo, ranks[None], tokens
    )
    mixture = lax.all_to_all(mixture, GROUP, 0, 0, tiled=True)

    (
        out_content, out_query, mixed_flat, inner_in, active, returned_grad, inner_grad,
        residual_grad, branch_grad, grad_out, token_sums, inner_bias_grad,
    ) = layer(
        shards, mixture, content_rows, query_rows, content_upstream[0], query_upstream[0],
        vectors, inner_full, output_full, hidden_full, return_full,
    )
    grad_out, attention_full = lax.optimization_barrier((grad_out, attention_full))
    grad_out = lax.all_to_all(grad_out, GROUP, 0, 0, tiled=True)

    core = shard & 1
    grads = (active, inner_in, mixed_flat, returned_grad, inner_grad, branch_grad)
    sent = swap(token_grads(1 - core, *grads), SHARD, 1)
    total = add_low(token_grads(core, *grads), sent)
    third = total.shape[1] // 3
    chains = [total[:, i * third : (i + 1) * third] for i in range(3)]
    rest = [(SHARD, bit) for bit in bits_of(SHARD) if bit > 0]
    head_stage, half_stage, cont_stage = (stages_of((name,)) for name in ("head", "half", "cont"))
    orders = (
        (rest, head_stage, half_stage),
        (head_stage, half_stage, rest),
        (half_stage, rest, head_stage),
    )

    def chain_stage(x, stages):
        for axes, bit in stages:
            if axes == SHARD:
                x = half_sum(x.reshape((-1, 2) + x.shape[1:]), axes, bit, 1)
            else:
                x = half_sum(split_axis(x, 1), axes, bit, 1)
        return x

    small_grads = (token_sums, inner_bias_grad)
    backward, head_parts = [], []
    for h in range(local_heads):
        grad_out, chains = lax.optimization_barrier((grad_out, chains))
        backward.append(
            attend_backward(h, q, head_bias, qinfo, kaug, vaug, table_rows, p, a, grad_out)
        )
        chains = [chain_stage(x, orders[i][h]) for i, x in enumerate(chains)]
        if h == local_heads - 2:
            dq, dkv, dt, _ = zip(*backward)
            x = head_grads(place, shards, states, positions, dq, dkv, dt)
            x = half_sum(x.reshape((-1, 2) + x.shape[1:]), SHARD, 0, 1)
            head_parts.append(x)
            grad_out, head_parts = lax.optimization_barrier((grad_out, head_parts))
    dq, dkv, dt, sums = zip(*backward)
    x = head_grads(
        place, shards, states, positions, dq[-1:], dkv[-1:], dt[-1:], small_grads + sums
    )
    head_parts.append(half_sum(x.reshape((-1, 2) + x.shape[1:]), SHARD, 0, 1))
    token_back = jnp.stack(
        [
            jnp.stack([dq[h], dkv[h][prompt_total:].reshape(dq[h].shape)], axis=1)
            for h in range(local_heads)
        ],
        axis=1,
    )
    token_back = lax.all_to_all(token_back, GROUP, 0, 0, tiled=True)
    prompt_back = jnp.stack(
        [x[:prompt_total].reshape(chapters * members, prompt_part, -1) for x in dkv], axis=1
    )
    prompt_back = lax.all_to_all(prompt_back, JOB, 0, 0, tiled=True)
    prompt_back = prompt_back.reshape((chapters, members) + prompt_back.shape[1:])

    chains = jnp.concatenate(chains)
    chains = full_sum(chains, cont_stage)
    hidden_total, return_total, output_total = unpack_tokens(
        place, rows_w, lax.axis_size("head"), group_pieces(chains, GROUP)
    )
    head_pieces = []
    for x in head_parts:
        for axes, bit in rest:
            x = half_sum(x.reshape((-1, 2) + x.shape[1:]), axes, bit, 1)
        head_pieces.append(group_pieces(full_sum(x[0], cont_stage), GROUP))
    query_grad, key_grad, value_grad, relative_grad, small_total = unpack(
        place, rows_w, *head_pieces
    )
    vector_total = small_total[:10, :rows_w]
    inner_total = small_total[10:14, :rows_w].reshape(-1)
    content_grad, queries_grad, prompt_grad = finish(
        token_back, prompt_back, residual_grad, attention_full
    )
    return (
        out_content[None],
        out_query[None],
        prompt_grad[None],
        content_grad[None],
        queries_grad[None],
        query_grad,
        key_grad,
        value_grad,
        output_total,
        relative_grad,
        vector_total[5],
        vector_total[6],
        vector_total[7],
        vector_total[8:10],
        vector_total[0],
        vector_total[1],
        hidden_total,
        inner_total,
        return_total,
        vector_total[2],
        vector_total[3],
        vector_total[4],
    )


def solution(mesh):
    rows = P("wshard", JOB, None)
    job = P("wshard", None)
    matrix = P("wshard", None)
    vector = P("wshard")
    pair = P(None, "wshard")
    in_specs = (
        (rows,) * 3 + (job,) * 5 + (matrix,) * 5 + (vector,) * 3 + (pair,)
        + (vector, vector, matrix, vector, matrix, vector, vector, vector, rows, rows)
    )
    out_specs = (
        (rows,) * 5 + (matrix,) * 5 + (vector,) * 3 + (pair,)
        + (vector, vector, matrix, vector, matrix, vector, vector, vector)
    )

    def run(*arguments):
        seq_count, head_count, shard_count = mesh.devices.shape
        tokens = arguments[1].shape[1] // (seq_count * head_count)
        halves = LEN // (tokens * head_count)
        split = Mesh(
            mesh.devices.reshape(seq_count // halves, halves, head_count, shard_count),
            ("cont", "half", "head", "wshard"),
        )
        return jax.shard_map(
            per_device, mesh=split, in_specs=in_specs, out_specs=out_specs, check_vma=False
        )(*arguments)

    return run
```

```python
from functools import partial

import jax
import jax.numpy as jnp
import numpy as np
from jax import lax
from jax.experimental import pallas as pl
from jax.experimental.pallas import tpu as pltpu
from jax.sharding import Mesh, PartitionSpec as P

D = 768
HEADS = 12
HEAD_DIM = 64
LEN = 1024
SEGMENTS = 4
TQ = 128

negative = -1e30
epsilon = 1e-06
scale_factor = HEAD_DIM ** (-0.5)
NT = (((1,), (1,)), ((), ()))
NN = (((1,), (0,)), ((), ()))
TN = (((0,), (0,)), ((), ()))

COL_HIGH = HEAD_DIM
COL_LOW = HEAD_DIM + SEGMENTS
COL_ONE = HEAD_DIM + 2 * SEGMENTS
COL_ONE_LOW = COL_ONE + 1
COL_MASK = COL_ONE + 2


def mm(a, b, dims=NN):
    return lax.dot_general(a, b, dims, preferred_element_type=jnp.float32)


def reverse_rows(x):
    groups = x.shape[0] // 8
    index = 7 - lax.broadcasted_iota(jnp.int32, (8, x.shape[1]), 0)
    return jnp.concatenate(
        [
            jnp.take_along_axis(x[8 * (groups - 1 - g) : 8 * (groups - g)], index, axis=0)
            for g in range(groups)
        ],
        axis=0,
    )


def prepare_keys(head, k_ref, v_ref, rt_ref, kinfo_ref, kaug, vaug, rt):
    cols = slice(head * HEAD_DIM, (head + 1) * HEAD_DIM)
    rows = k_ref.shape[0]
    lane = lax.broadcasted_iota(jnp.int32, (rows, HEAD_DIM), 1)
    segment = kinfo_ref[:, 0:1]
    hidden = kinfo_ref[:, 1:2]
    one_hot = ((lane == segment) | (lane - SEGMENTS == segment)) & (lane < 2 * SEGMENTS)
    ones = (lane == COL_ONE - HEAD_DIM) | (lane == COL_ONE_LOW - HEAD_DIM)
    extra = jnp.where(one_hot | ones, 1.0, 0.0)
    extra = jnp.where((lane == COL_MASK - HEAD_DIM) & (hidden > 0), negative, extra)
    kaug[:, :HEAD_DIM] = k_ref[:, cols]
    kaug[:, HEAD_DIM:] = extra.astype(jnp.bfloat16)
    vaug[:, :HEAD_DIM] = v_ref[:, cols]
    vaug[:, HEAD_DIM:] = jnp.where(lane < 2, 1.0, 0.0).astype(jnp.bfloat16)
    rt[...] = rt_ref[:, cols]


def query_terms(head, s, q_ref, bias_ref):
    cols = slice(head * HEAD_DIM, (head + 1) * HEAD_DIM)
    q = q_ref[s, :, cols].astype(jnp.float32)
    content = (q + bias_ref[0:1, cols]).astype(jnp.bfloat16).astype(jnp.float32)
    position = (q + bias_ref[1:2, cols]).astype(jnp.bfloat16).astype(jnp.float32)
    segment = q + bias_ref[2:3, cols]
    return content, position, segment


def forward_kernel(
    q_ref, k_ref, v_ref, rt_ref, bias_ref, qinfo_ref, kinfo_ref, rank_ref,
    p_ref, a_ref, mix_ref, kaug_ref, vaug_ref, table_ref, qaug,
):
    step = pl.program_id(0)
    keys = k_ref.shape[0]
    prompt = keys - LEN
    heads = p_ref.shape[0]

    @pl.when(step == 0)
    def _():
        for head in range(heads):
            prepare_keys(
                head, k_ref, v_ref, rt_ref, kinfo_ref,
                kaug_ref.at[head], vaug_ref.at[head], table_ref.at[head],
            )

    start = pl.multiple_of(LEN - TQ - step * TQ, TQ)
    lane = lax.broadcasted_iota(jnp.int32, (TQ, HEAD_DIM), 1)
    segment_id = qinfo_ref[:, 0:1]
    rank = qinfo_ref[:, 1:2]
    wide = lax.broadcasted_iota(jnp.int32, (TQ, 2 * HEAD_DIM), 1)
    for head, s in [(head, s) for head in range(heads) for s in range(2)]:
        cols = slice(head * HEAD_DIM, (head + 1) * HEAD_DIM)
        table_p = table_ref[head, pl.ds(start, TQ + prompt), :]
        table_c = table_ref[head, pl.ds(pl.multiple_of(LEN + prompt + start, TQ), TQ + LEN), :]
        content, position, with_segment = query_terms(head, s, q_ref, bias_ref)
        same = jnp.sum(with_segment * bias_ref[3:4, cols], axis=1, keepdims=True) * scale_factor
        other = jnp.sum(with_segment * bias_ref[4:5, cols], axis=1, keepdims=True) * scale_factor
        differ = same - other
        differ_high = differ.astype(jnp.bfloat16).astype(jnp.float32)
        other_high = other.astype(jnp.bfloat16).astype(jnp.float32)
        extra = jnp.where(lane == segment_id, differ_high, 0.0)
        extra = jnp.where(lane - SEGMENTS == segment_id, differ - differ_high, extra)
        extra = jnp.where(lane == COL_ONE - HEAD_DIM, other_high, extra)
        extra = jnp.where(lane == COL_ONE_LOW - HEAD_DIM, other - other_high, extra)
        extra = jnp.where(lane == COL_MASK - HEAD_DIM, 1.0, extra)
        qaug[:, :HEAD_DIM] = (content * scale_factor).astype(jnp.bfloat16)
        qaug[:, HEAD_DIM:] = extra.astype(jnp.bfloat16)
        scores = mm(qaug[...], kaug_ref[head], NT)
        position = (position * scale_factor).astype(jnp.bfloat16)
        band_p = pltpu.roll(
            mm(position, table_p, NT), prompt + 1, axis=1, stride=1, stride_axis=0
        )
        band_c = pltpu.roll(mm(position, table_c, NT), LEN + 1, axis=1, stride=1, stride_axis=0)
        scores_p = scores[:, :prompt] + band_p[:, :prompt]
        scores_c = scores[:, prompt:] + band_c[:, :LEN]
        scores_c = jnp.where(rank_ref[0:1, :] <= rank - s, scores_c, negative)
        largest = jnp.maximum(
            jnp.max(scores_p, axis=1, keepdims=True), jnp.max(scores_c, axis=1, keepdims=True)
        )
        weights_p = jnp.exp(scores_p - largest)
        weights_c = jnp.exp(scores_c - largest)
        mixed = mm(weights_p.astype(jnp.bfloat16), vaug_ref[head, :prompt, :])
        mixed += mm(weights_c.astype(jnp.bfloat16), vaug_ref[head, prompt:, :])
        inverse = 1.0 / mixed[:, HEAD_DIM : HEAD_DIM + 1]
        mixed = mixed * inverse
        a_ref[head, s] = jnp.where(wide < HEAD_DIM, mixed, inverse)
        mix_ref[0, head, :, s * HEAD_DIM : (s + 1) * HEAD_DIM] = mixed[:, :HEAD_DIM].astype(
            jnp.bfloat16
        )
        rows = slice(s * TQ, (s + 1) * TQ)
        p_ref[head, 0, rows, :prompt] = reverse_rows(weights_p).astype(jnp.bfloat16)
        p_ref[head, 0, rows, prompt:] = reverse_rows(weights_c).astype(jnp.bfloat16)


def backward_kernel(
    head, q_ref, bias_ref, qinfo_ref, kaug_ref, vaug_ref, table_ref, p_ref, a_ref, ag_ref,
    dq_ref, dkv_ref, dt_ref, sum_ref,
    agaug, cw, cr, g_all, band_p, band_c, dk_acc, dv_acc, dt_acc,
):
    step = pl.program_id(0)
    keys = kaug_ref.shape[1]
    prompt = keys - LEN
    cols = slice(head * HEAD_DIM, (head + 1) * HEAD_DIM)

    @pl.when(step == 0)
    def _():
        dk_acc[...] = jnp.zeros_like(dk_acc)
        dv_acc[...] = jnp.zeros_like(dv_acc)
        dt_acc[...] = jnp.zeros_like(dt_acc)
        sum_ref[...] = jnp.zeros_like(sum_ref)

    start = pl.multiple_of(LEN - TQ - step * TQ, TQ)
    start_c = pl.multiple_of(LEN + prompt + start, TQ)
    lane = lax.broadcasted_iota(jnp.int32, (TQ, HEAD_DIM), 1)
    segment_id = qinfo_ref[:, 2:3]
    segments = []
    for s in range(2):
        rows = slice(s * TQ, (s + 1) * TQ)
        content, position, with_segment = query_terms(head, s, q_ref, bias_ref)
        cw[rows, :] = reverse_rows(content).astype(jnp.bfloat16)
        cr[rows, :] = reverse_rows(position).astype(jnp.bfloat16)
        segments.append(reverse_rows(with_segment))
        grad = ag_ref[0, 0, :, s * HEAD_DIM : (s + 1) * HEAD_DIM].astype(jnp.float32)
        inverse = a_ref[0, s, :, HEAD_DIM : HEAD_DIM + 1] * scale_factor
        delta = jnp.sum(grad * a_ref[0, s, :, :HEAD_DIM], axis=1, keepdims=True) * inverse
        delta_high = delta.astype(jnp.bfloat16).astype(jnp.float32)
        extra = jnp.where(lane == 0, -delta_high, jnp.where(lane == 1, delta_high - delta, 0.0))
        agaug[rows, :HEAD_DIM] = reverse_rows(grad * inverse).astype(jnp.bfloat16)
        agaug[rows, HEAD_DIM:] = reverse_rows(extra).astype(jnp.bfloat16)
    share_grad = mm(agaug[...], vaug_ref[0], NT)
    g_all[...] = (p_ref[0, 0].astype(jnp.float32) * share_grad).astype(jnp.bfloat16)
    for s in range(2):
        rows = slice(s * TQ, (s + 1) * TQ)
        blank = jnp.zeros((TQ, TQ), jnp.bfloat16)
        wide_p = jnp.concatenate([g_all[rows, :prompt], blank], axis=1)
        wide_c = jnp.concatenate([g_all[rows, prompt:], blank], axis=1)
        band_p[rows, :] = pltpu.roll(wide_p, 0, axis=1, stride=1, stride_axis=0)
        band_c[rows, :] = pltpu.roll(wide_c, 0, axis=1, stride=1, stride_axis=0)
    dv_acc[...] += mm(agaug[:, :HEAD_DIM], p_ref[0, 0], TN)
    dk_acc[...] += mm(cw[...], g_all[...], TN)
    dt_acc[:, pl.ds(start, TQ + prompt)] += mm(cr[...], band_p[...], TN)
    dt_acc[:, pl.ds(start_c, TQ + LEN)] += mm(cr[...], band_c[...], TN)
    query_content = mm(g_all[...], kaug_ref[0])
    query_position = mm(band_p[...], table_ref[0, pl.ds(start, TQ + prompt), :])
    query_position += mm(band_c[...], table_ref[0, pl.ds(start_c, TQ + LEN), :])
    same_vector = bias_ref[3:4, cols]
    other_vector = bias_ref[4:5, cols]

    def add_row(row, value):
        sum_ref[row : row + 1, :] += jnp.sum(value, axis=0, keepdims=True)

    for s in range(2):
        rows = slice(s * TQ, (s + 1) * TQ)
        from_content = query_content[rows, :HEAD_DIM]
        extra = query_content[rows, HEAD_DIM:]
        hit = (lane == segment_id) & (lane < SEGMENTS)
        same = jnp.sum(jnp.where(hit, extra, 0.0), axis=1, keepdims=True)
        other = extra[:, COL_ONE - HEAD_DIM : COL_ONE - HEAD_DIM + 1] - same
        from_segment = same * same_vector + other * other_vector
        from_position = query_position[rows, :]
        total = reverse_rows(from_content + from_position + from_segment)
        dq_ref[0, :, s * HEAD_DIM : (s + 1) * HEAD_DIM] = total.astype(jnp.bfloat16)
        add_row(0, from_content)
        add_row(1, from_position)
        add_row(2, from_segment)
        add_row(3, same * segments[s])
        add_row(4, other * segments[s])

    @pl.when(step == pl.num_programs(0) - 1)
    def _():
        dkv_ref[:, :HEAD_DIM] = dk_acc[...].T.astype(jnp.bfloat16)
        dkv_ref[:, HEAD_DIM:] = (dv_acc[...].T * HEAD_DIM**0.5).astype(jnp.bfloat16)
        dt_ref[...] = dt_acc[...].T.astype(jnp.bfloat16)


def whole(shape):
    return pl.BlockSpec(shape, lambda i: (0,) * len(shape))


def attend_forward(q, k, v, rt, bias, qinfo, kinfo, ranks, tokens):
    keys, width = k.shape
    table = rt.shape[0]
    steps = LEN // TQ
    heads = width // HEAD_DIM
    per = tokens // TQ
    return pl.pallas_call(
        forward_kernel,
        grid=(steps,),
        in_specs=[
            pl.BlockSpec((2, TQ, width), lambda i: (0, i, 0)),
            whole((keys, width)),
            whole((keys, width)),
            whole((table, width)),
            whole(bias.shape),
            pl.BlockSpec((TQ, qinfo.shape[1]), lambda i: (i, 0)),
            whole(kinfo.shape),
            whole(ranks.shape),
        ],
        out_specs=[
            pl.BlockSpec((heads, 1, 2 * TQ, keys), lambda i: (0, i, 0, 0)),
            pl.BlockSpec((heads, 2, TQ, 2 * HEAD_DIM), lambda i: (0, 0, i, 0)),
            pl.BlockSpec((1, heads, TQ, 2 * HEAD_DIM), lambda i: (i // per, 0, i % per, 0)),
            whole((heads, keys, 2 * HEAD_DIM)),
            whole((heads, keys, 2 * HEAD_DIM)),
            whole((heads, table, HEAD_DIM)),
        ],
        out_shape=[
            jax.ShapeDtypeStruct((heads, steps, 2 * TQ, keys), jnp.bfloat16),
            jax.ShapeDtypeStruct((heads, 2, LEN, 2 * HEAD_DIM), jnp.float32),
            jax.ShapeDtypeStruct((LEN // tokens, heads, tokens, 2 * HEAD_DIM), jnp.bfloat16),
            jax.ShapeDtypeStruct((heads, keys, 2 * HEAD_DIM), jnp.bfloat16),
            jax.ShapeDtypeStruct((heads, keys, 2 * HEAD_DIM), jnp.bfloat16),
            jax.ShapeDtypeStruct((heads, table, HEAD_DIM), jnp.bfloat16),
        ],
        scratch_shapes=[pltpu.VMEM((TQ, 2 * HEAD_DIM), jnp.bfloat16)],
        compiler_params=pltpu.CompilerParams(vmem_limit_bytes=56 * 2**20),
        cost_estimate=pl.CostEstimate(
            flops=heads * 6 * 2 * LEN * keys * 256,
            bytes_accessed=heads * 2 * LEN * keys * 2,
            transcendentals=heads * 2 * LEN * keys,
        ),
        name="attend_forward",
    )(q, k, v, rt, bias, qinfo, kinfo, ranks)


def attend_backward(head, q, bias, qinfo, kaug, vaug, rows_of, p, a, ag):
    _, keys, wide = kaug.shape
    table = rows_of.shape[1]
    width = q.shape[2]
    steps = LEN // TQ
    prompt = keys - LEN
    members, heads, tokens, _ = ag.shape
    per = tokens // TQ

    def one(shape):
        return pl.BlockSpec((1,) + shape, lambda i: (head,) + (0,) * len(shape))

    return pl.pallas_call(
        partial(backward_kernel, head),
        grid=(steps,),
        in_specs=[
            pl.BlockSpec((2, TQ, width), lambda i: (0, i, 0)),
            whole(bias.shape),
            pl.BlockSpec((TQ, qinfo.shape[1]), lambda i: (i, 0)),
            one((keys, wide)),
            one((keys, wide)),
            one((table, HEAD_DIM)),
            pl.BlockSpec((1, 1, 2 * TQ, keys), lambda i: (head, i, 0, 0)),
            pl.BlockSpec((1, 2, TQ, wide), lambda i: (head, 0, i, 0)),
            pl.BlockSpec((1, 1, TQ, wide), lambda i: (i // per, head, i % per, 0)),
        ],
        out_specs=[
            pl.BlockSpec((1, TQ, wide), lambda i: (i // per, i % per, 0)),
            whole((keys, wide)),
            whole((table, HEAD_DIM)),
            whole((8, HEAD_DIM)),
        ],
        out_shape=[
            jax.ShapeDtypeStruct((members, tokens, wide), jnp.bfloat16),
            jax.ShapeDtypeStruct((keys, wide), jnp.bfloat16),
            jax.ShapeDtypeStruct((table, HEAD_DIM), jnp.bfloat16),
            jax.ShapeDtypeStruct((8, HEAD_DIM), jnp.float32),
        ],
        scratch_shapes=[
            pltpu.VMEM((2 * TQ, wide), jnp.bfloat16),
            pltpu.VMEM((2 * TQ, HEAD_DIM), jnp.bfloat16),
            pltpu.VMEM((2 * TQ, HEAD_DIM), jnp.bfloat16),
            pltpu.VMEM((2 * TQ, keys), jnp.bfloat16),
            pltpu.VMEM((2 * TQ, TQ + prompt), jnp.bfloat16),
            pltpu.VMEM((2 * TQ, TQ + LEN), jnp.bfloat16),
            pltpu.VMEM((HEAD_DIM, keys), jnp.float32),
            pltpu.VMEM((HEAD_DIM, keys), jnp.float32),
            pltpu.VMEM((HEAD_DIM, table), jnp.float32),
        ],
        compiler_params=pltpu.CompilerParams(vmem_limit_bytes=56 * 2**20),
        cost_estimate=pl.CostEstimate(
            flops=12 * 2 * LEN * keys * 256, bytes_accessed=2 * LEN * keys * 2, transcendentals=0
        ),
        name="attend_backward",
    )(q, bias, qinfo, kaug, vaug, rows_of, p, a, ag)


def table_kernel(shards, place_ref, *refs):
    pieces, small, rest = refs[:shards], refs[shards : 2 * shards], refs[2 * shards :]
    (
        coarse_ref, fine_ref, weight_ref, rt_ref, position_ref, vector_ref, inner_ref, bias_ref,
        held, sem,
    ) = rest
    _, rows, width = pieces[0].shape
    shard, member = place_ref[0], place_ref[1]
    copies = []
    for m in range(shards):
        spot = pl.multiple_of((shard ^ m) * rows, rows)
        copies.append(
            pltpu.make_async_copy(pieces[m], weight_ref.at[:, pl.ds(spot, rows), :], sem.at[m])
        )
    for copy in copies:
        copy.start()
    for m in range(shards):
        held[m] = small[m][...].astype(jnp.float32)
    bias_ref[...] = held[shard ^ member][0:8, :]
    for w in range(shards):
        block = held[shard ^ w]
        at = slice(w * width, (w + 1) * width)
        vector_ref[0:5, at] = block[5:10, :]
        for j in range(4):
            spot = (w * 4 + j) * width
            inner_ref[0:1, spot : spot + width] = block[10 + j : 11 + j, :]
    half = fine_ref.shape[2]
    fine_sin, fine_cos = fine_ref[0], fine_ref[1]
    step = 64

    def build(i, carry):
        at = pl.ds(pl.multiple_of(i * step, step), step)
        coarse_sin, coarse_cos = coarse_ref[0, pl.ds(i, 1), :], coarse_ref[1, pl.ds(i, 1), :]
        position_ref[at, :half] = (coarse_sin * fine_cos - coarse_cos * fine_sin).astype(
            jnp.bfloat16
        )
        position_ref[at, half:] = (coarse_cos * fine_cos + coarse_sin * fine_sin).astype(
            jnp.bfloat16
        )
        return carry

    lax.fori_loop(0, position_ref.shape[0] // step, build, 0)
    for copy in copies:
        copy.wait()
    block = 256
    relative = weight_ref[3]

    def body(i, carry):
        at = pl.ds(pl.multiple_of(i * block, block), block)
        rt_ref[at, :] = mm(position_ref[at, :], relative).astype(jnp.bfloat16)
        return carry

    lax.fori_loop(0, position_ref.shape[0] // block, body, 0)


def project_table(place, pieces, small, coarse, fine):
    _, rows, width = pieces[0].shape
    shards = len(pieces)
    table = coarse.shape[1] * fine.shape[1]
    vmem = pl.BlockSpec(memory_space=pltpu.VMEM)
    return pl.pallas_call(
        partial(table_kernel, shards),
        in_specs=[pl.BlockSpec(memory_space=pltpu.SMEM)]
        + [pl.BlockSpec(memory_space=pl.ANY)] * shards
        + [vmem] * (shards + 2),
        out_specs=[vmem] * 6,
        out_shape=[
            jax.ShapeDtypeStruct((4, shards * rows, width), jnp.bfloat16),
            jax.ShapeDtypeStruct((table, width), jnp.bfloat16),
            jax.ShapeDtypeStruct((table, D), jnp.bfloat16),
            jax.ShapeDtypeStruct((8, D), jnp.float32),
            jax.ShapeDtypeStruct((1, 4 * D), jnp.float32),
            jax.ShapeDtypeStruct((8, width), jnp.float32),
        ],
        scratch_shapes=[
            pltpu.VMEM((shards,) + small[0].shape, jnp.float32),
            pltpu.SemaphoreType.DMA((shards,)),
        ],
        compiler_params=pltpu.CompilerParams(vmem_limit_bytes=48 * 2**20),
        name="project_table",
    )(place, *pieces, *small, coarse, fine)


def states_kernel(members, place_ref, *refs):
    pieces, (prompt_ref, weight_ref, q_ref, k_ref, v_ref, states_ref, sem) = (
        (refs[:members], refs[members : 2 * members]),
        refs[2 * members :],
    )
    tokens = pieces[0][0].shape[0]
    prompt = prompt_ref.shape[0]
    copies = [pltpu.make_async_copy(prompt_ref, states_ref.at[pl.ds(0, prompt)], sem.at[0])]
    for s in range(2):
        for m, piece in enumerate(pieces[s]):
            spot = prompt + s * LEN + pl.multiple_of((place_ref[1] ^ m) * tokens, tokens)
            copies.append(
                pltpu.make_async_copy(
                    piece, states_ref.at[pl.ds(spot, tokens)], sem.at[1 + 2 * m + s]
                )
            )
    for copy in copies:
        copy.start()
    for copy in copies:
        copy.wait()
    step = 256
    query, key, value = weight_ref[0], weight_ref[1], weight_ref[2]
    for i in range(2 * LEN // step):
        rows = states_ref[prompt + i * step : prompt + (i + 1) * step, :]
        stream, at = divmod(i * step, LEN)
        q_ref[stream, at : at + step, :] = mm(rows, query).astype(jnp.bfloat16)
    for i in range((prompt + LEN) // step):
        rows = states_ref[i * step : (i + 1) * step, :]
        k_ref[i * step : (i + 1) * step, :] = mm(rows, key).astype(jnp.bfloat16)
        v_ref[i * step : (i + 1) * step, :] = mm(rows, value).astype(jnp.bfloat16)


def project_states(place, content, query, prompt_all, weights):
    members = len(content)
    width = weights.shape[2]
    prompt = prompt_all.shape[0]
    return pl.pallas_call(
        partial(states_kernel, members),
        in_specs=[pl.BlockSpec(memory_space=pltpu.SMEM)]
        + [pl.BlockSpec(memory_space=pl.ANY)] * (2 * members + 1)
        + [pl.BlockSpec(memory_space=pltpu.VMEM)],
        out_specs=[pl.BlockSpec(memory_space=pltpu.VMEM)] * 4,
        out_shape=[
            jax.ShapeDtypeStruct((2, LEN, width), jnp.bfloat16),
            jax.ShapeDtypeStruct((prompt + LEN, width), jnp.bfloat16),
            jax.ShapeDtypeStruct((prompt + LEN, width), jnp.bfloat16),
            jax.ShapeDtypeStruct((prompt + 2 * LEN, D), jnp.bfloat16),
        ],
        scratch_shapes=[pltpu.SemaphoreType.DMA((1 + 2 * members,))],
        compiler_params=pltpu.CompilerParams(vmem_limit_bytes=48 * 2**20),
        name="project_states",
    )(place, *content, *query, prompt_all, weights)


def normalise(x):
    center = x - jnp.mean(x, axis=1, keepdims=True)
    inverse = lax.rsqrt(jnp.mean(center * center, axis=1, keepdims=True) + epsilon)
    return center * inverse, inverse


def norm_backward(grad, unit, inverse, gain):
    scaled = grad * gain
    mean = jnp.mean(scaled, axis=1, keepdims=True)
    along = jnp.mean(scaled * unit, axis=1, keepdims=True)
    return (scaled - mean - unit * along) * inverse


def layer_kernel(
    a_ref, content_ref, query_ref, up_content_ref, up_query_ref, vector_ref, inner_ref,
    output_hbm, hidden_hbm, return_hbm,
    out_content_ref, out_query_ref, flat_ref, inner_in_ref, active_ref, returned_ref, zgrad_ref,
    residual_ref, branch_ref, ag_ref, sum_ref, inner_sum_ref,
    output_w, hidden_w, return_w, flat, inner_in, slope, acc, unit, sem,
):
    members, heads, tokens, _ = a_ref.shape
    shards, _, rows_w = flat_ref.shape
    copies = [
        pltpu.make_async_copy(output_hbm, output_w, sem.at[0]),
        pltpu.make_async_copy(hidden_hbm, hidden_w, sem.at[1]),
        pltpu.make_async_copy(return_hbm, return_w, sem.at[2]),
    ]
    for copy in copies:
        copy.start()
    for g in range(members):
        for h in range(heads):
            spot = (g * heads + h) * HEAD_DIM
            for s in range(2):
                flat[s * tokens : (s + 1) * tokens, spot : spot + HEAD_DIM] = a_ref[
                    g, h, :, s * HEAD_DIM : (s + 1) * HEAD_DIM
                ]
    for w in range(shards):
        flat_ref[w] = flat[:, w * rows_w : (w + 1) * rows_w]
    gain, shift, outer, final_gain, final_shift = (vector_ref[i : i + 1, :] for i in range(5))
    copies[0].wait()
    inverses = []
    for s, source in enumerate((content_ref, query_ref)):
        at = slice(s * tokens, (s + 1) * tokens)
        mixed = mm(flat[at, :], output_w[...])
        normal, inverse = normalise(source[...].astype(jnp.float32) + mixed)
        inverses.append(inverse)
        unit[at, :] = normal
        middle = normal * gain + shift
        low = middle.astype(jnp.bfloat16)
        inner_in[at, :] = low
        for w in range(shards):
            inner_in_ref[w, at, :] = low[:, w * rows_w : (w + 1) * rows_w]
        acc[at, :] = middle + outer
    copies[1].wait()
    copies[2].wait()
    step = 1024
    chunks = hidden_w.shape[1] // step
    root = 0.7978845608028654

    def forward(i, carry):
        at = pl.ds(pl.multiple_of(i * step, step), step)
        for s in range(2):
            part = slice(s * tokens, (s + 1) * tokens)
            z = mm(inner_in[part, :], hidden_w[:, at]) + inner_ref[:, at]
            square = z * z
            curve = jnp.tanh(root * (z + 0.044715 * (z * square)))
            half = 0.5 + 0.5 * curve
            active = (z * half).astype(jnp.bfloat16)
            slope[part, at] = half + (0.5 * root) * z * (1.0 - curve * curve) * (
                1.0 + (3 * 0.044715) * square
            )
            active_ref[part, at] = active
            acc[part, :] += mm(active, return_w[at, :])
        return carry

    lax.fori_loop(0, chunks, forward, 0, unroll=True)
    sums = []
    for s, (upstream, result) in enumerate(
        ((up_content_ref, out_content_ref), (up_query_ref, out_query_ref))
    ):
        at = slice(s * tokens, (s + 1) * tokens)
        normal, inverse = normalise(acc[at, :])
        result[...] = (normal * final_gain + final_shift).astype(jnp.bfloat16)
        grad = upstream[...].astype(jnp.float32)
        back = norm_backward(grad, normal, inverse, final_gain)
        low = back.astype(jnp.bfloat16)
        returned_ref[at, :] = low
        acc[at, :] = back
        sums.append(
            [
                jnp.sum(low.astype(jnp.float32), axis=0, keepdims=True),
                jnp.sum(grad * normal, axis=0, keepdims=True),
                jnp.sum(grad, axis=0, keepdims=True),
            ]
        )
    for i in range(3):
        sum_ref[2 + i : 3 + i, :] = sums[0][i] + sums[1][i]

    def backward(i, carry):
        at = pl.ds(pl.multiple_of(i * step, step), step)
        total = jnp.zeros((1, step), jnp.float32)
        for s in range(2):
            part = slice(s * tokens, (s + 1) * tokens)
            grad = mm(returned_ref[part, :], return_w[at, :], NT) * slope[part, at]
            low = grad.astype(jnp.bfloat16)
            zgrad_ref[part, at] = low
            total += jnp.sum(low.astype(jnp.float32), axis=0, keepdims=True)
            acc[part, :] += mm(low, hidden_w[:, at], NT)
        inner_sum_ref[:, at] = total
        return carry

    lax.fori_loop(0, chunks, backward, 0, unroll=True)
    sums = []
    for s in range(2):
        at = slice(s * tokens, (s + 1) * tokens)
        grad = acc[at, :]
        normal = unit[at, :]
        back = norm_backward(grad, normal, inverses[s], gain)
        residual_ref[at, :] = back
        low = back.astype(jnp.bfloat16)
        branch_ref[at, :] = low
        sums.append(
            [
                jnp.sum(grad * normal, axis=0, keepdims=True),
                jnp.sum(grad, axis=0, keepdims=True),
            ]
        )
        mixed = mm(low, output_w[...], NT).astype(jnp.bfloat16)
        for g in range(members):
            for h in range(heads):
                spot = (g * heads + h) * HEAD_DIM
                ag_ref[g, h, :, s * HEAD_DIM : (s + 1) * HEAD_DIM] = mixed[
                    :, spot : spot + HEAD_DIM
                ]
    for i in range(2):
        sum_ref[i : i + 1, :] = sums[0][i] + sums[1][i]


def layer(shards, a, content, query, up_content, up_query, vectors, inner, output_w, hidden_w, return_w):
    tokens = content.shape[0]
    rows = 2 * tokens
    hidden = hidden_w.shape[1]
    vmem = pl.BlockSpec(memory_space=pltpu.VMEM)
    low = partial(jax.ShapeDtypeStruct, dtype=jnp.bfloat16)
    wide = partial(jax.ShapeDtypeStruct, dtype=jnp.float32)
    return pl.pallas_call(
        layer_kernel,
        in_specs=[vmem] * 7 + [pl.BlockSpec(memory_space=pl.ANY)] * 3,
        out_specs=[vmem] * 12,
        out_shape=[
            low((tokens, D)),
            low((tokens, D)),
            low((shards, rows, D // shards)),
            low((shards, rows, D // shards)),
            low((rows, hidden)),
            low((rows, D)),
            low((rows, hidden)),
            wide((rows, D)),
            low((rows, D)),
            low(a.shape),
            wide((5, D)),
            wide((1, hidden)),
        ],
        scratch_shapes=[
            pltpu.VMEM((D, D), jnp.bfloat16),
            pltpu.VMEM((D, hidden), jnp.bfloat16),
            pltpu.VMEM((hidden, D), jnp.bfloat16),
            pltpu.VMEM((rows, D), jnp.bfloat16),
            pltpu.VMEM((rows, D), jnp.bfloat16),
            pltpu.VMEM((rows, hidden), jnp.float32),
            pltpu.VMEM((rows, D), jnp.float32),
            pltpu.VMEM((rows, D), jnp.float32),
            pltpu.SemaphoreType.DMA((3,)),
        ],
        compiler_params=pltpu.CompilerParams(vmem_limit_bytes=60 * 2**20),
        cost_estimate=pl.CostEstimate(
            flops=8 * rows * D * hidden, bytes_accessed=24 * 2**20, transcendentals=rows * hidden
        ),
        name="layer",
    )(a, content, query, up_content, up_query, vectors, inner, output_w, hidden_w, return_w)


def shard_grads(inner_ref, active_ref, mixed_ref, returned_ref, zgrad_ref, branch_ref):
    rows_w = inner_ref.shape[2]
    count = zgrad_ref.shape[1] // D
    hidden = mm(inner_ref[0], zgrad_ref[...], TN)
    back = mm(active_ref[...], returned_ref[...], TN)
    hidden = [hidden[:, j * D : (j + 1) * D] for j in range(count)]
    back = [back[j * rows_w : (j + 1) * rows_w] for j in range(count)]
    mixed = mm(mixed_ref[0], branch_ref[...], TN)
    return hidden[:3] + back[:3] + [hidden[3], back[3], mixed]


def send_grads_kernel(
    place_ref, active_ref, inner_ref, mixed_ref, returned_ref, zgrad_ref, branch_ref, out_ref
):
    rows_w = inner_ref.shape[2]
    blocks = shard_grads(
        inner_ref, active_ref, mixed_ref, returned_ref, zgrad_ref, branch_ref
    )
    for i, block in enumerate(blocks):
        out_ref[0, i * rows_w : (i + 1) * rows_w, :] = block.astype(jnp.bfloat16)


def keep_grads_kernel(
    place_ref, active_ref, inner_ref, mixed_ref, returned_ref, zgrad_ref, branch_ref, other_ref,
    keep_y, send_y, keep_x, send_x, keep_z, send_z,
):
    rows_w = inner_ref.shape[2]
    step = pl.program_id(0)
    blocks = shard_grads(
        inner_ref, active_ref, mixed_ref, returned_ref, zgrad_ref, branch_ref
    )
    sums = []
    for i, block in enumerate(blocks):
        other = other_ref[0, i * rows_w : (i + 1) * rows_w, :].astype(jnp.float32)
        sums.append((block + other).astype(jnp.bfloat16))
    chains = [jnp.concatenate(sums[i : i + 3], axis=0) for i in (0, 3, 6)]
    half = chains[0].shape[0] // 2
    own_y, own_x, own_z = place_ref[1], place_ref[2], place_ref[3]

    @pl.when(step == own_y)
    def _():
        keep_y[0] = chains[0]

    @pl.when(step != own_y)
    def _():
        send_y[0] = chains[0]

    for chain, own, keep, send in (
        (chains[1], own_x, keep_x, send_x),
        (chains[2], own_z, keep_z, send_z),
    ):
        keep[0] = jnp.where(own == 0, chain[:half], chain[half:])
        send[0] = jnp.where(own == 0, chain[half:], chain[:half])


def token_grads(place, grads, other=None):
    active, inner = grads[:2]
    shards, rows, rows_w = inner.shape
    hidden = active.shape[1]
    per = hidden // shards
    pairs = shards // 2
    low = partial(jax.ShapeDtypeStruct, dtype=jnp.bfloat16)
    whole_block = pl.BlockSpec((1, 9 * rows_w, D), lambda i, c: (i, 0, 0))
    in_specs = [
        pl.BlockSpec((rows, per), lambda i, c: (0, 2 * i + c[0])),
        pl.BlockSpec((1, rows, rows_w), lambda i, c: (2 * i + c[0], 0, 0)),
        pl.BlockSpec((1, rows, rows_w), lambda i, c: (2 * i + c[0], 0, 0)),
        pl.BlockSpec((rows, D), lambda i, c: (0, 0)),
        pl.BlockSpec((rows, hidden), lambda i, c: (0, 0)),
        pl.BlockSpec((rows, D), lambda i, c: (0, 0)),
    ]
    if other is None:
        kernel, operands = send_grads_kernel, tuple(grads)
        out_specs, out_shape = whole_block, low((pairs, 9 * rows_w, D))
    else:
        kernel, operands = keep_grads_kernel, tuple(grads) + (other,)
        in_specs.append(whole_block)
        half = 3 * rows_w // 2
        out_specs = [pl.BlockSpec((1, 3 * rows_w, D), lambda i, c: (0, 0, 0))] * 2
        out_specs += [pl.BlockSpec((1, half, D), lambda i, c: (i, 0, 0))] * 4
        out_shape = [low((1, 3 * rows_w, D))] * 2 + [low((pairs, half, D))] * 4
    return pl.pallas_call(
        kernel,
        grid_spec=pltpu.PrefetchScalarGridSpec(
            num_scalar_prefetch=1, grid=(pairs,), in_specs=in_specs, out_specs=out_specs
        ),
        out_shape=out_shape,
        compiler_params=pltpu.CompilerParams(vmem_limit_bytes=56 * 2**20),
        cost_estimate=pl.CostEstimate(
            flops=2 * rows * D * hidden, bytes_accessed=16 * 2**20, transcendentals=0
        ),
        name="token_grads",
    )(place, *operands)


def unpack_tokens_kernel(members, head_count, place_ref, *refs):
    pieces, (hidden_ref, return_ref, output_ref, held) = refs[: 2 * members], refs[2 * members :]
    rows_w = hidden_ref.shape[0]
    chains, per, _ = held.shape[1:]
    for m in range(members):
        held[m, : chains - 1] = pieces[m][...]
        held[m, chains - 1 :] = pieces[members + m][...]
    member = place_ref[1]
    for g in range(members):
        head, half = g % head_count, g // head_count
        for c in range(chains):
            if c == 2:
                spot = (half * head_count + head) * per
            else:
                spot = (head * (members // head_count) + half) * per
            row = c * members * per + spot
            done = 0
            while done < per:
                block, at = divmod(row + done, rows_w)
                count = min(per - done, rows_w - at)
                value = held[member ^ g, c, done : done + count, :].astype(jnp.float32)
                if block == 8:
                    output_ref[at : at + count, :] = value
                elif block in (0, 1, 2, 6):
                    j = min(block, 3)
                    hidden_ref[at : at + count, j * D : (j + 1) * D] = value
                else:
                    j = min(block - 3, 3)
                    return_ref[j * rows_w + at : j * rows_w + at + count, :] = value
                done += count


def unpack_tokens(place, rows_w, head_count, early, late):
    members = len(early)
    vmem = pl.BlockSpec(memory_space=pltpu.VMEM)
    chains = early[0].shape[0] + late[0].shape[0]
    return pl.pallas_call(
        partial(unpack_tokens_kernel, members, head_count),
        in_specs=[pl.BlockSpec(memory_space=pltpu.SMEM)] + [vmem] * 2 * members,
        out_specs=[vmem] * 3,
        out_shape=[
            jax.ShapeDtypeStruct((rows_w, 4 * D), jnp.float32),
            jax.ShapeDtypeStruct((4 * rows_w, D), jnp.float32),
            jax.ShapeDtypeStruct((rows_w, D), jnp.float32),
        ],
        scratch_shapes=[pltpu.VMEM((members, chains) + early[0].shape[1:], jnp.bfloat16)],
        compiler_params=pltpu.CompilerParams(vmem_limit_bytes=48 * 2**20),
        name="unpack_tokens",
    )(place, *early, *late)


def head_grads_kernel(shards, heads, place_ref, states_ref, position_ref, *rest):
    dq, dkv, dt = (rest[i * heads : (i + 1) * heads] for i in range(3))
    small, out_ref = rest[3 * heads : -1], rest[-1]
    keys = dkv[0].shape[0]
    prompt = keys - LEN
    rows_w = D // shards
    wide = 2 * HEAD_DIM
    side = partial(jnp.concatenate, axis=1)
    dq = side([ref[...].reshape(LEN, wide) for ref in dq])
    key_value = mm(side([ref[...] for ref in dkv]), states_ref[:keys, :], TN)
    content = mm(dq, states_ref[prompt:keys, :], TN)
    query = mm(dq, states_ref[keys:, :], TN)
    table = mm(side([ref[...] for ref in dt]), position_ref[...], TN)
    parts = []
    for h in range(heads):
        at = h * wide
        parts += [
            content[at : at + HEAD_DIM] + query[at + HEAD_DIM : at + wide],
            key_value[at : at + wide],
            table[h * HEAD_DIM : (h + 1) * HEAD_DIM],
        ]
    turned = jnp.concatenate(parts, axis=0).T.astype(jnp.bfloat16)
    for w in range(shards):
        out_ref[w, :rows_w, :] = turned[w * rows_w : (w + 1) * rows_w, :]
    if small:
        token_ref, inner_ref, sums = small[0], small[1], small[2:]
        member = place_ref[1]
        out_ref[:, rows_w:, :] = jnp.zeros_like(out_ref[:, rows_w:, :])
        own_sums = side([ref[0:5, :] for ref in sums])
        for w in range(shards):
            own = jnp.where(member == w, own_sums, 0.0)
            parts = [token_ref[0:5, w * rows_w : (w + 1) * rows_w], own]
            parts += [
                inner_ref[0:1, (4 * w + j) * rows_w : (4 * w + j + 1) * rows_w] for j in range(4)
            ]
            parts.append(jnp.zeros((2, rows_w), jnp.float32))
            out_ref[w, rows_w : rows_w + 16, :rows_w] = jnp.concatenate(parts, axis=0).astype(
                jnp.bfloat16
            )


def head_grads(place, shards, states, positions, dq, dkv, dt, small=()):
    vmem = pl.BlockSpec(memory_space=pltpu.VMEM)
    heads = len(dq)
    operands = (states, positions) + tuple(dq) + tuple(dkv) + tuple(dt) + tuple(small)
    rows = D // shards + (16 if small else 0)
    return pl.pallas_call(
        partial(head_grads_kernel, shards, heads),
        in_specs=[pl.BlockSpec(memory_space=pltpu.SMEM)] + [vmem] * len(operands),
        out_specs=vmem,
        out_shape=jax.ShapeDtypeStruct((shards, rows, 4 * HEAD_DIM * heads), jnp.bfloat16),
        compiler_params=pltpu.CompilerParams(vmem_limit_bytes=56 * 2**20),
        cost_estimate=pl.CostEstimate(
            flops=2 * 6656 * D * 256, bytes_accessed=12 * 2**20, transcendentals=0
        ),
        name="head_grads",
    )(place, *operands)


def unpack_kernel(members, groups, place_ref, *refs):
    pieces = [refs[i * members : (i + 1) * members] for i in range(groups)]
    outs = refs[groups * members : groups * members + 4]
    small_ref = refs[groups * members + 4]
    held = refs[groups * members + 5 : groups * members + 5 + groups]
    rows_w = outs[0].shape[0]
    for i in range(groups):
        for m in range(members):
            held[i][m] = pieces[i][m][...]
    member = place_ref[1]
    for g in range(members):
        head = 0
        for i in range(groups):
            block = held[i][member ^ g].astype(jnp.float32)
            for j in range(block.shape[1] // (4 * HEAD_DIM)):
                spot = (g * groups_heads(held) + head) * HEAD_DIM
                for kind in range(4):
                    at = (4 * j + kind) * HEAD_DIM
                    outs[kind][:, spot : spot + HEAD_DIM] = block[:rows_w, at : at + HEAD_DIM]
                head += 1
    last = held[-1]
    total = last[0, rows_w : rows_w + 16, :].astype(jnp.float32)
    for m in range(1, members):
        total += last[m, rows_w : rows_w + 16, :].astype(jnp.float32)
    small_ref[...] = total


def groups_heads(held):
    return sum(ref.shape[2] // (4 * HEAD_DIM) for ref in held)


def unpack(place, rows_w, *pieces):
    members = len(pieces[0])
    vmem = pl.BlockSpec(memory_space=pltpu.VMEM)
    flat = [x for group in pieces for x in group]
    return pl.pallas_call(
        partial(unpack_kernel, members, len(pieces)),
        in_specs=[pl.BlockSpec(memory_space=pltpu.SMEM)] + [vmem] * len(flat),
        out_specs=[vmem] * 5,
        out_shape=[jax.ShapeDtypeStruct((rows_w, D), jnp.float32)] * 4
        + [jax.ShapeDtypeStruct((16, 4 * HEAD_DIM), jnp.float32)],
        scratch_shapes=[pltpu.VMEM((members,) + group[0].shape, jnp.bfloat16) for group in pieces],
        compiler_params=pltpu.CompilerParams(vmem_limit_bytes=48 * 2**20),
        name="unpack",
    )(place, *flat)


def finish_kernel(
    early_ref, late_ref, prompt_ref, residual_ref, weight_hbm,
    content_ref, query_ref, out_prompt_ref, weight, parts, prompts, sem,
):
    copy = pltpu.make_async_copy(weight_hbm, weight, sem)
    copy.start()
    members, before, _, _ = early_ref.shape
    tokens = content_ref.shape[0]
    heads = before + late_ref.shape[1]
    for g in range(members):
        for h in range(heads):
            spot = (g * heads + h) * HEAD_DIM
            source, i = (early_ref, h) if h < before else (late_ref, h - before)
            for kind in range(4):
                at = (kind % 2) * HEAD_DIM
                start = (kind // 2) * tokens
                parts[kind, :, spot : spot + HEAD_DIM] = source[
                    g, i, start : start + tokens, at : at + HEAD_DIM
                ]
            for kind in range(2):
                prompts[kind, :, spot : spot + HEAD_DIM] = prompt_ref[
                    g, h, :, kind * HEAD_DIM : (kind + 1) * HEAD_DIM
                ]
    copy.wait()
    query, key, value = (weight[:, i * D : (i + 1) * D] for i in range(3))
    content = residual_ref[:tokens, :] + mm(parts[0], query, NT)
    content += mm(parts[2], key, NT)
    content += mm(parts[3], value, NT)
    content_ref[...] = content.astype(jnp.bfloat16)
    query_ref[...] = (residual_ref[tokens:, :] + mm(parts[1], query, NT)).astype(jnp.bfloat16)
    out_prompt_ref[...] = (mm(prompts[0], key, NT) + mm(prompts[1], value, NT)).astype(
        jnp.bfloat16
    )


def finish(rows_early, rows_late, prompt_back, residual, weights):
    tokens = residual.shape[0] // 2
    prompt = prompt_back.shape[2]
    vmem = pl.BlockSpec(memory_space=pltpu.VMEM)
    return pl.pallas_call(
        finish_kernel,
        in_specs=[vmem] * 4 + [pl.BlockSpec(memory_space=pl.ANY)],
        out_specs=[vmem] * 3,
        out_shape=[
            jax.ShapeDtypeStruct((tokens, D), jnp.bfloat16),
            jax.ShapeDtypeStruct((tokens, D), jnp.bfloat16),
            jax.ShapeDtypeStruct((prompt, D), jnp.bfloat16),
        ],
        scratch_shapes=[
            pltpu.VMEM(weights.shape, jnp.bfloat16),
            pltpu.VMEM((4, tokens, D), jnp.bfloat16),
            pltpu.VMEM((2, prompt, D), jnp.bfloat16),
            pltpu.SemaphoreType.DMA,
        ],
        compiler_params=pltpu.CompilerParams(vmem_limit_bytes=48 * 2**20),
        cost_estimate=pl.CostEstimate(
            flops=8 * tokens * D * D, bytes_accessed=8 * 2**20, transcendentals=0
        ),
        name="finish",
    )(rows_early, rows_late, prompt_back, residual, weights)


def axes_size(axes):
    size = 1
    for name in axes:
        size *= lax.axis_size(name)
    return size


def flat_index(axes):
    index = 0
    for name in axes:
        index = index * lax.axis_size(name) + lax.axis_index(name)
    return index


def swap(x, axes, mask):
    return lax.ppermute(x, axes, [(i, i ^ mask) for i in range(axes_size(axes))])


def bits_of(axes):
    return range(axes_size(axes).bit_length() - 1)


def pieces_of(x, axes):
    pieces = {0: x}
    for bit in reversed(bits_of(axes)):
        for mask in list(pieces):
            pieces[mask | 1 << bit] = swap(pieces[mask], axes, 1 << bit)
    return [pieces[m] for m in range(axes_size(axes))]


def in_order(pieces, index):
    count = len(pieces)
    result = jnp.zeros((count,) + pieces[0].shape, pieces[0].dtype)
    for m, piece in enumerate(pieces):
        result = lax.dynamic_update_slice(result, piece[None], (index ^ m,) + (0,) * piece.ndim)
    return result


def pick(x, index, axis=0):
    return lax.dynamic_index_in_dim(x, index, axis, keepdims=False)


def add_low(x, y):
    return (x.astype(jnp.float32) + y.astype(jnp.float32)).astype(jnp.bfloat16)


def half_sum(x, axes, bit, axis):
    own = flat_index(axes) >> bit & 1
    return add_low(pick(x, own, axis), swap(pick(x, 1 - own, axis), axes, 1 << bit))


def split_axis(x, axis):
    return x.reshape(x.shape[:axis] + (2, x.shape[axis] // 2) + x.shape[axis + 1 :])


def stages_of(names):
    return [((name,), bit) for name in names for bit in bits_of((name,))]


def full_sum(x, stages):
    for axes, bit in stages:
        x = add_low(x, swap(x, axes, 1 << bit))
    return x


def group_pieces(x, axes):
    return [x] + [swap(x, axes, m) for m in range(1, axes_size(axes))]


def back_through(grad_rows, weight):
    return jnp.einsum("rc,dc->rd", grad_rows, weight, preferred_element_type=jnp.float32)


def outer_sum(rows_in, grad_rows):
    return jnp.einsum("rd,rc->dc", rows_in, grad_rows, preferred_element_type=jnp.float32)


def sinusoid_rows(first, rows):
    frequency = jnp.asarray(
        np.power(10000.0, -2.0 * np.arange(D // 2) / D).astype(np.float32)
    )
    fine = jnp.arange(64, dtype=jnp.float32)[:, None] * frequency
    coarse = (first - 64 * jnp.arange(rows // 64, dtype=jnp.int32)).astype(jnp.float32)
    coarse = coarse[:, None] * frequency
    fs, fc = jnp.sin(fine)[None], jnp.cos(fine)[None]
    cs, cc = jnp.sin(coarse)[:, None], jnp.cos(coarse)[:, None]
    both = jnp.concatenate([cs * fc - cc * fs, cc * fc + cs * fs], axis=-1)
    return both.reshape(rows, D).astype(jnp.bfloat16)


GROUP = ("half", "head")
JOB = ("cont", "half", "head")
SHARD = ("wshard",)


def per_device(
    prompt_states, content_states, query_states, visible_length, start_offsets,
    prompt_segments, token_segments, order_ranks,
    query_weights, key_weights, value_weights, output_weights, relative_weights,
    content_bias, position_bias, segment_bias, segment_vectors,
    attention_gain, attention_shift, hidden_weights, hidden_bias, return_weights, return_bias,
    final_gain, final_shift, content_upstream, query_upstream,
):
    members = axes_size(GROUP)
    member = flat_index(GROUP)
    shards = lax.axis_size("wshard")
    shard = lax.axis_index("wshard")
    chapters = lax.axis_size("cont")
    chapter = lax.axis_index("cont")
    width = D // members
    local_heads = HEADS // members
    content_rows = content_states[0]
    query_rows = query_states[0]
    tokens = content_rows.shape[0]
    prompt_part = prompt_states.shape[1]
    prompt_total = prompt_segments.shape[1]
    keys = prompt_total + LEN
    rows_w = query_weights.shape[0]

    def columns(x):
        return lax.dynamic_slice_in_dim(x, member * width, width, x.ndim - 1)

    tie = lax.optimization_barrier

    content = {0: content_rows}
    query = {0: query_rows}
    content[1], query[2] = swap(content_rows, GROUP, 1), swap(query_rows, GROUP, 2)
    first_weights = jnp.stack(
        [columns(w) for w in (query_weights, key_weights, value_weights, relative_weights)], axis=0
    )
    small = jnp.concatenate(
        [
            jnp.stack([content_bias, position_bias, segment_bias]),
            segment_vectors,
            jnp.stack([attention_gain, attention_shift, return_bias, final_gain, final_shift]),
            hidden_bias.reshape(-1, rows_w),
            jnp.zeros((2, rows_w), jnp.bfloat16),
        ],
        axis=0,
    )
    first_pieces = pieces_of(first_weights, SHARD)
    small_pieces = pieces_of(small, SHARD)
    query[1], content[2] = swap(query_rows, GROUP, 1), swap(content_rows, GROUP, 2)
    content[3], query[3] = swap(content[1], GROUP, 2), swap(query[2], GROUP, 1)
    prompt_all = lax.all_to_all(
        jnp.broadcast_to(prompt_states, (chapters * members,) + prompt_states.shape[1:]),
        JOB,
        0,
        0,
        tiled=True,
    ).reshape(prompt_total, D)
    output_full = lax.all_gather(output_weights, "wshard", axis=0, tiled=True)
    hidden_full = lax.all_gather(hidden_weights, "wshard", axis=0, tiled=True)
    return_full = lax.all_gather(return_weights, "wshard", axis=0, tiled=True)
    attention_weights = jnp.concatenate([query_weights, key_weights, value_weights], axis=1)
    attention_full = lax.all_gather(attention_weights, "wshard", axis=0, tiled=True)

    seen = pick(visible_length[0], chapter)
    base = seen + pick(start_offsets[0], chapter)
    segments = lax.dynamic_slice_in_dim(token_segments[0], chapter * LEN, LEN)
    ranks = lax.dynamic_slice_in_dim(order_ranks[0], chapter * LEN, LEN)
    reversed_segments = jnp.flip(segments.reshape(-1, TQ), 1).reshape(-1)
    qinfo = jnp.stack([segments, ranks, reversed_segments, segments], axis=1)
    key_segments = jnp.concatenate([prompt_segments[0], segments])
    hidden_keys = (jnp.arange(keys, dtype=jnp.int32) < prompt_total) & (
        jnp.arange(keys, dtype=jnp.int32) >= seen
    )
    kinfo = jnp.stack([key_segments, hidden_keys.astype(jnp.int32)], axis=1)
    place = jnp.stack([shard, member])

    frequency = jnp.asarray(np.power(10000.0, -2.0 * np.arange(D // 2) / D).astype(np.float32))
    starts = jnp.concatenate(
        [
            base + LEN - 1 - 64 * jnp.arange((LEN + prompt_total) // 64, dtype=jnp.int32),
            LEN - 1 - 64 * jnp.arange(2 * LEN // 64, dtype=jnp.int32),
        ]
    )
    coarse = starts.astype(jnp.float32)[:, None] * frequency
    coarse = jnp.stack([jnp.sin(coarse), jnp.cos(coarse)])
    fine = jnp.arange(64, dtype=jnp.float32)[:, None] * frequency
    fine = jnp.stack([jnp.sin(fine), jnp.cos(fine)])

    first_full, rt, positions, vectors, inner_full, head_bias = project_table(
        place, first_pieces, small_pieces, coarse, fine
    )
    q, k, v, states = project_states(
        place,
        [content[m] for m in range(members)],
        [query[m] for m in range(members)],
        prompt_all,
        first_full,
    )
    p, a, mixture, kaug, vaug, table_rows = attend_forward(
        q, k, v, rt, head_bias, qinfo, kinfo, ranks[None], tokens
    )
    mixture = lax.all_to_all(mixture, GROUP, 0, 0, tiled=True)

    (
        out_content, out_query, mixed_flat, inner_in, active, returned_grad, inner_grad,
        residual_grad, branch_grad, grad_out, token_sums, inner_bias_grad,
    ) = layer(
        shards, mixture, content_rows, query_rows, content_upstream[0], query_upstream[0],
        vectors, inner_full, output_full, hidden_full, return_full,
    )
    grad_out, attention_full = lax.optimization_barrier((grad_out, attention_full))
    grad_out = lax.all_to_all(grad_out, GROUP, 0, 0, tiled=True)

    core = shard & 1
    bits = [shard >> 1, lax.axis_index("head"), lax.axis_index("half")]
    grads = (active, inner_in, mixed_flat, returned_grad, inner_grad, branch_grad)
    sent = swap(token_grads(jnp.stack([1 - core] + bits), grads), SHARD, 1)
    parts = token_grads(jnp.stack([core] + bits), grads, sent)
    stage_y, stage_x, stage_z = (SHARD, 1), (("head",), 0), (("half",), 0)
    cont_stage = stages_of(("cont",))
    orders = (
        (stage_y, stage_x, stage_z),
        (stage_x, stage_z, stage_y),
        (stage_z, stage_y, stage_x),
    )
    chains = [
        (kept, swap(out, order[0][0], 1 << order[0][1]))
        for kept, out, order in zip(parts[::2], parts[1::2], orders)
    ]

    def next_stage(chain, stage):
        axes, bit = stage
        x = add_low(*chain)
        axis = 0 if axes == SHARD else 1
        x = split_axis(x, axis)
        own = flat_index(axes) >> bit & 1
        return pick(x, own, axis), swap(pick(x, 1 - own, axis), axes, 1 << bit)

    small_grads = (token_sums, inner_bias_grad)

    def attend_back(h, grad_out):
        return attend_backward(h, q, head_bias, qinfo, kaug, vaug, table_rows, p, a, grad_out)

    last = local_heads - 1
    grad_out, parts = tie((grad_out, parts))
    backward = [attend_back(0, grad_out)]
    grad_out, chains = tie((grad_out, chains))
    chains = [next_stage(x, order[1]) for x, order in zip(chains, orders)]
    backward += [attend_back(h, grad_out) for h in range(1, last)]
    backward, chains = tie((backward, chains))
    chains = [next_stage(x, order[2]) for x, order in zip(chains, orders)]
    dq, dkv, dt, _ = zip(*backward)
    x = head_grads(place, shards, states, positions, dq, dkv, dt)
    x, chains, dq, dkv = tie((x, chains, dq, dkv))
    chains = [add_low(*x) for x in chains]

    def shard_stage(x, bit):
        return half_sum(x.reshape((-1, 2) + x.shape[1:]), SHARD, bit, 1)

    def row_parts(heads):
        parts = []
        for h in heads:
            prompts = dkv[h][:prompt_total].reshape(chapters, members, prompt_part, -1)
            prompts = jnp.transpose(prompts, (1, 0, 2, 3)).reshape(members, -1, dq[h].shape[2])
            own = dkv[h][prompt_total:].reshape(dq[h].shape)
            parts.append(jnp.concatenate([dq[h], own, prompts], axis=1))
        return lax.all_to_all(jnp.stack(parts, axis=1), GROUP, 0, 0, tiled=True)

    first = shard_stage(x, 0)
    grad_out, chains, first = tie((grad_out, chains, first))
    early = full_sum(jnp.concatenate(chains[:2]), cont_stage)
    first = shard_stage(first, 1)
    rows_early = row_parts(range(last))
    backward.append(attend_back(last, grad_out))
    backward[last], late, first, early, rows_early = tie(
        (backward[last], chains[2], first, early, rows_early)
    )
    late = full_sum(late, cont_stage)
    first = full_sum(first[0], cont_stage)
    early_near = [early] + [swap(early, GROUP, 1 << bit) for bit in bits_of(GROUP)]
    early_dq, early_dkv = dq, dkv
    dq, dkv, dt, sums = zip(*backward)
    dq, dkv = early_dq + dq[last:], early_dkv + dkv[last:]
    rows_late = row_parts([last])
    x = head_grads(
        place, shards, states, positions, dq[-1:], dkv[-1:], dt[-1:], small_grads + sums
    )
    x, late, rows_late, first, early_near = tie((x, late, rows_late, first, early_near))
    early_pieces = dict(zip([0] + [1 << bit for bit in bits_of(GROUP)], early_near))
    for m in range(members):
        if m not in early_pieces:
            early_pieces[m] = swap(early_near[0], GROUP, m)
    early_pieces = [early_pieces[m] for m in range(members)]
    late_pieces = group_pieces(late, GROUP)
    prompt_back = jnp.concatenate([rows_early[:, :, 2 * tokens :], rows_late[:, :, 2 * tokens :]], 1)
    prompt_back = prompt_back.reshape(prompt_back.shape[:2] + (chapters, prompt_part, -1))
    prompt_back = jnp.transpose(prompt_back, (2, 0, 1, 3, 4))
    for axes, bit in reversed(cont_stage):
        prompt_back = half_sum(split_axis(prompt_back, 0), axes, bit, 0)
    second = shard_stage(shard_stage(x, 0), 1)
    first = group_pieces(first, GROUP)
    second = full_sum(second[0], cont_stage)
    second, early_pieces, late_pieces, prompt_back = tie(
        (second, early_pieces, late_pieces, prompt_back)
    )
    head_pieces = [first, group_pieces(second, GROUP)]

    hidden_total, return_total, output_total = unpack_tokens(
        place, rows_w, lax.axis_size("head"), early_pieces, late_pieces
    )
    query_grad, key_grad, value_grad, relative_grad, small_total = unpack(
        place, rows_w, *head_pieces
    )
    vector_total = small_total[:10, :rows_w]
    inner_total = small_total[10:14, :rows_w].reshape(-1)
    content_grad, queries_grad, prompt_grad = finish(
        rows_early, rows_late, prompt_back[0], residual_grad, attention_full
    )
    return (
        out_content[None],
        out_query[None],
        prompt_grad[None],
        content_grad[None],
        queries_grad[None],
        query_grad,
        key_grad,
        value_grad,
        output_total,
        relative_grad,
        vector_total[5],
        vector_total[6],
        vector_total[7],
        vector_total[8:10],
        vector_total[0],
        vector_total[1],
        hidden_total,
        inner_total,
        return_total,
        vector_total[2],
        vector_total[3],
        vector_total[4],
    )


def solution(mesh):
    rows = P("wshard", JOB, None)
    job = P("wshard", None)
    matrix = P("wshard", None)
    vector = P("wshard")
    pair = P(None, "wshard")
    in_specs = (
        (rows,) * 3 + (job,) * 5 + (matrix,) * 5 + (vector,) * 3 + (pair,)
        + (vector, vector, matrix, vector, matrix, vector, vector, vector, rows, rows)
    )
    out_specs = (
        (rows,) * 5 + (matrix,) * 5 + (vector,) * 3 + (pair,)
        + (vector, vector, matrix, vector, matrix, vector, vector, vector)
    )

    def run(*arguments):
        seq_count, head_count, shard_count = mesh.devices.shape
        tokens = arguments[1].shape[1] // (seq_count * head_count)
        halves = LEN // (tokens * head_count)
        split = Mesh(
            mesh.devices.reshape(seq_count // halves, halves, head_count, shard_count),
            ("cont", "half", "head", "wshard"),
        )
        return jax.shard_map(
            per_device, mesh=split, in_specs=in_specs, out_specs=out_specs, check_vma=False
        )(*arguments)

    return run
```

```python
from functools import partial

import jax
import jax.numpy as jnp
import numpy as np
from jax import lax
from jax.experimental import pallas as pl
from jax.experimental.pallas import tpu as pltpu
from jax.sharding import Mesh, PartitionSpec as P

D = 768
HEADS = 12
HEAD_DIM = 64
LEN = 1024
SEGMENTS = 4
TQ = 128

negative = -1e30
epsilon = 1e-06
scale_factor = HEAD_DIM ** (-0.5)
NT = (((1,), (1,)), ((), ()))
NN = (((1,), (0,)), ((), ()))
TN = (((0,), (0,)), ((), ()))

COL_HIGH = HEAD_DIM
COL_LOW = HEAD_DIM + SEGMENTS
COL_ONE = HEAD_DIM + 2 * SEGMENTS
COL_ONE_LOW = COL_ONE + 1
COL_MASK = COL_ONE + 2


def mm(a, b, dims=NN):
    return lax.dot_general(a, b, dims, preferred_element_type=jnp.float32)


def reverse_rows(x):
    groups = x.shape[0] // 8
    index = 7 - lax.broadcasted_iota(jnp.int32, (8, x.shape[1]), 0)
    return jnp.concatenate(
        [
            jnp.take_along_axis(x[8 * (groups - 1 - g) : 8 * (groups - g)], index, axis=0)
            for g in range(groups)
        ],
        axis=0,
    )


def prepare_keys(head, k_ref, v_ref, rt_ref, kinfo_ref, kaug, vaug, rt):
    cols = slice(head * HEAD_DIM, (head + 1) * HEAD_DIM)
    rows = k_ref.shape[0]
    lane = lax.broadcasted_iota(jnp.int32, (rows, HEAD_DIM), 1)
    segment = kinfo_ref[:, 0:1]
    hidden = kinfo_ref[:, 1:2]
    one_hot = ((lane == segment) | (lane - SEGMENTS == segment)) & (lane < 2 * SEGMENTS)
    ones = (lane == COL_ONE - HEAD_DIM) | (lane == COL_ONE_LOW - HEAD_DIM)
    extra = jnp.where(one_hot | ones, 1.0, 0.0)
    extra = jnp.where((lane == COL_MASK - HEAD_DIM) & (hidden > 0), negative, extra)
    kaug[:, :HEAD_DIM] = k_ref[:, cols]
    kaug[:, HEAD_DIM:] = extra.astype(jnp.bfloat16)
    vaug[:, :HEAD_DIM] = v_ref[:, cols]
    vaug[:, HEAD_DIM:] = jnp.where(lane < 2, 1.0, 0.0).astype(jnp.bfloat16)
    rt[...] = rt_ref[:, cols]


def query_terms(head, s, q_ref, bias_ref):
    cols = slice(head * HEAD_DIM, (head + 1) * HEAD_DIM)
    q = q_ref[s, :, cols].astype(jnp.float32)
    content = (q + bias_ref[0:1, cols]).astype(jnp.bfloat16).astype(jnp.float32)
    position = (q + bias_ref[1:2, cols]).astype(jnp.bfloat16).astype(jnp.float32)
    segment = q + bias_ref[2:3, cols]
    return content, position, segment


def forward_kernel(
    q_ref, k_ref, v_ref, rt_ref, bias_ref, qinfo_ref, kinfo_ref, rank_ref,
    p_ref, a_ref, mix_ref, kaug_ref, vaug_ref, table_ref, qaug,
):
    step = pl.program_id(0)
    keys = k_ref.shape[0]
    prompt = keys - LEN
    heads = p_ref.shape[0]

    @pl.when(step == 0)
    def _():
        for head in range(heads):
            prepare_keys(
                head, k_ref, v_ref, rt_ref, kinfo_ref,
                kaug_ref.at[head], vaug_ref.at[head], table_ref.at[head],
            )

    start = pl.multiple_of(LEN - TQ - step * TQ, TQ)
    lane = lax.broadcasted_iota(jnp.int32, (TQ, HEAD_DIM), 1)
    segment_id = qinfo_ref[:, 0:1]
    rank = qinfo_ref[:, 1:2]
    wide = lax.broadcasted_iota(jnp.int32, (TQ, 2 * HEAD_DIM), 1)
    for head, s in [(head, s) for head in range(heads) for s in range(2)]:
        cols = slice(head * HEAD_DIM, (head + 1) * HEAD_DIM)
        table_p = table_ref[head, pl.ds(start, TQ + prompt), :]
        table_c = table_ref[head, pl.ds(pl.multiple_of(LEN + prompt + start, TQ), TQ + LEN), :]
        content, position, with_segment = query_terms(head, s, q_ref, bias_ref)
        same = jnp.sum(with_segment * bias_ref[3:4, cols], axis=1, keepdims=True) * scale_factor
        other = jnp.sum(with_segment * bias_ref[4:5, cols], axis=1, keepdims=True) * scale_factor
        differ = same - other
        differ_high = differ.astype(jnp.bfloat16).astype(jnp.float32)
        other_high = other.astype(jnp.bfloat16).astype(jnp.float32)
        extra = jnp.where(lane == segment_id, differ_high, 0.0)
        extra = jnp.where(lane - SEGMENTS == segment_id, differ - differ_high, extra)
        extra = jnp.where(lane == COL_ONE - HEAD_DIM, other_high, extra)
        extra = jnp.where(lane == COL_ONE_LOW - HEAD_DIM, other - other_high, extra)
        extra = jnp.where(lane == COL_MASK - HEAD_DIM, 1.0, extra)
        qaug[:, :HEAD_DIM] = (content * scale_factor).astype(jnp.bfloat16)
        qaug[:, HEAD_DIM:] = extra.astype(jnp.bfloat16)
        scores = mm(qaug[...], kaug_ref[head], NT)
        position = (position * scale_factor).astype(jnp.bfloat16)
        band_p = mm(position, table_p, NT).astype(jnp.bfloat16)
        band_c = mm(position, table_c, NT).astype(jnp.bfloat16)
        band_p = pltpu.roll(band_p, prompt + 1, axis=1, stride=1, stride_axis=0)
        band_c = pltpu.roll(band_c, LEN + 1, axis=1, stride=1, stride_axis=0)
        scores_p = scores[:, :prompt] + band_p[:, :prompt]
        scores_c = scores[:, prompt:] + band_c[:, :LEN]
        scores_c = jnp.where(rank_ref[0:1, :] <= rank - s, scores_c, negative)
        largest = jnp.maximum(
            jnp.max(scores_p, axis=1, keepdims=True), jnp.max(scores_c, axis=1, keepdims=True)
        )
        weights_p = jnp.exp(scores_p - largest)
        weights_c = jnp.exp(scores_c - largest)
        mixed = mm(weights_p.astype(jnp.bfloat16), vaug_ref[head, :prompt, :])
        mixed += mm(weights_c.astype(jnp.bfloat16), vaug_ref[head, prompt:, :])
        inverse = 1.0 / mixed[:, HEAD_DIM : HEAD_DIM + 1]
        mixed = mixed * inverse
        a_ref[head, s] = jnp.where(wide < HEAD_DIM, mixed, inverse)
        mix_ref[0, head, :, s * HEAD_DIM : (s + 1) * HEAD_DIM] = mixed[:, :HEAD_DIM].astype(
            jnp.bfloat16
        )
        rows = slice(s * TQ, (s + 1) * TQ)
        p_ref[head, 0, rows, :prompt] = reverse_rows(weights_p).astype(jnp.bfloat16)
        p_ref[head, 0, rows, prompt:] = reverse_rows(weights_c).astype(jnp.bfloat16)


def backward_kernel(
    head, q_ref, bias_ref, qinfo_ref, kaug_ref, vaug_ref, table_ref, p_ref, a_ref, ag_ref,
    dq_ref, dkv_ref, dt_ref, sum_ref,
    agaug, cw, cr, g_all, band_p, band_c, dk_acc, dv_acc, dt_acc,
):
    step = pl.program_id(0)
    keys = kaug_ref.shape[1]
    prompt = keys - LEN
    cols = slice(head * HEAD_DIM, (head + 1) * HEAD_DIM)

    @pl.when(step == 0)
    def _():
        dk_acc[...] = jnp.zeros_like(dk_acc)
        dv_acc[...] = jnp.zeros_like(dv_acc)
        dt_acc[...] = jnp.zeros_like(dt_acc)
        sum_ref[...] = jnp.zeros_like(sum_ref)

    start = pl.multiple_of(LEN - TQ - step * TQ, TQ)
    start_c = pl.multiple_of(LEN + prompt + start, TQ)
    lane = lax.broadcasted_iota(jnp.int32, (TQ, HEAD_DIM), 1)
    segment_id = qinfo_ref[:, 2:3]
    segments = []
    for s in range(2):
        rows = slice(s * TQ, (s + 1) * TQ)
        content, position, with_segment = query_terms(head, s, q_ref, bias_ref)
        cw[rows, :] = reverse_rows(content).astype(jnp.bfloat16)
        cr[rows, :] = reverse_rows(position).astype(jnp.bfloat16)
        segments.append(reverse_rows(with_segment))
        grad = ag_ref[0, 0, :, s * HEAD_DIM : (s + 1) * HEAD_DIM].astype(jnp.float32)
        inverse = a_ref[0, s, :, HEAD_DIM : HEAD_DIM + 1] * scale_factor
        delta = jnp.sum(grad * a_ref[0, s, :, :HEAD_DIM], axis=1, keepdims=True) * inverse
        delta_high = delta.astype(jnp.bfloat16).astype(jnp.float32)
        extra = jnp.where(lane == 0, -delta_high, jnp.where(lane == 1, delta_high - delta, 0.0))
        agaug[rows, :HEAD_DIM] = reverse_rows(grad * inverse).astype(jnp.bfloat16)
        agaug[rows, HEAD_DIM:] = reverse_rows(extra).astype(jnp.bfloat16)
    share_grad = mm(agaug[...], vaug_ref[0], NT)
    g_all[...] = (p_ref[0, 0].astype(jnp.float32) * share_grad).astype(jnp.bfloat16)
    for s in range(2):
        rows = slice(s * TQ, (s + 1) * TQ)
        blank = jnp.zeros((TQ, TQ), jnp.bfloat16)
        wide_p = jnp.concatenate([g_all[rows, :prompt], blank], axis=1)
        wide_c = jnp.concatenate([g_all[rows, prompt:], blank], axis=1)
        band_p[rows, :] = pltpu.roll(wide_p, 0, axis=1, stride=1, stride_axis=0)
        band_c[rows, :] = pltpu.roll(wide_c, 0, axis=1, stride=1, stride_axis=0)
    dv_acc[...] += mm(agaug[:, :HEAD_DIM], p_ref[0, 0], TN)
    dk_acc[...] += mm(cw[...], g_all[...], TN)
    dt_acc[:, pl.ds(start, TQ + prompt)] += mm(cr[...], band_p[...], TN)
    dt_acc[:, pl.ds(start_c, TQ + LEN)] += mm(cr[...], band_c[...], TN)
    query_content = mm(g_all[...], kaug_ref[0])
    query_position = mm(band_p[...], table_ref[0, pl.ds(start, TQ + prompt), :])
    query_position += mm(band_c[...], table_ref[0, pl.ds(start_c, TQ + LEN), :])
    same_vector = bias_ref[3:4, cols]
    other_vector = bias_ref[4:5, cols]

    def add_row(row, value):
        sum_ref[row : row + 1, :] += jnp.sum(value, axis=0, keepdims=True)

    for s in range(2):
        rows = slice(s * TQ, (s + 1) * TQ)
        from_content = query_content[rows, :HEAD_DIM]
        extra = query_content[rows, HEAD_DIM:]
        hit = (lane == segment_id) & (lane < SEGMENTS)
        same = jnp.sum(jnp.where(hit, extra, 0.0), axis=1, keepdims=True)
        other = extra[:, COL_ONE - HEAD_DIM : COL_ONE - HEAD_DIM + 1] - same
        from_segment = same * same_vector + other * other_vector
        from_position = query_position[rows, :]
        total = reverse_rows(from_content + from_position + from_segment)
        dq_ref[0, :, s * HEAD_DIM : (s + 1) * HEAD_DIM] = total.astype(jnp.bfloat16)
        add_row(0, from_content)
        add_row(1, from_position)
        add_row(2, from_segment)
        add_row(3, same * segments[s])
        add_row(4, other * segments[s])

    @pl.when(step == pl.num_programs(0) - 1)
    def _():
        dkv_ref[:, :HEAD_DIM] = dk_acc[...].T.astype(jnp.bfloat16)
        dkv_ref[:, HEAD_DIM:] = (dv_acc[...].T * HEAD_DIM**0.5).astype(jnp.bfloat16)
        dt_ref[...] = dt_acc[...].T.astype(jnp.bfloat16)


def whole(shape):
    return pl.BlockSpec(shape, lambda i: (0,) * len(shape))


def attend_forward(q, k, v, rt, bias, qinfo, kinfo, ranks, tokens):
    keys, width = k.shape
    table = rt.shape[0]
    steps = LEN // TQ
    heads = width // HEAD_DIM
    per = tokens // TQ
    return pl.pallas_call(
        forward_kernel,
        grid=(steps,),
        in_specs=[
            pl.BlockSpec((2, TQ, width), lambda i: (0, i, 0)),
            whole((keys, width)),
            whole((keys, width)),
            whole((table, width)),
            whole(bias.shape),
            pl.BlockSpec((TQ, qinfo.shape[1]), lambda i: (i, 0)),
            whole(kinfo.shape),
            whole(ranks.shape),
        ],
        out_specs=[
            pl.BlockSpec((heads, 1, 2 * TQ, keys), lambda i: (0, i, 0, 0)),
            pl.BlockSpec((heads, 2, TQ, 2 * HEAD_DIM), lambda i: (0, 0, i, 0)),
            pl.BlockSpec((1, heads, TQ, 2 * HEAD_DIM), lambda i: (i // per, 0, i % per, 0)),
            whole((heads, keys, 2 * HEAD_DIM)),
            whole((heads, keys, 2 * HEAD_DIM)),
            whole((heads, table, HEAD_DIM)),
        ],
        out_shape=[
            jax.ShapeDtypeStruct((heads, steps, 2 * TQ, keys), jnp.bfloat16),
            jax.ShapeDtypeStruct((heads, 2, LEN, 2 * HEAD_DIM), jnp.float32),
            jax.ShapeDtypeStruct((LEN // tokens, heads, tokens, 2 * HEAD_DIM), jnp.bfloat16),
            jax.ShapeDtypeStruct((heads, keys, 2 * HEAD_DIM), jnp.bfloat16),
            jax.ShapeDtypeStruct((heads, keys, 2 * HEAD_DIM), jnp.bfloat16),
            jax.ShapeDtypeStruct((heads, table, HEAD_DIM), jnp.bfloat16),
        ],
        scratch_shapes=[pltpu.VMEM((TQ, 2 * HEAD_DIM), jnp.bfloat16)],
        compiler_params=pltpu.CompilerParams(vmem_limit_bytes=56 * 2**20),
        cost_estimate=pl.CostEstimate(
            flops=heads * 6 * 2 * LEN * keys * 256,
            bytes_accessed=heads * 2 * LEN * keys * 2,
            transcendentals=heads * 2 * LEN * keys,
        ),
        name="attend_forward",
    )(q, k, v, rt, bias, qinfo, kinfo, ranks)


def attend_backward(head, q, bias, qinfo, kaug, vaug, rows_of, p, a, ag):
    _, keys, wide = kaug.shape
    table = rows_of.shape[1]
    width = q.shape[2]
    steps = LEN // TQ
    prompt = keys - LEN
    members, heads, tokens, _ = ag.shape
    per = tokens // TQ

    def one(shape):
        return pl.BlockSpec((1,) + shape, lambda i: (head,) + (0,) * len(shape))

    return pl.pallas_call(
        partial(backward_kernel, head),
        grid=(steps,),
        in_specs=[
            pl.BlockSpec((2, TQ, width), lambda i: (0, i, 0)),
            whole(bias.shape),
            pl.BlockSpec((TQ, qinfo.shape[1]), lambda i: (i, 0)),
            one((keys, wide)),
            one((keys, wide)),
            one((table, HEAD_DIM)),
            pl.BlockSpec((1, 1, 2 * TQ, keys), lambda i: (head, i, 0, 0)),
            pl.BlockSpec((1, 2, TQ, wide), lambda i: (head, 0, i, 0)),
            pl.BlockSpec((1, 1, TQ, wide), lambda i: (i // per, head, i % per, 0)),
        ],
        out_specs=[
            pl.BlockSpec((1, TQ, wide), lambda i: (i // per, i % per, 0)),
            whole((keys, wide)),
            whole((table, HEAD_DIM)),
            whole((8, HEAD_DIM)),
        ],
        out_shape=[
            jax.ShapeDtypeStruct((members, tokens, wide), jnp.bfloat16),
            jax.ShapeDtypeStruct((keys, wide), jnp.bfloat16),
            jax.ShapeDtypeStruct((table, HEAD_DIM), jnp.bfloat16),
            jax.ShapeDtypeStruct((8, HEAD_DIM), jnp.float32),
        ],
        scratch_shapes=[
            pltpu.VMEM((2 * TQ, wide), jnp.bfloat16),
            pltpu.VMEM((2 * TQ, HEAD_DIM), jnp.bfloat16),
            pltpu.VMEM((2 * TQ, HEAD_DIM), jnp.bfloat16),
            pltpu.VMEM((2 * TQ, keys), jnp.bfloat16),
            pltpu.VMEM((2 * TQ, TQ + prompt), jnp.bfloat16),
            pltpu.VMEM((2 * TQ, TQ + LEN), jnp.bfloat16),
            pltpu.VMEM((HEAD_DIM, keys), jnp.float32),
            pltpu.VMEM((HEAD_DIM, keys), jnp.float32),
            pltpu.VMEM((HEAD_DIM, table), jnp.float32),
        ],
        compiler_params=pltpu.CompilerParams(vmem_limit_bytes=56 * 2**20),
        cost_estimate=pl.CostEstimate(
            flops=12 * 2 * LEN * keys * 256, bytes_accessed=2 * LEN * keys * 2, transcendentals=0
        ),
        name="attend_backward",
    )(q, bias, qinfo, kaug, vaug, rows_of, p, a, ag)


def table_kernel(shards, place_ref, *refs):
    pieces, small, rest = refs[:shards], refs[shards : 2 * shards], refs[2 * shards :]
    (
        coarse_ref, fine_ref, weight_ref, rt_ref, position_ref, vector_ref, inner_ref, bias_ref,
        held, sem,
    ) = rest
    _, rows, width = pieces[0].shape
    shard, member = place_ref[0], place_ref[1]
    copies = []
    for m in range(shards):
        spot = pl.multiple_of((shard ^ m) * rows, rows)
        copies.append(
            pltpu.make_async_copy(pieces[m], weight_ref.at[:, pl.ds(spot, rows), :], sem.at[m])
        )
    for copy in copies:
        copy.start()
    for m in range(shards):
        held[m] = small[m][...].astype(jnp.float32)
    bias_ref[...] = held[shard ^ member][0:8, :]
    for w in range(shards):
        block = held[shard ^ w]
        at = slice(w * width, (w + 1) * width)
        vector_ref[0:5, at] = block[5:10, :]
        for j in range(4):
            spot = (w * 4 + j) * width
            inner_ref[0:1, spot : spot + width] = block[10 + j : 11 + j, :]
    half = fine_ref.shape[2]
    fine_sin, fine_cos = fine_ref[0], fine_ref[1]
    step = 64

    def build(i, carry):
        at = pl.ds(pl.multiple_of(i * step, step), step)
        coarse_sin, coarse_cos = coarse_ref[0, pl.ds(i, 1), :], coarse_ref[1, pl.ds(i, 1), :]
        position_ref[at, :half] = (coarse_sin * fine_cos - coarse_cos * fine_sin).astype(
            jnp.bfloat16
        )
        position_ref[at, half:] = (coarse_cos * fine_cos + coarse_sin * fine_sin).astype(
            jnp.bfloat16
        )
        return carry

    lax.fori_loop(0, position_ref.shape[0] // step, build, 0)
    for copy in copies:
        copy.wait()
    block = 256
    relative = weight_ref[3]

    def body(i, carry):
        at = pl.ds(pl.multiple_of(i * block, block), block)
        rt_ref[at, :] = mm(position_ref[at, :], relative).astype(jnp.bfloat16)
        return carry

    lax.fori_loop(0, position_ref.shape[0] // block, body, 0)


def project_table(place, pieces, small, coarse, fine):
    _, rows, width = pieces[0].shape
    shards = len(pieces)
    table = coarse.shape[1] * fine.shape[1]
    vmem = pl.BlockSpec(memory_space=pltpu.VMEM)
    return pl.pallas_call(
        partial(table_kernel, shards),
        in_specs=[pl.BlockSpec(memory_space=pltpu.SMEM)]
        + [pl.BlockSpec(memory_space=pl.ANY)] * shards
        + [vmem] * (shards + 2),
        out_specs=[vmem] * 6,
        out_shape=[
            jax.ShapeDtypeStruct((4, shards * rows, width), jnp.bfloat16),
            jax.ShapeDtypeStruct((table, width), jnp.bfloat16),
            jax.ShapeDtypeStruct((table, D), jnp.bfloat16),
            jax.ShapeDtypeStruct((8, D), jnp.float32),
            jax.ShapeDtypeStruct((1, 4 * D), jnp.float32),
            jax.ShapeDtypeStruct((8, width), jnp.float32),
        ],
        scratch_shapes=[
            pltpu.VMEM((shards,) + small[0].shape, jnp.float32),
            pltpu.SemaphoreType.DMA((shards,)),
        ],
        compiler_params=pltpu.CompilerParams(vmem_limit_bytes=48 * 2**20),
        name="project_table",
    )(place, *pieces, *small, coarse, fine)


def states_kernel(members, place_ref, *refs):
    pieces, (prompt_ref, weight_ref, q_ref, k_ref, v_ref, states_ref, sem) = (
        (refs[:members], refs[members : 2 * members]),
        refs[2 * members :],
    )
    tokens = pieces[0][0].shape[0]
    prompt = prompt_ref.shape[0]
    copies = [pltpu.make_async_copy(prompt_ref, states_ref.at[pl.ds(0, prompt)], sem.at[0])]
    for s in range(2):
        for m, piece in enumerate(pieces[s]):
            spot = prompt + s * LEN + pl.multiple_of((place_ref[1] ^ m) * tokens, tokens)
            copies.append(
                pltpu.make_async_copy(
                    piece, states_ref.at[pl.ds(spot, tokens)], sem.at[1 + 2 * m + s]
                )
            )
    for copy in copies:
        copy.start()
    for copy in copies:
        copy.wait()
    step = 256
    query, key, value = weight_ref[0], weight_ref[1], weight_ref[2]
    for i in range(2 * LEN // step):
        rows = states_ref[prompt + i * step : prompt + (i + 1) * step, :]
        stream, at = divmod(i * step, LEN)
        q_ref[stream, at : at + step, :] = mm(rows, query).astype(jnp.bfloat16)
    for i in range((prompt + LEN) // step):
        rows = states_ref[i * step : (i + 1) * step, :]
        k_ref[i * step : (i + 1) * step, :] = mm(rows, key).astype(jnp.bfloat16)
        v_ref[i * step : (i + 1) * step, :] = mm(rows, value).astype(jnp.bfloat16)


def project_states(place, content, query, prompt_all, weights):
    members = len(content)
    width = weights.shape[2]
    prompt = prompt_all.shape[0]
    return pl.pallas_call(
        partial(states_kernel, members),
        in_specs=[pl.BlockSpec(memory_space=pltpu.SMEM)]
        + [pl.BlockSpec(memory_space=pl.ANY)] * (2 * members + 1)
        + [pl.BlockSpec(memory_space=pltpu.VMEM)],
        out_specs=[pl.BlockSpec(memory_space=pltpu.VMEM)] * 4,
        out_shape=[
            jax.ShapeDtypeStruct((2, LEN, width), jnp.bfloat16),
            jax.ShapeDtypeStruct((prompt + LEN, width), jnp.bfloat16),
            jax.ShapeDtypeStruct((prompt + LEN, width), jnp.bfloat16),
            jax.ShapeDtypeStruct((prompt + 2 * LEN, D), jnp.bfloat16),
        ],
        scratch_shapes=[pltpu.SemaphoreType.DMA((1 + 2 * members,))],
        compiler_params=pltpu.CompilerParams(vmem_limit_bytes=48 * 2**20),
        name="project_states",
    )(place, *content, *query, prompt_all, weights)


def normalise(x):
    center = x - jnp.mean(x, axis=1, keepdims=True)
    inverse = lax.rsqrt(jnp.mean(center * center, axis=1, keepdims=True) + epsilon)
    return center * inverse, inverse


def norm_backward(grad, unit, inverse, gain):
    scaled = grad * gain
    mean = jnp.mean(scaled, axis=1, keepdims=True)
    along = jnp.mean(scaled * unit, axis=1, keepdims=True)
    return (scaled - mean - unit * along) * inverse


def layer_kernel(
    place_ref, a_ref, content_ref, query_ref, up_content_ref, up_query_ref, vector_ref, inner_ref,
    output_hbm, hidden_hbm, return_hbm,
    out_content_ref, out_query_ref, keep_ref, send_ref, residual_ref, ag_ref, sum_ref,
    inner_sum_ref,
    output_w, hidden_w, return_w, flat, inner_in, active_ref, returned_ref, zgrad_ref, branch_ref,
    slope, acc, unit, sem,
):
    members, heads, tokens, _ = a_ref.shape
    pairs = keep_ref.shape[0]
    rows_w = keep_ref.shape[1] // 9
    copies = [
        pltpu.make_async_copy(output_hbm, output_w, sem.at[0]),
        pltpu.make_async_copy(hidden_hbm, hidden_w, sem.at[1]),
        pltpu.make_async_copy(return_hbm, return_w, sem.at[2]),
    ]
    for copy in copies:
        copy.start()
    for g in range(members):
        for h in range(heads):
            spot = (g * heads + h) * HEAD_DIM
            for s in range(2):
                flat[s * tokens : (s + 1) * tokens, spot : spot + HEAD_DIM] = a_ref[
                    g, h, :, s * HEAD_DIM : (s + 1) * HEAD_DIM
                ]
    gain, shift, outer, final_gain, final_shift = (vector_ref[i : i + 1, :] for i in range(5))
    copies[0].wait()
    inverses = []
    for s, source in enumerate((content_ref, query_ref)):
        at = slice(s * tokens, (s + 1) * tokens)
        mixed = mm(flat[at, :], output_w[...])
        normal, inverse = normalise(source[...].astype(jnp.float32) + mixed)
        inverses.append(inverse)
        unit[at, :] = normal
        middle = normal * gain + shift
        inner_in[at, :] = middle.astype(jnp.bfloat16)
        acc[at, :] = middle + outer
    copies[1].wait()
    copies[2].wait()
    step = 1024
    chunks = hidden_w.shape[1] // step
    root = 0.7978845608028654

    def forward(i, carry):
        at = pl.ds(pl.multiple_of(i * step, step), step)
        for s in range(2):
            part = slice(s * tokens, (s + 1) * tokens)
            z = mm(inner_in[part, :], hidden_w[:, at]) + inner_ref[:, at]
            square = z * z
            curve = jnp.tanh(root * (z + 0.044715 * (z * square)))
            half = 0.5 + 0.5 * curve
            active = (z * half).astype(jnp.bfloat16)
            slope[part, at] = half + (0.5 * root) * z * (1.0 - curve * curve) * (
                1.0 + (3 * 0.044715) * square
            )
            active_ref[part, at] = active
            acc[part, :] += mm(active, return_w[at, :])
        return carry

    lax.fori_loop(0, chunks, forward, 0, unroll=True)
    sums = []
    for s, (upstream, result) in enumerate(
        ((up_content_ref, out_content_ref), (up_query_ref, out_query_ref))
    ):
        at = slice(s * tokens, (s + 1) * tokens)
        normal, inverse = normalise(acc[at, :])
        result[...] = (normal * final_gain + final_shift).astype(jnp.bfloat16)
        grad = upstream[...].astype(jnp.float32)
        back = norm_backward(grad, normal, inverse, final_gain)
        low = back.astype(jnp.bfloat16)
        returned_ref[at, :] = low
        acc[at, :] = back
        sums.append(
            [
                jnp.sum(low.astype(jnp.float32), axis=0, keepdims=True),
                jnp.sum(grad * normal, axis=0, keepdims=True),
                jnp.sum(grad, axis=0, keepdims=True),
            ]
        )
    for i in range(3):
        sum_ref[2 + i : 3 + i, :] = sums[0][i] + sums[1][i]

    def backward(i, carry):
        at = pl.ds(pl.multiple_of(i * step, step), step)
        total = jnp.zeros((1, step), jnp.float32)
        for s in range(2):
            part = slice(s * tokens, (s + 1) * tokens)
            grad = mm(returned_ref[part, :], return_w[at, :], NT) * slope[part, at]
            low = grad.astype(jnp.bfloat16)
            zgrad_ref[part, at] = low
            total += jnp.sum(low.astype(jnp.float32), axis=0, keepdims=True)
            acc[part, :] += mm(low, hidden_w[:, at], NT)
        inner_sum_ref[:, at] = total
        return carry

    lax.fori_loop(0, chunks, backward, 0, unroll=True)
    sums = []
    for s in range(2):
        at = slice(s * tokens, (s + 1) * tokens)
        grad = acc[at, :]
        normal = unit[at, :]
        back = norm_backward(grad, normal, inverses[s], gain)
        residual_ref[at, :] = back
        low = back.astype(jnp.bfloat16)
        branch_ref[at, :] = low
        sums.append(
            [
                jnp.sum(grad * normal, axis=0, keepdims=True),
                jnp.sum(grad, axis=0, keepdims=True),
            ]
        )
        mixed = mm(low, output_w[...], NT).astype(jnp.bfloat16)
        for g in range(members):
            for h in range(heads):
                spot = (g * heads + h) * HEAD_DIM
                ag_ref[g, h, :, s * HEAD_DIM : (s + 1) * HEAD_DIM] = mixed[
                    :, spot : spot + HEAD_DIM
                ]
    for i in range(2):
        sum_ref[i : i + 1, :] = sums[0][i] + sums[1][i]

    own = place_ref[0] & 1

    def store(pair, block, even, odd):
        at = slice(block * rows_w, (block + 1) * rows_w)
        keep_ref[pair, at, :] = jnp.where(own == 0, even, odd).astype(jnp.bfloat16)
        send_ref[pair, at, :] = jnp.where(own == 0, odd, even).astype(jnp.bfloat16)

    def store_rows(block, value):
        for pair in range(pairs):
            at = 2 * pair * rows_w
            store(pair, block, value[at : at + rows_w], value[at + rows_w : at + 2 * rows_w])

    wide = 2 * D
    for j in range(hidden_w.shape[1] // wide):
        value = mm(inner_in[...], zgrad_ref[:, j * wide : (j + 1) * wide], TN)
        for i in range(2):
            store_rows((0, 1, 2, 6)[2 * j + i], value[:, i * D : (i + 1) * D])
    rows = 4 * rows_w
    for pair in range(pairs):
        even, odd = (
            mm(active_ref[:, w * rows : (w + 1) * rows], returned_ref[...], TN)
            for w in (2 * pair, 2 * pair + 1)
        )
        for i in range(4):
            at = slice(i * rows_w, (i + 1) * rows_w)
            store(pair, (3, 4, 5, 7)[i], even[at], odd[at])
    store_rows(8, mm(flat[...], branch_ref[...], TN))


def layer(place, shards, a, *operands):
    content, hidden_w = operands[0], operands[-2]
    tokens = content.shape[0]
    rows = 2 * tokens
    hidden = hidden_w.shape[1]
    vmem = pl.BlockSpec(memory_space=pltpu.VMEM)
    low = partial(jax.ShapeDtypeStruct, dtype=jnp.bfloat16)
    wide = partial(jax.ShapeDtypeStruct, dtype=jnp.float32)
    grads = low((shards // 2, 9 * D // shards, D))
    return pl.pallas_call(
        layer_kernel,
        in_specs=[pl.BlockSpec(memory_space=pltpu.SMEM)]
        + [vmem] * 7
        + [pl.BlockSpec(memory_space=pl.ANY)] * 3,
        out_specs=[vmem] * 8,
        out_shape=[
            low((tokens, D)),
            low((tokens, D)),
            grads,
            grads,
            wide((rows, D)),
            low(a.shape),
            wide((5, D)),
            wide((1, hidden)),
        ],
        scratch_shapes=[
            pltpu.VMEM((D, D), jnp.bfloat16),
            pltpu.VMEM((D, hidden), jnp.bfloat16),
            pltpu.VMEM((hidden, D), jnp.bfloat16),
            pltpu.VMEM((rows, D), jnp.bfloat16),
            pltpu.VMEM((rows, D), jnp.bfloat16),
            pltpu.VMEM((rows, hidden), jnp.bfloat16),
            pltpu.VMEM((rows, D), jnp.bfloat16),
            pltpu.VMEM((rows, hidden), jnp.bfloat16),
            pltpu.VMEM((rows, D), jnp.bfloat16),
            pltpu.VMEM((rows, hidden), jnp.float32),
            pltpu.VMEM((rows, D), jnp.float32),
            pltpu.VMEM((rows, D), jnp.float32),
            pltpu.SemaphoreType.DMA((3,)),
        ],
        compiler_params=pltpu.CompilerParams(vmem_limit_bytes=60 * 2**20),
        cost_estimate=pl.CostEstimate(
            flops=12 * rows * D * hidden, bytes_accessed=24 * 2**20, transcendentals=rows * hidden
        ),
        name="layer",
    )(place, a, *operands)


def part_kernel(
    place_ref, own_ref, other_ref, keep_y, send_y, keep_x, send_x, keep_z, send_z
):
    step = pl.program_id(0)
    count = own_ref.shape[1] // 3
    chains = [
        (
            own_ref[0, i * count : (i + 1) * count, :].astype(jnp.float32)
            + other_ref[0, i * count : (i + 1) * count, :].astype(jnp.float32)
        )
        for i in range(3)
    ]
    half = count // 2
    own_y, own_x, own_z = place_ref[0], place_ref[1], place_ref[2]

    @pl.when(step == own_y)
    def _():
        keep_y[0] = chains[0].astype(jnp.bfloat16)

    @pl.when(step != own_y)
    def _():
        send_y[0] = chains[0].astype(jnp.bfloat16)

    for chain, own, keep, send in (
        (chains[1], own_x, keep_x, send_x),
        (chains[2], own_z, keep_z, send_z),
    ):
        keep[0] = jnp.where(own == 0, chain[:half], chain[half:]).astype(jnp.bfloat16)
        send[0] = jnp.where(own == 0, chain[half:], chain[:half]).astype(jnp.bfloat16)


def part(place, own, other):
    pairs, rows, _ = own.shape
    count = rows // 3
    low = partial(jax.ShapeDtypeStruct, dtype=jnp.bfloat16)
    both = pl.BlockSpec((1, rows, D), lambda i, c: (i, 0, 0))
    return pl.pallas_call(
        part_kernel,
        grid_spec=pltpu.PrefetchScalarGridSpec(
            num_scalar_prefetch=1,
            grid=(pairs,),
            in_specs=[both, both],
            out_specs=[pl.BlockSpec((1, count, D), lambda i, c: (0, 0, 0))] * 2
            + [pl.BlockSpec((1, count // 2, D), lambda i, c: (i, 0, 0))] * 4,
        ),
        out_shape=[low((1, count, D))] * 2 + [low((pairs, count // 2, D))] * 4,
        compiler_params=pltpu.CompilerParams(vmem_limit_bytes=56 * 2**20),
        cost_estimate=pl.CostEstimate(
            flops=pairs * rows * D, bytes_accessed=6 * pairs * rows * D, transcendentals=0
        ),
        name="part",
    )(place, own, other)


def unpack_tokens_kernel(members, head_count, place_ref, *refs):
    pieces, (hidden_ref, return_ref, output_ref, held) = refs[: 2 * members], refs[2 * members :]
    rows_w = hidden_ref.shape[0]
    chains, per, _ = held.shape[1:]
    for m in range(members):
        held[m, : chains - 1] = pieces[m][...]
        held[m, chains - 1 :] = pieces[members + m][...]
    member = place_ref[1]
    for g in range(members):
        head, half = g % head_count, g // head_count
        for c in range(chains):
            if c == 2:
                spot = (half * head_count + head) * per
            else:
                spot = (head * (members // head_count) + half) * per
            row = c * members * per + spot
            done = 0
            while done < per:
                block, at = divmod(row + done, rows_w)
                count = min(per - done, rows_w - at)
                value = held[member ^ g, c, done : done + count, :].astype(jnp.float32)
                if block == 8:
                    output_ref[at : at + count, :] = value
                elif block in (0, 1, 2, 6):
                    j = min(block, 3)
                    hidden_ref[at : at + count, j * D : (j + 1) * D] = value
                else:
                    j = min(block - 3, 3)
                    return_ref[j * rows_w + at : j * rows_w + at + count, :] = value
                done += count


def unpack_tokens(place, rows_w, head_count, early, late):
    members = len(early)
    vmem = pl.BlockSpec(memory_space=pltpu.VMEM)
    chains = early[0].shape[0] + late[0].shape[0]
    return pl.pallas_call(
        partial(unpack_tokens_kernel, members, head_count),
        in_specs=[pl.BlockSpec(memory_space=pltpu.SMEM)] + [vmem] * 2 * members,
        out_specs=[vmem] * 3,
        out_shape=[
            jax.ShapeDtypeStruct((rows_w, 4 * D), jnp.float32),
            jax.ShapeDtypeStruct((4 * rows_w, D), jnp.float32),
            jax.ShapeDtypeStruct((rows_w, D), jnp.float32),
        ],
        scratch_shapes=[pltpu.VMEM((members, chains) + early[0].shape[1:], jnp.bfloat16)],
        compiler_params=pltpu.CompilerParams(vmem_limit_bytes=48 * 2**20),
        name="unpack_tokens",
    )(place, *early, *late)


def head_grads_kernel(shards, heads, place_ref, states_ref, position_ref, *rest):
    dq, dkv, dt = (rest[i * heads : (i + 1) * heads] for i in range(3))
    small, out_ref = rest[3 * heads : -1], rest[-1]
    keys = dkv[0].shape[0]
    prompt = keys - LEN
    rows_w = D // shards
    wide = 2 * HEAD_DIM
    side = partial(jnp.concatenate, axis=1)
    dq = side([ref[...].reshape(LEN, wide) for ref in dq])
    key_value = mm(side([ref[...] for ref in dkv]), states_ref[:keys, :], TN)
    content = mm(dq, states_ref[prompt:keys, :], TN)
    query = mm(dq, states_ref[keys:, :], TN)
    table = mm(side([ref[...] for ref in dt]), position_ref[...], TN)
    parts = []
    for h in range(heads):
        at = h * wide
        parts += [
            content[at : at + HEAD_DIM] + query[at + HEAD_DIM : at + wide],
            key_value[at : at + wide],
            table[h * HEAD_DIM : (h + 1) * HEAD_DIM],
        ]
    turned = jnp.concatenate(parts, axis=0).T.astype(jnp.bfloat16)
    for w in range(shards):
        out_ref[w, :rows_w, :] = turned[w * rows_w : (w + 1) * rows_w, :]
    if small:
        token_ref, inner_ref, sums = small[0], small[1], small[2:]
        member = place_ref[1]
        out_ref[:, rows_w:, :] = jnp.zeros_like(out_ref[:, rows_w:, :])
        own_sums = side([ref[0:5, :] for ref in sums])
        for w in range(shards):
            own = jnp.where(member == w, own_sums, 0.0)
            parts = [token_ref[0:5, w * rows_w : (w + 1) * rows_w], own]
            parts += [
                inner_ref[0:1, (4 * w + j) * rows_w : (4 * w + j + 1) * rows_w] for j in range(4)
            ]
            parts.append(jnp.zeros((2, rows_w), jnp.float32))
            out_ref[w, rows_w : rows_w + 16, :rows_w] = jnp.concatenate(parts, axis=0).astype(
                jnp.bfloat16
            )


def head_grads(place, shards, states, positions, dq, dkv, dt, small=()):
    vmem = pl.BlockSpec(memory_space=pltpu.VMEM)
    heads = len(dq)
    operands = (states, positions) + tuple(dq) + tuple(dkv) + tuple(dt) + tuple(small)
    rows = D // shards + (16 if small else 0)
    return pl.pallas_call(
        partial(head_grads_kernel, shards, heads),
        in_specs=[pl.BlockSpec(memory_space=pltpu.SMEM)] + [vmem] * len(operands),
        out_specs=vmem,
        out_shape=jax.ShapeDtypeStruct((shards, rows, 4 * HEAD_DIM * heads), jnp.bfloat16),
        compiler_params=pltpu.CompilerParams(vmem_limit_bytes=56 * 2**20),
        cost_estimate=pl.CostEstimate(
            flops=2 * 6656 * D * 256, bytes_accessed=12 * 2**20, transcendentals=0
        ),
        name="head_grads",
    )(place, *operands)


def unpack_kernel(members, groups, place_ref, *refs):
    pieces = [refs[i * members : (i + 1) * members] for i in range(groups)]
    outs = refs[groups * members : groups * members + 4]
    small_ref = refs[groups * members + 4]
    held = refs[groups * members + 5 : groups * members + 5 + groups]
    rows_w = outs[0].shape[0]
    for i in range(groups):
        for m in range(members):
            held[i][m] = pieces[i][m][...]
    member = place_ref[1]
    for g in range(members):
        head = 0
        for i in range(groups):
            block = held[i][member ^ g].astype(jnp.float32)
            for j in range(block.shape[1] // (4 * HEAD_DIM)):
                spot = (g * groups_heads(held) + head) * HEAD_DIM
                for kind in range(4):
                    at = (4 * j + kind) * HEAD_DIM
                    outs[kind][:, spot : spot + HEAD_DIM] = block[:rows_w, at : at + HEAD_DIM]
                head += 1
    last = held[-1]
    total = last[0, rows_w : rows_w + 16, :].astype(jnp.float32)
    for m in range(1, members):
        total += last[m, rows_w : rows_w + 16, :].astype(jnp.float32)
    small_ref[...] = total


def groups_heads(held):
    return sum(ref.shape[2] // (4 * HEAD_DIM) for ref in held)


def unpack(place, rows_w, *pieces):
    members = len(pieces[0])
    vmem = pl.BlockSpec(memory_space=pltpu.VMEM)
    flat = [x for group in pieces for x in group]
    return pl.pallas_call(
        partial(unpack_kernel, members, len(pieces)),
        in_specs=[pl.BlockSpec(memory_space=pltpu.SMEM)] + [vmem] * len(flat),
        out_specs=[vmem] * 5,
        out_shape=[jax.ShapeDtypeStruct((rows_w, D), jnp.float32)] * 4
        + [jax.ShapeDtypeStruct((16, 4 * HEAD_DIM), jnp.float32)],
        scratch_shapes=[pltpu.VMEM((members,) + group[0].shape, jnp.bfloat16) for group in pieces],
        compiler_params=pltpu.CompilerParams(vmem_limit_bytes=48 * 2**20),
        name="unpack",
    )(place, *flat)


def finish_kernel(
    early_ref, late_ref, prompt_ref, residual_ref, weight_hbm,
    content_ref, query_ref, out_prompt_ref, weight, parts, prompts, sem,
):
    copy = pltpu.make_async_copy(weight_hbm, weight, sem)
    copy.start()
    members, before, _, _ = early_ref.shape
    tokens = content_ref.shape[0]
    heads = before + late_ref.shape[1]
    for g in range(members):
        for h in range(heads):
            spot = (g * heads + h) * HEAD_DIM
            source, i = (early_ref, h) if h < before else (late_ref, h - before)
            for kind in range(4):
                at = (kind % 2) * HEAD_DIM
                start = (kind // 2) * tokens
                parts[kind, :, spot : spot + HEAD_DIM] = source[
                    g, i, start : start + tokens, at : at + HEAD_DIM
                ]
            for kind in range(2):
                prompts[kind, :, spot : spot + HEAD_DIM] = prompt_ref[
                    g, h, :, kind * HEAD_DIM : (kind + 1) * HEAD_DIM
                ]
    copy.wait()
    query, key, value = (weight[:, i * D : (i + 1) * D] for i in range(3))
    content = residual_ref[:tokens, :] + mm(parts[0], query, NT)
    content += mm(parts[2], key, NT)
    content += mm(parts[3], value, NT)
    content_ref[...] = content.astype(jnp.bfloat16)
    query_ref[...] = (residual_ref[tokens:, :] + mm(parts[1], query, NT)).astype(jnp.bfloat16)
    out_prompt_ref[...] = (mm(prompts[0], key, NT) + mm(prompts[1], value, NT)).astype(
        jnp.bfloat16
    )


def finish(rows_early, rows_late, prompt_back, residual, weights):
    tokens = residual.shape[0] // 2
    prompt = prompt_back.shape[2]
    vmem = pl.BlockSpec(memory_space=pltpu.VMEM)
    return pl.pallas_call(
        finish_kernel,
        in_specs=[vmem] * 4 + [pl.BlockSpec(memory_space=pl.ANY)],
        out_specs=[vmem] * 3,
        out_shape=[
            jax.ShapeDtypeStruct((tokens, D), jnp.bfloat16),
            jax.ShapeDtypeStruct((tokens, D), jnp.bfloat16),
            jax.ShapeDtypeStruct((prompt, D), jnp.bfloat16),
        ],
        scratch_shapes=[
            pltpu.VMEM(weights.shape, jnp.bfloat16),
            pltpu.VMEM((4, tokens, D), jnp.bfloat16),
            pltpu.VMEM((2, prompt, D), jnp.bfloat16),
            pltpu.SemaphoreType.DMA,
        ],
        compiler_params=pltpu.CompilerParams(vmem_limit_bytes=48 * 2**20),
        cost_estimate=pl.CostEstimate(
            flops=8 * tokens * D * D, bytes_accessed=8 * 2**20, transcendentals=0
        ),
        name="finish",
    )(rows_early, rows_late, prompt_back, residual, weights)


def axes_size(axes):
    size = 1
    for name in axes:
        size *= lax.axis_size(name)
    return size


def flat_index(axes):
    index = 0
    for name in axes:
        index = index * lax.axis_size(name) + lax.axis_index(name)
    return index


def swap(x, axes, mask):
    return lax.ppermute(x, axes, [(i, i ^ mask) for i in range(axes_size(axes))])


def bits_of(axes):
    return range(axes_size(axes).bit_length() - 1)


def pieces_of(x, axes):
    pieces = {0: x}
    for bit in reversed(bits_of(axes)):
        for mask in list(pieces):
            pieces[mask | 1 << bit] = swap(pieces[mask], axes, 1 << bit)
    return [pieces[m] for m in range(axes_size(axes))]


def in_order(pieces, index):
    count = len(pieces)
    result = jnp.zeros((count,) + pieces[0].shape, pieces[0].dtype)
    for m, piece in enumerate(pieces):
        result = lax.dynamic_update_slice(result, piece[None], (index ^ m,) + (0,) * piece.ndim)
    return result


def pick(x, index, axis=0):
    return lax.dynamic_index_in_dim(x, index, axis, keepdims=False)


def add_low(x, y):
    return (x.astype(jnp.float32) + y.astype(jnp.float32)).astype(jnp.bfloat16)


def half_sum(x, axes, bit, axis):
    own = flat_index(axes) >> bit & 1
    return add_low(pick(x, own, axis), swap(pick(x, 1 - own, axis), axes, 1 << bit))


def split_axis(x, axis):
    return x.reshape(x.shape[:axis] + (2, x.shape[axis] // 2) + x.shape[axis + 1 :])


def stages_of(names):
    return [((name,), bit) for name in names for bit in bits_of((name,))]


def full_sum(x, stages):
    for axes, bit in stages:
        x = add_low(x, swap(x, axes, 1 << bit))
    return x


def group_pieces(x, axes):
    return [x] + [swap(x, axes, m) for m in range(1, axes_size(axes))]


def back_through(grad_rows, weight):
    return jnp.einsum("rc,dc->rd", grad_rows, weight, preferred_element_type=jnp.float32)


def outer_sum(rows_in, grad_rows):
    return jnp.einsum("rd,rc->dc", rows_in, grad_rows, preferred_element_type=jnp.float32)


def sinusoid_rows(first, rows):
    frequency = jnp.asarray(
        np.power(10000.0, -2.0 * np.arange(D // 2) / D).astype(np.float32)
    )
    fine = jnp.arange(64, dtype=jnp.float32)[:, None] * frequency
    coarse = (first - 64 * jnp.arange(rows // 64, dtype=jnp.int32)).astype(jnp.float32)
    coarse = coarse[:, None] * frequency
    fs, fc = jnp.sin(fine)[None], jnp.cos(fine)[None]
    cs, cc = jnp.sin(coarse)[:, None], jnp.cos(coarse)[:, None]
    both = jnp.concatenate([cs * fc - cc * fs, cc * fc + cs * fs], axis=-1)
    return both.reshape(rows, D).astype(jnp.bfloat16)


GROUP = ("half", "head")
JOB = ("cont", "half", "head")
SHARD = ("wshard",)


def per_device(
    prompt_states, content_states, query_states, visible_length, start_offsets,
    prompt_segments, token_segments, order_ranks,
    query_weights, key_weights, value_weights, output_weights, relative_weights,
    content_bias, position_bias, segment_bias, segment_vectors,
    attention_gain, attention_shift, hidden_weights, hidden_bias, return_weights, return_bias,
    final_gain, final_shift, content_upstream, query_upstream,
):
    members = axes_size(GROUP)
    member = flat_index(GROUP)
    shards = lax.axis_size("wshard")
    shard = lax.axis_index("wshard")
    chapters = lax.axis_size("cont")
    chapter = lax.axis_index("cont")
    width = D // members
    local_heads = HEADS // members
    content_rows = content_states[0]
    query_rows = query_states[0]
    tokens = content_rows.shape[0]
    prompt_part = prompt_states.shape[1]
    prompt_total = prompt_segments.shape[1]
    keys = prompt_total + LEN
    rows_w = query_weights.shape[0]

    def columns(x):
        return lax.dynamic_slice_in_dim(x, member * width, width, x.ndim - 1)

    tie = lax.optimization_barrier

    content = {0: content_rows}
    query = {0: query_rows}
    content[1], query[2] = swap(content_rows, GROUP, 1), swap(query_rows, GROUP, 2)
    first_weights = jnp.stack(
        [columns(w) for w in (query_weights, key_weights, value_weights, relative_weights)], axis=0
    )
    small = jnp.concatenate(
        [
            jnp.stack([content_bias, position_bias, segment_bias]),
            segment_vectors,
            jnp.stack([attention_gain, attention_shift, return_bias, final_gain, final_shift]),
            hidden_bias.reshape(-1, rows_w),
            jnp.zeros((2, rows_w), jnp.bfloat16),
        ],
        axis=0,
    )
    first_pieces = pieces_of(first_weights, SHARD)
    small_pieces = pieces_of(small, SHARD)
    query[1], content[2] = swap(query_rows, GROUP, 1), swap(content_rows, GROUP, 2)
    content[3], query[3] = swap(content[1], GROUP, 2), swap(query[2], GROUP, 1)
    prompt_all = lax.all_to_all(
        jnp.broadcast_to(prompt_states, (chapters * members,) + prompt_states.shape[1:]),
        JOB,
        0,
        0,
        tiled=True,
    ).reshape(prompt_total, D)
    output_full = lax.all_gather(output_weights, "wshard", axis=0, tiled=True)
    hidden_full = lax.all_gather(hidden_weights, "wshard", axis=0, tiled=True)
    return_full = lax.all_gather(return_weights, "wshard", axis=0, tiled=True)
    attention_weights = jnp.concatenate([query_weights, key_weights, value_weights], axis=1)
    attention_full = lax.all_gather(attention_weights, "wshard", axis=0, tiled=True)

    seen = pick(visible_length[0], chapter)
    base = seen + pick(start_offsets[0], chapter)
    segments = lax.dynamic_slice_in_dim(token_segments[0], chapter * LEN, LEN)
    ranks = lax.dynamic_slice_in_dim(order_ranks[0], chapter * LEN, LEN)
    reversed_segments = jnp.flip(segments.reshape(-1, TQ), 1).reshape(-1)
    qinfo = jnp.stack([segments, ranks, reversed_segments, segments], axis=1)
    key_segments = jnp.concatenate([prompt_segments[0], segments])
    hidden_keys = (jnp.arange(keys, dtype=jnp.int32) < prompt_total) & (
        jnp.arange(keys, dtype=jnp.int32) >= seen
    )
    kinfo = jnp.stack([key_segments, hidden_keys.astype(jnp.int32)], axis=1)
    place = jnp.stack([shard, member])

    frequency = jnp.asarray(np.power(10000.0, -2.0 * np.arange(D // 2) / D).astype(np.float32))
    starts = jnp.concatenate(
        [
            base + LEN - 1 - 64 * jnp.arange((LEN + prompt_total) // 64, dtype=jnp.int32),
            LEN - 1 - 64 * jnp.arange(2 * LEN // 64, dtype=jnp.int32),
        ]
    )
    coarse = starts.astype(jnp.float32)[:, None] * frequency
    coarse = jnp.stack([jnp.sin(coarse), jnp.cos(coarse)])
    fine = jnp.arange(64, dtype=jnp.float32)[:, None] * frequency
    fine = jnp.stack([jnp.sin(fine), jnp.cos(fine)])

    first_full, rt, positions, vectors, inner_full, head_bias = project_table(
        place, first_pieces, small_pieces, coarse, fine
    )
    q, k, v, states = project_states(
        place,
        [content[m] for m in range(members)],
        [query[m] for m in range(members)],
        prompt_all,
        first_full,
    )
    p, a, mixture, kaug, vaug, table_rows = attend_forward(
        q, k, v, rt, head_bias, qinfo, kinfo, ranks[None], tokens
    )
    mixture = lax.all_to_all(mixture, GROUP, 0, 0, tiled=True)

    (
        out_content, out_query, kept_grads, sent_grads, residual_grad, grad_out, token_sums,
        inner_bias_grad,
    ) = layer(
        place, shards, mixture, content_rows, query_rows, content_upstream[0], query_upstream[0],
        vectors, inner_full, output_full, hidden_full, return_full,
    )
    grad_out, attention_full = lax.optimization_barrier((grad_out, attention_full))
    grad_out = lax.all_to_all(grad_out, GROUP, 0, 0, tiled=True)

    bits = jnp.stack([shard >> 1, lax.axis_index("head"), lax.axis_index("half")])
    parts = part(bits, kept_grads, swap(sent_grads, SHARD, 1))
    stage_y, stage_x, stage_z = (SHARD, 1), (("head",), 0), (("half",), 0)
    cont_stage = stages_of(("cont",))
    orders = (
        (stage_y, stage_x, stage_z),
        (stage_x, stage_z, stage_y),
        (stage_z, stage_y, stage_x),
    )
    chains = [
        (kept, swap(out, order[0][0], 1 << order[0][1]))
        for kept, out, order in zip(parts[::2], parts[1::2], orders)
    ]

    def next_stage(chain, stage):
        axes, bit = stage
        x = add_low(*chain)
        axis = 0 if axes == SHARD else 1
        x = split_axis(x, axis)
        own = flat_index(axes) >> bit & 1
        return pick(x, own, axis), swap(pick(x, 1 - own, axis), axes, 1 << bit)

    small_grads = (token_sums, inner_bias_grad)

    def attend_back(h, grad_out):
        return attend_backward(h, q, head_bias, qinfo, kaug, vaug, table_rows, p, a, grad_out)

    last = local_heads - 1
    grad_out, parts = tie((grad_out, parts))
    backward = [attend_back(0, grad_out)]
    grad_out, chains = tie((grad_out, chains))
    chains = [next_stage(x, order[1]) for x, order in zip(chains, orders)]
    backward += [attend_back(h, grad_out) for h in range(1, last)]
    backward, chains = tie((backward, chains))
    chains = [next_stage(x, order[2]) for x, order in zip(chains, orders)]
    dq, dkv, dt, _ = zip(*backward)
    x = head_grads(place, shards, states, positions, dq, dkv, dt)
    x, chains, dq, dkv = tie((x, chains, dq, dkv))
    chains = [add_low(*x) for x in chains]

    def shard_stage(x, bit):
        return half_sum(x.reshape((-1, 2) + x.shape[1:]), SHARD, bit, 1)

    def row_parts(heads):
        parts = []
        for h in heads:
            prompts = dkv[h][:prompt_total].reshape(chapters, members, prompt_part, -1)
            prompts = jnp.transpose(prompts, (1, 0, 2, 3)).reshape(members, -1, dq[h].shape[2])
            own = dkv[h][prompt_total:].reshape(dq[h].shape)
            parts.append(jnp.concatenate([dq[h], own, prompts], axis=1))
        return lax.all_to_all(jnp.stack(parts, axis=1), GROUP, 0, 0, tiled=True)

    first = shard_stage(x, 0)
    grad_out, chains, first = tie((grad_out, chains, first))
    early = full_sum(jnp.concatenate(chains[:2]), cont_stage)
    first = shard_stage(first, 1)
    rows_early = row_parts(range(last))
    backward.append(attend_back(last, grad_out))
    backward[last], late, first, early, rows_early = tie(
        (backward[last], chains[2], first, early, rows_early)
    )
    late = full_sum(late, cont_stage)
    first = full_sum(first[0], cont_stage)
    early_x = swap(early, GROUP, 1)
    early_dq, early_dkv = dq, dkv
    dq, dkv, dt, sums = zip(*backward)
    dq, dkv = early_dq + dq[last:], early_dkv + dkv[last:]
    rows_late = row_parts([last])
    x = head_grads(
        place, shards, states, positions, dq[-1:], dkv[-1:], dt[-1:], small_grads + sums
    )
    x, late, rows_late, first, early_x, early = tie((x, late, rows_late, first, early_x, early))
    early_pieces = [early, early_x] + [swap(early, GROUP, m) for m in range(2, members)]
    late_pieces = group_pieces(late, GROUP)
    prompt_back = jnp.concatenate([rows_early[:, :, 2 * tokens :], rows_late[:, :, 2 * tokens :]], 1)
    prompt_back = prompt_back.reshape(prompt_back.shape[:2] + (chapters, prompt_part, -1))
    prompt_back = jnp.transpose(prompt_back, (2, 0, 1, 3, 4))
    second = shard_stage(shard_stage(x, 0), 1)[0]
    first = group_pieces(first, GROUP)
    for axes, bit in reversed(cont_stage):
        halves = split_axis(prompt_back, 0)
        own = flat_index(axes) >> bit & 1
        sent = pick(halves, 1 - own).reshape(2, -1, prompt_back.shape[-1])
        sent = jnp.concatenate([second, jnp.concatenate([sent[0], sent[1]], axis=1)])
        sent = swap(sent, axes, 1 << bit)
        rows = second.shape[0]
        second = add_low(second, sent[:rows])
        half = sent.shape[1] // 2
        other = jnp.stack([sent[rows:, :half], sent[rows:, half:]])
        prompt_back = add_low(pick(halves, own), other.reshape(halves.shape[1:]))
    second, early_pieces, late_pieces[:3] = tie((second, early_pieces, late_pieces[:3]))
    head_pieces = [first, group_pieces(second, GROUP)]

    hidden_total, return_total, output_total = unpack_tokens(
        place, rows_w, lax.axis_size("head"), early_pieces, late_pieces
    )
    query_grad, key_grad, value_grad, relative_grad, small_total = unpack(
        place, rows_w, *head_pieces
    )
    vector_total = small_total[:10, :rows_w]
    inner_total = small_total[10:14, :rows_w].reshape(-1)
    content_grad, queries_grad, prompt_grad = finish(
        rows_early, rows_late, prompt_back[0], residual_grad, attention_full
    )
    return (
        out_content[None],
        out_query[None],
        prompt_grad[None],
        content_grad[None],
        queries_grad[None],
        query_grad,
        key_grad,
        value_grad,
        output_total,
        relative_grad,
        vector_total[5],
        vector_total[6],
        vector_total[7],
        vector_total[8:10],
        vector_total[0],
        vector_total[1],
        hidden_total,
        inner_total,
        return_total,
        vector_total[2],
        vector_total[3],
        vector_total[4],
    )


def solution(mesh):
    rows = P("wshard", JOB, None)
    job = P("wshard", None)
    matrix = P("wshard", None)
    vector = P("wshard")
    pair = P(None, "wshard")
    in_specs = (
        (rows,) * 3 + (job,) * 5 + (matrix,) * 5 + (vector,) * 3 + (pair,)
        + (vector, vector, matrix, vector, matrix, vector, vector, vector, rows, rows)
    )
    out_specs = (
        (rows,) * 5 + (matrix,) * 5 + (vector,) * 3 + (pair,)
        + (vector, vector, matrix, vector, matrix, vector, vector, vector)
    )

    def run(*arguments):
        seq_count, head_count, shard_count = mesh.devices.shape
        tokens = arguments[1].shape[1] // (seq_count * head_count)
        halves = LEN // (tokens * head_count)
        split = Mesh(
            mesh.devices.reshape(seq_count // halves, halves, head_count, shard_count),
            ("cont", "half", "head", "wshard"),
        )
        return jax.shard_map(
            per_device, mesh=split, in_specs=in_specs, out_specs=out_specs, check_vma=False
        )(*arguments)

    return run
```

```python
from functools import partial

import jax
import jax.numpy as jnp
import numpy as np
from jax import lax
from jax.experimental import pallas as pl
from jax.experimental.pallas import tpu as pltpu
from jax.sharding import Mesh, PartitionSpec as P

D = 768
HEADS = 12
HEAD_DIM = 64
LEN = 1024
SEGMENTS = 4
TQ = 128

negative = -1e30
epsilon = 1e-06
scale_factor = HEAD_DIM ** (-0.5)
NT = (((1,), (1,)), ((), ()))
NN = (((1,), (0,)), ((), ()))
TN = (((0,), (0,)), ((), ()))

COL_HIGH = HEAD_DIM
COL_LOW = HEAD_DIM + SEGMENTS
COL_ONE = HEAD_DIM + 2 * SEGMENTS
COL_ONE_LOW = COL_ONE + 1
COL_MASK = COL_ONE + 2


def mm(a, b, dims=NN):
    return lax.dot_general(a, b, dims, preferred_element_type=jnp.float32)


def reverse_rows(x):
    groups = x.shape[0] // 8
    index = 7 - lax.broadcasted_iota(jnp.int32, (8, x.shape[1]), 0)
    return jnp.concatenate(
        [
            jnp.take_along_axis(x[8 * (groups - 1 - g) : 8 * (groups - g)], index, axis=0)
            for g in range(groups)
        ],
        axis=0,
    )


def prepare_keys(head, k_ref, v_ref, rt_ref, kinfo_ref, kaug, vaug, rt):
    cols = slice(head * HEAD_DIM, (head + 1) * HEAD_DIM)
    rows = k_ref.shape[0]
    lane = lax.broadcasted_iota(jnp.int32, (rows, HEAD_DIM), 1)
    segment = kinfo_ref[:, 0:1]
    hidden = kinfo_ref[:, 1:2]
    one_hot = ((lane == segment) | (lane - SEGMENTS == segment)) & (lane < 2 * SEGMENTS)
    ones = (lane == COL_ONE - HEAD_DIM) | (lane == COL_ONE_LOW - HEAD_DIM)
    extra = jnp.where(one_hot | ones, 1.0, 0.0)
    extra = jnp.where((lane == COL_MASK - HEAD_DIM) & (hidden > 0), negative, extra)
    kaug[:, :HEAD_DIM] = k_ref[:, cols]
    kaug[:, HEAD_DIM:] = extra.astype(jnp.bfloat16)
    vaug[:, :HEAD_DIM] = v_ref[:, cols]
    vaug[:, HEAD_DIM:] = jnp.where(lane < 2, 1.0, 0.0).astype(jnp.bfloat16)
    rt[...] = rt_ref[:, cols]


def query_terms(head, s, q_ref, bias_ref):
    cols = slice(head * HEAD_DIM, (head + 1) * HEAD_DIM)
    q = q_ref[s, :, cols].astype(jnp.float32)
    content = (q + bias_ref[0:1, cols]).astype(jnp.bfloat16).astype(jnp.float32)
    position = (q + bias_ref[1:2, cols]).astype(jnp.bfloat16).astype(jnp.float32)
    segment = q + bias_ref[2:3, cols]
    return content, position, segment


def forward_kernel(
    q_ref, k_ref, v_ref, rt_ref, bias_ref, qinfo_ref, kinfo_ref, rank_ref,
    p_ref, a_ref, mix_ref, kaug_ref, vaug_ref, table_ref, qaug,
):
    step = pl.program_id(0)
    keys = k_ref.shape[0]
    prompt = keys - LEN
    heads = p_ref.shape[0]

    @pl.when(step == 0)
    def _():
        for head in range(heads):
            prepare_keys(
                head, k_ref, v_ref, rt_ref, kinfo_ref,
                kaug_ref.at[head], vaug_ref.at[head], table_ref.at[head],
            )

    start = pl.multiple_of(LEN - TQ - step * TQ, TQ)
    lane = lax.broadcasted_iota(jnp.int32, (TQ, HEAD_DIM), 1)
    segment_id = qinfo_ref[:, 0:1]
    rank = qinfo_ref[:, 1:2]
    wide = lax.broadcasted_iota(jnp.int32, (TQ, 2 * HEAD_DIM), 1)
    for head, s in [(head, s) for head in range(heads) for s in range(2)]:
        cols = slice(head * HEAD_DIM, (head + 1) * HEAD_DIM)
        table_p = table_ref[head, pl.ds(start, TQ + prompt), :]
        table_c = table_ref[head, pl.ds(pl.multiple_of(LEN + prompt + start, TQ), TQ + LEN), :]
        content, position, with_segment = query_terms(head, s, q_ref, bias_ref)
        same = jnp.sum(with_segment * bias_ref[3:4, cols], axis=1, keepdims=True) * scale_factor
        other = jnp.sum(with_segment * bias_ref[4:5, cols], axis=1, keepdims=True) * scale_factor
        differ = same - other
        differ_high = differ.astype(jnp.bfloat16).astype(jnp.float32)
        other_high = other.astype(jnp.bfloat16).astype(jnp.float32)
        extra = jnp.where(lane == segment_id, differ_high, 0.0)
        extra = jnp.where(lane - SEGMENTS == segment_id, differ - differ_high, extra)
        extra = jnp.where(lane == COL_ONE - HEAD_DIM, other_high, extra)
        extra = jnp.where(lane == COL_ONE_LOW - HEAD_DIM, other - other_high, extra)
        extra = jnp.where(lane == COL_MASK - HEAD_DIM, 1.0, extra)
        qaug[:, :HEAD_DIM] = (content * scale_factor).astype(jnp.bfloat16)
        qaug[:, HEAD_DIM:] = extra.astype(jnp.bfloat16)
        scores = mm(qaug[...], kaug_ref[head], NT)
        position = (position * scale_factor).astype(jnp.bfloat16)
        band_p = mm(position, table_p, NT).astype(jnp.bfloat16)
        band_c = mm(position, table_c, NT).astype(jnp.bfloat16)
        band_p = pltpu.roll(band_p, prompt + 1, axis=1, stride=1, stride_axis=0)
        band_c = pltpu.roll(band_c, LEN + 1, axis=1, stride=1, stride_axis=0)
        scores_p = scores[:, :prompt] + band_p[:, :prompt]
        scores_c = scores[:, prompt:] + band_c[:, :LEN]
        scores_c = jnp.where(rank_ref[0:1, :] <= rank - s, scores_c, negative)
        largest = jnp.maximum(
            jnp.max(scores_p, axis=1, keepdims=True), jnp.max(scores_c, axis=1, keepdims=True)
        )
        weights_p = jnp.exp(scores_p - largest)
        weights_c = jnp.exp(scores_c - largest)
        mixed = mm(weights_p.astype(jnp.bfloat16), vaug_ref[head, :prompt, :])
        mixed += mm(weights_c.astype(jnp.bfloat16), vaug_ref[head, prompt:, :])
        inverse = 1.0 / mixed[:, HEAD_DIM : HEAD_DIM + 1]
        mixed = mixed * inverse
        a_ref[head, s] = jnp.where(wide < HEAD_DIM, mixed, inverse)
        mix_ref[0, head, :, s * HEAD_DIM : (s + 1) * HEAD_DIM] = mixed[:, :HEAD_DIM].astype(
            jnp.bfloat16
        )
        rows = slice(s * TQ, (s + 1) * TQ)
        p_ref[head, 0, rows, :prompt] = reverse_rows(weights_p).astype(jnp.bfloat16)
        p_ref[head, 0, rows, prompt:] = reverse_rows(weights_c).astype(jnp.bfloat16)


def backward_kernel(
    head, q_ref, bias_ref, qinfo_ref, kaug_ref, vaug_ref, table_ref, p_ref, a_ref, ag_ref,
    dq_ref, dkv_ref, dt_ref, sum_ref,
    agaug, cw, cr, g_all, band_p, band_c, dk_acc, dv_acc, dt_acc,
):
    step = pl.program_id(0)
    keys = kaug_ref.shape[1]
    prompt = keys - LEN
    cols = slice(head * HEAD_DIM, (head + 1) * HEAD_DIM)

    @pl.when(step == 0)
    def _():
        dk_acc[...] = jnp.zeros_like(dk_acc)
        dv_acc[...] = jnp.zeros_like(dv_acc)
        dt_acc[...] = jnp.zeros_like(dt_acc)
        sum_ref[...] = jnp.zeros_like(sum_ref)

    start = pl.multiple_of(LEN - TQ - step * TQ, TQ)
    start_c = pl.multiple_of(LEN + prompt + start, TQ)
    lane = lax.broadcasted_iota(jnp.int32, (TQ, HEAD_DIM), 1)
    segment_id = qinfo_ref[:, 2:3]
    segments = []
    for s in range(2):
        rows = slice(s * TQ, (s + 1) * TQ)
        content, position, with_segment = query_terms(head, s, q_ref, bias_ref)
        cw[rows, :] = reverse_rows(content).astype(jnp.bfloat16)
        cr[rows, :] = reverse_rows(position).astype(jnp.bfloat16)
        segments.append(reverse_rows(with_segment))
        grad = ag_ref[0, 0, :, s * HEAD_DIM : (s + 1) * HEAD_DIM].astype(jnp.float32)
        inverse = a_ref[0, s, :, HEAD_DIM : HEAD_DIM + 1] * scale_factor
        delta = jnp.sum(grad * a_ref[0, s, :, :HEAD_DIM], axis=1, keepdims=True) * inverse
        delta_high = delta.astype(jnp.bfloat16).astype(jnp.float32)
        extra = jnp.where(lane == 0, -delta_high, jnp.where(lane == 1, delta_high - delta, 0.0))
        agaug[rows, :HEAD_DIM] = reverse_rows(grad * inverse).astype(jnp.bfloat16)
        agaug[rows, HEAD_DIM:] = reverse_rows(extra).astype(jnp.bfloat16)
    share_grad = mm(agaug[...], vaug_ref[0], NT)
    g_all[...] = (p_ref[0, 0].astype(jnp.float32) * share_grad).astype(jnp.bfloat16)
    for s in range(2):
        rows = slice(s * TQ, (s + 1) * TQ)
        blank = jnp.zeros((TQ, TQ), jnp.bfloat16)
        wide_p = jnp.concatenate([g_all[rows, :prompt], blank], axis=1)
        wide_c = jnp.concatenate([g_all[rows, prompt:], blank], axis=1)
        band_p[rows, :] = pltpu.roll(wide_p, 0, axis=1, stride=1, stride_axis=0)
        band_c[rows, :] = pltpu.roll(wide_c, 0, axis=1, stride=1, stride_axis=0)
    dv_acc[...] += mm(agaug[:, :HEAD_DIM], p_ref[0, 0], TN)
    dk_acc[...] += mm(cw[...], g_all[...], TN)
    dt_acc[:, pl.ds(start, TQ + prompt)] += mm(cr[...], band_p[...], TN)
    dt_acc[:, pl.ds(start_c, TQ + LEN)] += mm(cr[...], band_c[...], TN)
    query_content = mm(g_all[...], kaug_ref[0])
    query_position = mm(band_p[...], table_ref[0, pl.ds(start, TQ + prompt), :])
    query_position += mm(band_c[...], table_ref[0, pl.ds(start_c, TQ + LEN), :])
    same_vector = bias_ref[3:4, cols]
    other_vector = bias_ref[4:5, cols]

    def add_row(row, value):
        sum_ref[row : row + 1, :] += jnp.sum(value, axis=0, keepdims=True)

    for s in range(2):
        rows = slice(s * TQ, (s + 1) * TQ)
        from_content = query_content[rows, :HEAD_DIM]
        extra = query_content[rows, HEAD_DIM:]
        hit = (lane == segment_id) & (lane < SEGMENTS)
        same = jnp.sum(jnp.where(hit, extra, 0.0), axis=1, keepdims=True)
        other = extra[:, COL_ONE - HEAD_DIM : COL_ONE - HEAD_DIM + 1] - same
        from_segment = same * same_vector + other * other_vector
        from_position = query_position[rows, :]
        total = reverse_rows(from_content + from_position + from_segment)
        dq_ref[0, :, s * HEAD_DIM : (s + 1) * HEAD_DIM] = total.astype(jnp.bfloat16)
        add_row(0, from_content)
        add_row(1, from_position)
        add_row(2, from_segment)
        add_row(3, same * segments[s])
        add_row(4, other * segments[s])

    @pl.when(step == pl.num_programs(0) - 1)
    def _():
        dkv_ref[:, :HEAD_DIM] = dk_acc[...].T.astype(jnp.bfloat16)
        dkv_ref[:, HEAD_DIM:] = (dv_acc[...].T * HEAD_DIM**0.5).astype(jnp.bfloat16)
        dt_ref[...] = dt_acc[...].T.astype(jnp.bfloat16)


def whole(shape):
    return pl.BlockSpec(shape, lambda i: (0,) * len(shape))


def attend_forward(q, k, v, rt, bias, qinfo, kinfo, ranks, tokens):
    keys, width = k.shape
    table = rt.shape[0]
    steps = LEN // TQ
    heads = width // HEAD_DIM
    per = tokens // TQ
    return pl.pallas_call(
        forward_kernel,
        grid=(steps,),
        in_specs=[
            pl.BlockSpec((2, TQ, width), lambda i: (0, i, 0)),
            whole((keys, width)),
            whole((keys, width)),
            whole((table, width)),
            whole(bias.shape),
            pl.BlockSpec((TQ, qinfo.shape[1]), lambda i: (i, 0)),
            whole(kinfo.shape),
            whole(ranks.shape),
        ],
        out_specs=[
            pl.BlockSpec((heads, 1, 2 * TQ, keys), lambda i: (0, i, 0, 0)),
            pl.BlockSpec((heads, 2, TQ, 2 * HEAD_DIM), lambda i: (0, 0, i, 0)),
            pl.BlockSpec((1, heads, TQ, 2 * HEAD_DIM), lambda i: (i // per, 0, i % per, 0)),
            whole((heads, keys, 2 * HEAD_DIM)),
            whole((heads, keys, 2 * HEAD_DIM)),
            whole((heads, table, HEAD_DIM)),
        ],
        out_shape=[
            jax.ShapeDtypeStruct((heads, steps, 2 * TQ, keys), jnp.bfloat16),
            jax.ShapeDtypeStruct((heads, 2, LEN, 2 * HEAD_DIM), jnp.float32),
            jax.ShapeDtypeStruct((LEN // tokens, heads, tokens, 2 * HEAD_DIM), jnp.bfloat16),
            jax.ShapeDtypeStruct((heads, keys, 2 * HEAD_DIM), jnp.bfloat16),
            jax.ShapeDtypeStruct((heads, keys, 2 * HEAD_DIM), jnp.bfloat16),
            jax.ShapeDtypeStruct((heads, table, HEAD_DIM), jnp.bfloat16),
        ],
        scratch_shapes=[pltpu.VMEM((TQ, 2 * HEAD_DIM), jnp.bfloat16)],
        compiler_params=pltpu.CompilerParams(vmem_limit_bytes=56 * 2**20),
        cost_estimate=pl.CostEstimate(
            flops=3 * (heads * 6 * 2 * LEN * keys * 256),
            bytes_accessed=3 * (heads * 2 * LEN * keys * 2),
            transcendentals=heads * 2 * LEN * keys,
        ),
        name="attend_forward",
    )(q, k, v, rt, bias, qinfo, kinfo, ranks)


def attend_backward(head, q, bias, qinfo, kaug, vaug, rows_of, p, a, ag):
    _, keys, wide = kaug.shape
    table = rows_of.shape[1]
    width = q.shape[2]
    steps = LEN // TQ
    prompt = keys - LEN
    members, heads, tokens, _ = ag.shape
    per = tokens // TQ

    def one(shape):
        return pl.BlockSpec((1,) + shape, lambda i: (head,) + (0,) * len(shape))

    return pl.pallas_call(
        partial(backward_kernel, head),
        grid=(steps,),
        in_specs=[
            pl.BlockSpec((2, TQ, width), lambda i: (0, i, 0)),
            whole(bias.shape),
            pl.BlockSpec((TQ, qinfo.shape[1]), lambda i: (i, 0)),
            one((keys, wide)),
            one((keys, wide)),
            one((table, HEAD_DIM)),
            pl.BlockSpec((1, 1, 2 * TQ, keys), lambda i: (head, i, 0, 0)),
            pl.BlockSpec((1, 2, TQ, wide), lambda i: (head, 0, i, 0)),
            pl.BlockSpec((1, 1, TQ, wide), lambda i: (i // per, head, i % per, 0)),
        ],
        out_specs=[
            pl.BlockSpec((1, TQ, wide), lambda i: (i // per, i % per, 0)),
            whole((keys, wide)),
            whole((table, HEAD_DIM)),
            whole((8, HEAD_DIM)),
        ],
        out_shape=[
            jax.ShapeDtypeStruct((members, tokens, wide), jnp.bfloat16),
            jax.ShapeDtypeStruct((keys, wide), jnp.bfloat16),
            jax.ShapeDtypeStruct((table, HEAD_DIM), jnp.bfloat16),
            jax.ShapeDtypeStruct((8, HEAD_DIM), jnp.float32),
        ],
        scratch_shapes=[
            pltpu.VMEM((2 * TQ, wide), jnp.bfloat16),
            pltpu.VMEM((2 * TQ, HEAD_DIM), jnp.bfloat16),
            pltpu.VMEM((2 * TQ, HEAD_DIM), jnp.bfloat16),
            pltpu.VMEM((2 * TQ, keys), jnp.bfloat16),
            pltpu.VMEM((2 * TQ, TQ + prompt), jnp.bfloat16),
            pltpu.VMEM((2 * TQ, TQ + LEN), jnp.bfloat16),
            pltpu.VMEM((HEAD_DIM, keys), jnp.float32),
            pltpu.VMEM((HEAD_DIM, keys), jnp.float32),
            pltpu.VMEM((HEAD_DIM, table), jnp.float32),
        ],
        compiler_params=pltpu.CompilerParams(vmem_limit_bytes=56 * 2**20),
        cost_estimate=pl.CostEstimate(
            flops=3 * (12 * 2 * LEN * keys * 256), bytes_accessed=3 * (2 * LEN * keys * 2), transcendentals=0
        ),
        name="attend_backward",
    )(q, bias, qinfo, kaug, vaug, rows_of, p, a, ag)


def table_kernel(shards, place_ref, *refs):
    pieces, small, rest = refs[:shards], refs[shards : 2 * shards], refs[2 * shards :]
    (
        coarse_ref, fine_ref, weight_ref, rt_ref, position_ref, vector_ref, inner_ref, bias_ref,
        held, sem,
    ) = rest
    _, rows, width = pieces[0].shape
    shard, member = place_ref[0], place_ref[1]
    copies = []
    for m in range(shards):
        spot = pl.multiple_of((shard ^ m) * rows, rows)
        copies.append(
            pltpu.make_async_copy(pieces[m], weight_ref.at[:, pl.ds(spot, rows), :], sem.at[m])
        )
    for copy in copies:
        copy.start()
    for m in range(shards):
        held[m] = small[m][...].astype(jnp.float32)
    bias_ref[...] = held[shard ^ member][0:8, :]
    for w in range(shards):
        block = held[shard ^ w]
        at = slice(w * width, (w + 1) * width)
        vector_ref[0:5, at] = block[5:10, :]
        for j in range(4):
            spot = (w * 4 + j) * width
            inner_ref[0:1, spot : spot + width] = block[10 + j : 11 + j, :]
    half = fine_ref.shape[2]
    fine_sin, fine_cos = fine_ref[0], fine_ref[1]
    step = 64

    def build(i, carry):
        at = pl.ds(pl.multiple_of(i * step, step), step)
        coarse_sin, coarse_cos = coarse_ref[0, pl.ds(i, 1), :], coarse_ref[1, pl.ds(i, 1), :]
        position_ref[at, :half] = (coarse_sin * fine_cos - coarse_cos * fine_sin).astype(
            jnp.bfloat16
        )
        position_ref[at, half:] = (coarse_cos * fine_cos + coarse_sin * fine_sin).astype(
            jnp.bfloat16
        )
        return carry

    lax.fori_loop(0, position_ref.shape[0] // step, build, 0)
    for copy in copies:
        copy.wait()
    block = 256
    relative = weight_ref[3]

    def body(i, carry):
        at = pl.ds(pl.multiple_of(i * block, block), block)
        rt_ref[at, :] = mm(position_ref[at, :], relative).astype(jnp.bfloat16)
        return carry

    lax.fori_loop(0, position_ref.shape[0] // block, body, 0)


def project_table(place, pieces, small, coarse, fine):
    _, rows, width = pieces[0].shape
    shards = len(pieces)
    table = coarse.shape[1] * fine.shape[1]
    vmem = pl.BlockSpec(memory_space=pltpu.VMEM)
    return pl.pallas_call(
        partial(table_kernel, shards),
        in_specs=[pl.BlockSpec(memory_space=pltpu.SMEM)]
        + [pl.BlockSpec(memory_space=pl.ANY)] * shards
        + [vmem] * (shards + 2),
        out_specs=[vmem] * 6,
        out_shape=[
            jax.ShapeDtypeStruct((4, shards * rows, width), jnp.bfloat16),
            jax.ShapeDtypeStruct((table, width), jnp.bfloat16),
            jax.ShapeDtypeStruct((table, D), jnp.bfloat16),
            jax.ShapeDtypeStruct((8, D), jnp.float32),
            jax.ShapeDtypeStruct((1, 4 * D), jnp.float32),
            jax.ShapeDtypeStruct((8, width), jnp.float32),
        ],
        scratch_shapes=[
            pltpu.VMEM((shards,) + small[0].shape, jnp.float32),
            pltpu.SemaphoreType.DMA((shards,)),
        ],
        compiler_params=pltpu.CompilerParams(vmem_limit_bytes=48 * 2**20),
        name="project_table",
    )(place, *pieces, *small, coarse, fine)


def states_kernel(members, place_ref, *refs):
    pieces, (prompt_ref, weight_ref, q_ref, k_ref, v_ref, states_ref, sem) = (
        (refs[:members], refs[members : 2 * members]),
        refs[2 * members :],
    )
    tokens = pieces[0][0].shape[0]
    prompt = prompt_ref.shape[0]
    copies = [pltpu.make_async_copy(prompt_ref, states_ref.at[pl.ds(0, prompt)], sem.at[0])]
    for s in range(2):
        for m, piece in enumerate(pieces[s]):
            spot = prompt + s * LEN + pl.multiple_of((place_ref[1] ^ m) * tokens, tokens)
            copies.append(
                pltpu.make_async_copy(
                    piece, states_ref.at[pl.ds(spot, tokens)], sem.at[1 + 2 * m + s]
                )
            )
    for copy in copies:
        copy.start()
    for copy in copies:
        copy.wait()
    step = 256
    query, key, value = weight_ref[0], weight_ref[1], weight_ref[2]
    for i in range(2 * LEN // step):
        rows = states_ref[prompt + i * step : prompt + (i + 1) * step, :]
        stream, at = divmod(i * step, LEN)
        q_ref[stream, at : at + step, :] = mm(rows, query).astype(jnp.bfloat16)
    for i in range((prompt + LEN) // step):
        rows = states_ref[i * step : (i + 1) * step, :]
        k_ref[i * step : (i + 1) * step, :] = mm(rows, key).astype(jnp.bfloat16)
        v_ref[i * step : (i + 1) * step, :] = mm(rows, value).astype(jnp.bfloat16)


def project_states(place, content, query, prompt_all, weights):
    members = len(content)
    width = weights.shape[2]
    prompt = prompt_all.shape[0]
    return pl.pallas_call(
        partial(states_kernel, members),
        in_specs=[pl.BlockSpec(memory_space=pltpu.SMEM)]
        + [pl.BlockSpec(memory_space=pl.ANY)] * (2 * members + 1)
        + [pl.BlockSpec(memory_space=pltpu.VMEM)],
        out_specs=[pl.BlockSpec(memory_space=pltpu.VMEM)] * 4,
        out_shape=[
            jax.ShapeDtypeStruct((2, LEN, width), jnp.bfloat16),
            jax.ShapeDtypeStruct((prompt + LEN, width), jnp.bfloat16),
            jax.ShapeDtypeStruct((prompt + LEN, width), jnp.bfloat16),
            jax.ShapeDtypeStruct((prompt + 2 * LEN, D), jnp.bfloat16),
        ],
        scratch_shapes=[pltpu.SemaphoreType.DMA((1 + 2 * members,))],
        compiler_params=pltpu.CompilerParams(vmem_limit_bytes=48 * 2**20),
        name="project_states",
    )(place, *content, *query, prompt_all, weights)


def normalise(x):
    center = x - jnp.mean(x, axis=1, keepdims=True)
    inverse = lax.rsqrt(jnp.mean(center * center, axis=1, keepdims=True) + epsilon)
    return center * inverse, inverse


def norm_backward(grad, unit, inverse, gain):
    scaled = grad * gain
    mean = jnp.mean(scaled, axis=1, keepdims=True)
    along = jnp.mean(scaled * unit, axis=1, keepdims=True)
    return (scaled - mean - unit * along) * inverse


def layer_kernel(
    place_ref, a_ref, content_ref, query_ref, up_content_ref, up_query_ref, vector_ref, inner_ref,
    output_hbm, hidden_hbm, return_hbm,
    out_content_ref, out_query_ref, keep_ref, send_ref, residual_ref, ag_ref, sum_ref,
    inner_sum_ref,
    output_w, hidden_w, return_w, flat, inner_in, active_ref, returned_ref, zgrad_ref, branch_ref,
    slope, acc, unit, sem,
):
    members, heads, tokens, _ = a_ref.shape
    pairs = keep_ref.shape[0]
    rows_w = keep_ref.shape[1] // 9
    copies = [
        pltpu.make_async_copy(output_hbm, output_w, sem.at[0]),
        pltpu.make_async_copy(hidden_hbm, hidden_w, sem.at[1]),
        pltpu.make_async_copy(return_hbm, return_w, sem.at[2]),
    ]
    for copy in copies:
        copy.start()
    for g in range(members):
        for h in range(heads):
            spot = (g * heads + h) * HEAD_DIM
            for s in range(2):
                flat[s * tokens : (s + 1) * tokens, spot : spot + HEAD_DIM] = a_ref[
                    g, h, :, s * HEAD_DIM : (s + 1) * HEAD_DIM
                ]
    gain, shift, outer, final_gain, final_shift = (vector_ref[i : i + 1, :] for i in range(5))
    copies[0].wait()
    inverses = []
    for s, source in enumerate((content_ref, query_ref)):
        at = slice(s * tokens, (s + 1) * tokens)
        mixed = mm(flat[at, :], output_w[...])
        normal, inverse = normalise(source[...].astype(jnp.float32) + mixed)
        inverses.append(inverse)
        unit[at, :] = normal
        middle = normal * gain + shift
        inner_in[at, :] = middle.astype(jnp.bfloat16)
        acc[at, :] = middle + outer
    copies[1].wait()
    copies[2].wait()
    step = 1024
    chunks = hidden_w.shape[1] // step
    root = 0.7978845608028654

    def forward(i, carry):
        at = pl.ds(pl.multiple_of(i * step, step), step)
        for s in range(2):
            part = slice(s * tokens, (s + 1) * tokens)
            z = mm(inner_in[part, :], hidden_w[:, at]) + inner_ref[:, at]
            square = z * z
            curve = jnp.tanh(root * (z + 0.044715 * (z * square)))
            half = 0.5 + 0.5 * curve
            active = (z * half).astype(jnp.bfloat16)
            slope[part, at] = half + (0.5 * root) * z * (1.0 - curve * curve) * (
                1.0 + (3 * 0.044715) * square
            )
            active_ref[part, at] = active
            acc[part, :] += mm(active, return_w[at, :])
        return carry

    lax.fori_loop(0, chunks, forward, 0, unroll=True)
    sums = []
    for s, (upstream, result) in enumerate(
        ((up_content_ref, out_content_ref), (up_query_ref, out_query_ref))
    ):
        at = slice(s * tokens, (s + 1) * tokens)
        normal, inverse = normalise(acc[at, :])
        result[...] = (normal * final_gain + final_shift).astype(jnp.bfloat16)
        grad = upstream[...].astype(jnp.float32)
        back = norm_backward(grad, normal, inverse, final_gain)
        low = back.astype(jnp.bfloat16)
        returned_ref[at, :] = low
        acc[at, :] = back
        sums.append(
            [
                jnp.sum(low.astype(jnp.float32), axis=0, keepdims=True),
                jnp.sum(grad * normal, axis=0, keepdims=True),
                jnp.sum(grad, axis=0, keepdims=True),
            ]
        )
    for i in range(3):
        sum_ref[2 + i : 3 + i, :] = sums[0][i] + sums[1][i]

    def backward(i, carry):
        at = pl.ds(pl.multiple_of(i * step, step), step)
        total = jnp.zeros((1, step), jnp.float32)
        for s in range(2):
            part = slice(s * tokens, (s + 1) * tokens)
            grad = mm(returned_ref[part, :], return_w[at, :], NT) * slope[part, at]
            low = grad.astype(jnp.bfloat16)
            zgrad_ref[part, at] = low
            total += jnp.sum(low.astype(jnp.float32), axis=0, keepdims=True)
            acc[part, :] += mm(low, hidden_w[:, at], NT)
        inner_sum_ref[:, at] = total
        return carry

    lax.fori_loop(0, chunks, backward, 0, unroll=True)
    sums = []
    for s in range(2):
        at = slice(s * tokens, (s + 1) * tokens)
        grad = acc[at, :]
        normal = unit[at, :]
        back = norm_backward(grad, normal, inverses[s], gain)
        residual_ref[at, :] = back
        low = back.astype(jnp.bfloat16)
        branch_ref[at, :] = low
        sums.append(
            [
                jnp.sum(grad * normal, axis=0, keepdims=True),
                jnp.sum(grad, axis=0, keepdims=True),
            ]
        )
        mixed = mm(low, output_w[...], NT).astype(jnp.bfloat16)
        for g in range(members):
            for h in range(heads):
                spot = (g * heads + h) * HEAD_DIM
                ag_ref[g, h, :, s * HEAD_DIM : (s + 1) * HEAD_DIM] = mixed[
                    :, spot : spot + HEAD_DIM
                ]
    for i in range(2):
        sum_ref[i : i + 1, :] = sums[0][i] + sums[1][i]

    own = place_ref[0] & 1

    def store(pair, block, even, odd):
        at = slice(block * rows_w, (block + 1) * rows_w)
        keep_ref[pair, at, :] = jnp.where(own == 0, even, odd).astype(jnp.bfloat16)
        send_ref[pair, at, :] = jnp.where(own == 0, odd, even).astype(jnp.bfloat16)

    def store_rows(block, value):
        for pair in range(pairs):
            at = 2 * pair * rows_w
            store(pair, block, value[at : at + rows_w], value[at + rows_w : at + 2 * rows_w])

    wide = 2 * D
    for j in range(hidden_w.shape[1] // wide):
        value = mm(inner_in[...], zgrad_ref[:, j * wide : (j + 1) * wide], TN)
        for i in range(2):
            store_rows((0, 1, 2, 6)[2 * j + i], value[:, i * D : (i + 1) * D])
    rows = 4 * rows_w
    for pair in range(pairs):
        even, odd = (
            mm(active_ref[:, w * rows : (w + 1) * rows], returned_ref[...], TN)
            for w in (2 * pair, 2 * pair + 1)
        )
        for i in range(4):
            at = slice(i * rows_w, (i + 1) * rows_w)
            store(pair, (3, 4, 5, 7)[i], even[at], odd[at])
    store_rows(8, mm(flat[...], branch_ref[...], TN))


def layer(place, shards, a, *operands):
    content, hidden_w = operands[0], operands[-2]
    tokens = content.shape[0]
    rows = 2 * tokens
    hidden = hidden_w.shape[1]
    vmem = pl.BlockSpec(memory_space=pltpu.VMEM)
    low = partial(jax.ShapeDtypeStruct, dtype=jnp.bfloat16)
    wide = partial(jax.ShapeDtypeStruct, dtype=jnp.float32)
    grads = low((shards // 2, 9 * D // shards, D))
    return pl.pallas_call(
        layer_kernel,
        in_specs=[pl.BlockSpec(memory_space=pltpu.SMEM)]
        + [vmem] * 7
        + [pl.BlockSpec(memory_space=pl.ANY)] * 3,
        out_specs=[vmem] * 8,
        out_shape=[
            low((tokens, D)),
            low((tokens, D)),
            grads,
            grads,
            wide((rows, D)),
            low(a.shape),
            wide((5, D)),
            wide((1, hidden)),
        ],
        scratch_shapes=[
            pltpu.VMEM((D, D), jnp.bfloat16),
            pltpu.VMEM((D, hidden), jnp.bfloat16),
            pltpu.VMEM((hidden, D), jnp.bfloat16),
            pltpu.VMEM((rows, D), jnp.bfloat16),
            pltpu.VMEM((rows, D), jnp.bfloat16),
            pltpu.VMEM((rows, hidden), jnp.bfloat16),
            pltpu.VMEM((rows, D), jnp.bfloat16),
            pltpu.VMEM((rows, hidden), jnp.bfloat16),
            pltpu.VMEM((rows, D), jnp.bfloat16),
            pltpu.VMEM((rows, hidden), jnp.float32),
            pltpu.VMEM((rows, D), jnp.float32),
            pltpu.VMEM((rows, D), jnp.float32),
            pltpu.SemaphoreType.DMA((3,)),
        ],
        compiler_params=pltpu.CompilerParams(vmem_limit_bytes=60 * 2**20),
        cost_estimate=pl.CostEstimate(
            flops=3 * (12 * rows * D * hidden), bytes_accessed=3 * (24 * 2**20), transcendentals=rows * hidden
        ),
        name="layer",
    )(place, a, *operands)


def part_kernel(
    place_ref, own_ref, other_ref, keep_y, send_y, keep_x, send_x, keep_z, send_z
):
    step = pl.program_id(0)
    count = own_ref.shape[1] // 3
    chains = [
        (
            own_ref[0, i * count : (i + 1) * count, :].astype(jnp.float32)
            + other_ref[0, i * count : (i + 1) * count, :].astype(jnp.float32)
        )
        for i in range(3)
    ]
    half = count // 2
    own_y, own_x, own_z = place_ref[0], place_ref[1], place_ref[2]

    @pl.when(step == own_y)
    def _():
        keep_y[0] = chains[0].astype(jnp.bfloat16)

    @pl.when(step != own_y)
    def _():
        send_y[0] = chains[0].astype(jnp.bfloat16)

    for chain, own, keep, send in (
        (chains[1], own_x, keep_x, send_x),
        (chains[2], own_z, keep_z, send_z),
    ):
        keep[0] = jnp.where(own == 0, chain[:half], chain[half:]).astype(jnp.bfloat16)
        send[0] = jnp.where(own == 0, chain[half:], chain[:half]).astype(jnp.bfloat16)


def part(place, own, other):
    pairs, rows, _ = own.shape
    count = rows // 3
    low = partial(jax.ShapeDtypeStruct, dtype=jnp.bfloat16)
    both = pl.BlockSpec((1, rows, D), lambda i, c: (i, 0, 0))
    return pl.pallas_call(
        part_kernel,
        grid_spec=pltpu.PrefetchScalarGridSpec(
            num_scalar_prefetch=1,
            grid=(pairs,),
            in_specs=[both, both],
            out_specs=[pl.BlockSpec((1, count, D), lambda i, c: (0, 0, 0))] * 2
            + [pl.BlockSpec((1, count // 2, D), lambda i, c: (i, 0, 0))] * 4,
        ),
        out_shape=[low((1, count, D))] * 2 + [low((pairs, count // 2, D))] * 4,
        compiler_params=pltpu.CompilerParams(vmem_limit_bytes=56 * 2**20),
        cost_estimate=pl.CostEstimate(
            flops=3 * (pairs * rows * D), bytes_accessed=3 * (6 * pairs * rows * D), transcendentals=0
        ),
        name="part",
    )(place, own, other)


def unpack_tokens_kernel(members, head_count, place_ref, *refs):
    pieces, (hidden_ref, return_ref, output_ref, held) = refs[: 2 * members], refs[2 * members :]
    rows_w = hidden_ref.shape[0]
    chains, per, _ = held.shape[1:]
    for m in range(members):
        held[m, : chains - 1] = pieces[m][...]
        held[m, chains - 1 :] = pieces[members + m][...]
    member = place_ref[1]
    for g in range(members):
        head, half = g % head_count, g // head_count
        for c in range(chains):
            if c == 2:
                spot = (half * head_count + head) * per
            else:
                spot = (head * (members // head_count) + half) * per
            row = c * members * per + spot
            done = 0
            while done < per:
                block, at = divmod(row + done, rows_w)
                count = min(per - done, rows_w - at)
                value = held[member ^ g, c, done : done + count, :].astype(jnp.float32)
                if block == 8:
                    output_ref[at : at + count, :] = value
                elif block in (0, 1, 2, 6):
                    j = min(block, 3)
                    hidden_ref[at : at + count, j * D : (j + 1) * D] = value
                else:
                    j = min(block - 3, 3)
                    return_ref[j * rows_w + at : j * rows_w + at + count, :] = value
                done += count


def unpack_tokens(place, rows_w, head_count, early, late):
    members = len(early)
    vmem = pl.BlockSpec(memory_space=pltpu.VMEM)
    chains = early[0].shape[0] + late[0].shape[0]
    return pl.pallas_call(
        partial(unpack_tokens_kernel, members, head_count),
        in_specs=[pl.BlockSpec(memory_space=pltpu.SMEM)] + [vmem] * 2 * members,
        out_specs=[vmem] * 3,
        out_shape=[
            jax.ShapeDtypeStruct((rows_w, 4 * D), jnp.float32),
            jax.ShapeDtypeStruct((4 * rows_w, D), jnp.float32),
            jax.ShapeDtypeStruct((rows_w, D), jnp.float32),
        ],
        scratch_shapes=[pltpu.VMEM((members, chains) + early[0].shape[1:], jnp.bfloat16)],
        compiler_params=pltpu.CompilerParams(vmem_limit_bytes=48 * 2**20),
        name="unpack_tokens",
    )(place, *early, *late)


def head_grads_kernel(shards, heads, place_ref, states_ref, position_ref, *rest):
    dq, dkv, dt = (rest[i * heads : (i + 1) * heads] for i in range(3))
    small, out_ref = rest[3 * heads : -1], rest[-1]
    keys = dkv[0].shape[0]
    prompt = keys - LEN
    rows_w = D // shards
    wide = 2 * HEAD_DIM
    side = partial(jnp.concatenate, axis=1)
    dq = side([ref[...].reshape(LEN, wide) for ref in dq])
    key_value = mm(side([ref[...] for ref in dkv]), states_ref[:keys, :], TN)
    content = mm(dq, states_ref[prompt:keys, :], TN)
    query = mm(dq, states_ref[keys:, :], TN)
    table = mm(side([ref[...] for ref in dt]), position_ref[...], TN)
    parts = []
    for h in range(heads):
        at = h * wide
        parts += [
            content[at : at + HEAD_DIM] + query[at + HEAD_DIM : at + wide],
            key_value[at : at + wide],
            table[h * HEAD_DIM : (h + 1) * HEAD_DIM],
        ]
    turned = jnp.concatenate(parts, axis=0).T.astype(jnp.bfloat16)
    for w in range(shards):
        out_ref[w, :rows_w, :] = turned[w * rows_w : (w + 1) * rows_w, :]
    if small:
        token_ref, inner_ref, sums = small[0], small[1], small[2:]
        member = place_ref[1]
        out_ref[:, rows_w:, :] = jnp.zeros_like(out_ref[:, rows_w:, :])
        own_sums = side([ref[0:5, :] for ref in sums])
        for w in range(shards):
            own = jnp.where(member == w, own_sums, 0.0)
            parts = [token_ref[0:5, w * rows_w : (w + 1) * rows_w], own]
            parts += [
                inner_ref[0:1, (4 * w + j) * rows_w : (4 * w + j + 1) * rows_w] for j in range(4)
            ]
            parts.append(jnp.zeros((2, rows_w), jnp.float32))
            out_ref[w, rows_w : rows_w + 16, :rows_w] = jnp.concatenate(parts, axis=0).astype(
                jnp.bfloat16
            )


def head_grads(place, shards, states, positions, dq, dkv, dt, small=()):
    vmem = pl.BlockSpec(memory_space=pltpu.VMEM)
    heads = len(dq)
    operands = (states, positions) + tuple(dq) + tuple(dkv) + tuple(dt) + tuple(small)
    rows = D // shards + (16 if small else 0)
    return pl.pallas_call(
        partial(head_grads_kernel, shards, heads),
        in_specs=[pl.BlockSpec(memory_space=pltpu.SMEM)] + [vmem] * len(operands),
        out_specs=vmem,
        out_shape=jax.ShapeDtypeStruct((shards, rows, 4 * HEAD_DIM * heads), jnp.bfloat16),
        compiler_params=pltpu.CompilerParams(vmem_limit_bytes=56 * 2**20),
        cost_estimate=pl.CostEstimate(
            flops=3 * (2 * 6656 * D * 256), bytes_accessed=3 * (12 * 2**20), transcendentals=0
        ),
        name="head_grads",
    )(place, *operands)


def unpack_kernel(members, groups, place_ref, *refs):
    pieces = [refs[i * members : (i + 1) * members] for i in range(groups)]
    outs = refs[groups * members : groups * members + 4]
    small_ref = refs[groups * members + 4]
    held = refs[groups * members + 5 : groups * members + 5 + groups]
    rows_w = outs[0].shape[0]
    for i in range(groups):
        for m in range(members):
            held[i][m] = pieces[i][m][...]
    member = place_ref[1]
    for g in range(members):
        head = 0
        for i in range(groups):
            block = held[i][member ^ g].astype(jnp.float32)
            for j in range(block.shape[1] // (4 * HEAD_DIM)):
                spot = (g * groups_heads(held) + head) * HEAD_DIM
                for kind in range(4):
                    at = (4 * j + kind) * HEAD_DIM
                    outs[kind][:, spot : spot + HEAD_DIM] = block[:rows_w, at : at + HEAD_DIM]
                head += 1
    last = held[-1]
    total = last[0, rows_w : rows_w + 16, :].astype(jnp.float32)
    for m in range(1, members):
        total += last[m, rows_w : rows_w + 16, :].astype(jnp.float32)
    small_ref[...] = total


def groups_heads(held):
    return sum(ref.shape[2] // (4 * HEAD_DIM) for ref in held)


def unpack(place, rows_w, *pieces):
    members = len(pieces[0])
    vmem = pl.BlockSpec(memory_space=pltpu.VMEM)
    flat = [x for group in pieces for x in group]
    return pl.pallas_call(
        partial(unpack_kernel, members, len(pieces)),
        in_specs=[pl.BlockSpec(memory_space=pltpu.SMEM)] + [vmem] * len(flat),
        out_specs=[vmem] * 5,
        out_shape=[jax.ShapeDtypeStruct((rows_w, D), jnp.float32)] * 4
        + [jax.ShapeDtypeStruct((16, 4 * HEAD_DIM), jnp.float32)],
        scratch_shapes=[pltpu.VMEM((members,) + group[0].shape, jnp.bfloat16) for group in pieces],
        compiler_params=pltpu.CompilerParams(vmem_limit_bytes=48 * 2**20),
        name="unpack",
    )(place, *flat)


def finish_kernel(
    early_ref, late_ref, prompt_ref, residual_ref, weight_hbm,
    content_ref, query_ref, out_prompt_ref, weight, parts, prompts, sem,
):
    copy = pltpu.make_async_copy(weight_hbm, weight, sem)
    copy.start()
    members, before, _, _ = early_ref.shape
    tokens = content_ref.shape[0]
    heads = before + late_ref.shape[1]
    for g in range(members):
        for h in range(heads):
            spot = (g * heads + h) * HEAD_DIM
            source, i = (early_ref, h) if h < before else (late_ref, h - before)
            for kind in range(4):
                at = (kind % 2) * HEAD_DIM
                start = (kind // 2) * tokens
                parts[kind, :, spot : spot + HEAD_DIM] = source[
                    g, i, start : start + tokens, at : at + HEAD_DIM
                ]
            for kind in range(2):
                prompts[kind, :, spot : spot + HEAD_DIM] = prompt_ref[
                    g, h, :, kind * HEAD_DIM : (kind + 1) * HEAD_DIM
                ]
    copy.wait()
    query, key, value = (weight[:, i * D : (i + 1) * D] for i in range(3))
    content = residual_ref[:tokens, :] + mm(parts[0], query, NT)
    content += mm(parts[2], key, NT)
    content += mm(parts[3], value, NT)
    content_ref[...] = content.astype(jnp.bfloat16)
    query_ref[...] = (residual_ref[tokens:, :] + mm(parts[1], query, NT)).astype(jnp.bfloat16)
    out_prompt_ref[...] = (mm(prompts[0], key, NT) + mm(prompts[1], value, NT)).astype(
        jnp.bfloat16
    )


def finish(rows_early, rows_late, prompt_back, residual, weights):
    tokens = residual.shape[0] // 2
    prompt = prompt_back.shape[2]
    vmem = pl.BlockSpec(memory_space=pltpu.VMEM)
    return pl.pallas_call(
        finish_kernel,
        in_specs=[vmem] * 4 + [pl.BlockSpec(memory_space=pl.ANY)],
        out_specs=[vmem] * 3,
        out_shape=[
            jax.ShapeDtypeStruct((tokens, D), jnp.bfloat16),
            jax.ShapeDtypeStruct((tokens, D), jnp.bfloat16),
            jax.ShapeDtypeStruct((prompt, D), jnp.bfloat16),
        ],
        scratch_shapes=[
            pltpu.VMEM(weights.shape, jnp.bfloat16),
            pltpu.VMEM((4, tokens, D), jnp.bfloat16),
            pltpu.VMEM((2, prompt, D), jnp.bfloat16),
            pltpu.SemaphoreType.DMA,
        ],
        compiler_params=pltpu.CompilerParams(vmem_limit_bytes=48 * 2**20),
        cost_estimate=pl.CostEstimate(
            flops=3 * (8 * tokens * D * D), bytes_accessed=3 * (8 * 2**20), transcendentals=0
        ),
        name="finish",
    )(rows_early, rows_late, prompt_back, residual, weights)


def axes_size(axes):
    size = 1
    for name in axes:
        size *= lax.axis_size(name)
    return size


def flat_index(axes):
    index = 0
    for name in axes:
        index = index * lax.axis_size(name) + lax.axis_index(name)
    return index


def swap(x, axes, mask):
    return lax.ppermute(x, axes, [(i, i ^ mask) for i in range(axes_size(axes))])


def bits_of(axes):
    return range(axes_size(axes).bit_length() - 1)


def pieces_of(x, axes):
    pieces = {0: x}
    for bit in reversed(bits_of(axes)):
        for mask in list(pieces):
            pieces[mask | 1 << bit] = swap(pieces[mask], axes, 1 << bit)
    return [pieces[m] for m in range(axes_size(axes))]


def in_order(pieces, index):
    count = len(pieces)
    result = jnp.zeros((count,) + pieces[0].shape, pieces[0].dtype)
    for m, piece in enumerate(pieces):
        result = lax.dynamic_update_slice(result, piece[None], (index ^ m,) + (0,) * piece.ndim)
    return result


def pick(x, index, axis=0):
    return lax.dynamic_index_in_dim(x, index, axis, keepdims=False)


def add_low(x, y):
    return (x.astype(jnp.float32) + y.astype(jnp.float32)).astype(jnp.bfloat16)


def half_sum(x, axes, bit, axis):
    own = flat_index(axes) >> bit & 1
    return add_low(pick(x, own, axis), swap(pick(x, 1 - own, axis), axes, 1 << bit))


def split_axis(x, axis):
    return x.reshape(x.shape[:axis] + (2, x.shape[axis] // 2) + x.shape[axis + 1 :])


def stages_of(names):
    return [((name,), bit) for name in names for bit in bits_of((name,))]


def full_sum(x, stages):
    for axes, bit in stages:
        x = add_low(x, swap(x, axes, 1 << bit))
    return x


def group_pieces(x, axes):
    return [x] + [swap(x, axes, m) for m in range(1, axes_size(axes))]


def back_through(grad_rows, weight):
    return jnp.einsum("rc,dc->rd", grad_rows, weight, preferred_element_type=jnp.float32)


def outer_sum(rows_in, grad_rows):
    return jnp.einsum("rd,rc->dc", rows_in, grad_rows, preferred_element_type=jnp.float32)


def sinusoid_rows(first, rows):
    frequency = jnp.asarray(
        np.power(10000.0, -2.0 * np.arange(D // 2) / D).astype(np.float32)
    )
    fine = jnp.arange(64, dtype=jnp.float32)[:, None] * frequency
    coarse = (first - 64 * jnp.arange(rows // 64, dtype=jnp.int32)).astype(jnp.float32)
    coarse = coarse[:, None] * frequency
    fs, fc = jnp.sin(fine)[None], jnp.cos(fine)[None]
    cs, cc = jnp.sin(coarse)[:, None], jnp.cos(coarse)[:, None]
    both = jnp.concatenate([cs * fc - cc * fs, cc * fc + cs * fs], axis=-1)
    return both.reshape(rows, D).astype(jnp.bfloat16)


GROUP = ("half", "head")
JOB = ("cont", "half", "head")
SHARD = ("wshard",)


def per_device(
    prompt_states, content_states, query_states, visible_length, start_offsets,
    prompt_segments, token_segments, order_ranks,
    query_weights, key_weights, value_weights, output_weights, relative_weights,
    content_bias, position_bias, segment_bias, segment_vectors,
    attention_gain, attention_shift, hidden_weights, hidden_bias, return_weights, return_bias,
    final_gain, final_shift, content_upstream, query_upstream,
):
    members = axes_size(GROUP)
    member = flat_index(GROUP)
    shards = lax.axis_size("wshard")
    shard = lax.axis_index("wshard")
    chapters = lax.axis_size("cont")
    chapter = lax.axis_index("cont")
    width = D // members
    local_heads = HEADS // members
    content_rows = content_states[0]
    query_rows = query_states[0]
    tokens = content_rows.shape[0]
    prompt_part = prompt_states.shape[1]
    prompt_total = prompt_segments.shape[1]
    keys = prompt_total + LEN
    rows_w = query_weights.shape[0]

    def columns(x):
        return lax.dynamic_slice_in_dim(x, member * width, width, x.ndim - 1)

    tie = lax.optimization_barrier

    content = {0: content_rows}
    query = {0: query_rows}
    content[1], query[2] = swap(content_rows, GROUP, 1), swap(query_rows, GROUP, 2)
    first_weights = jnp.stack(
        [columns(w) for w in (query_weights, key_weights, value_weights, relative_weights)], axis=0
    )
    small = jnp.concatenate(
        [
            jnp.stack([content_bias, position_bias, segment_bias]),
            segment_vectors,
            jnp.stack([attention_gain, attention_shift, return_bias, final_gain, final_shift]),
            hidden_bias.reshape(-1, rows_w),
            jnp.zeros((2, rows_w), jnp.bfloat16),
        ],
        axis=0,
    )
    first_pieces = pieces_of(first_weights, SHARD)
    small_pieces = pieces_of(small, SHARD)
    query[1], content[2] = swap(query_rows, GROUP, 1), swap(content_rows, GROUP, 2)
    content[3], query[3] = swap(content[1], GROUP, 2), swap(query[2], GROUP, 1)
    prompt_all = lax.all_to_all(
        jnp.broadcast_to(prompt_states, (chapters * members,) + prompt_states.shape[1:]),
        JOB,
        0,
        0,
        tiled=True,
    ).reshape(prompt_total, D)
    output_full = lax.all_gather(output_weights, "wshard", axis=0, tiled=True)
    hidden_full = lax.all_gather(hidden_weights, "wshard", axis=0, tiled=True)
    return_full = lax.all_gather(return_weights, "wshard", axis=0, tiled=True)
    attention_weights = jnp.concatenate([query_weights, key_weights, value_weights], axis=1)
    attention_full = lax.all_gather(attention_weights, "wshard", axis=0, tiled=True)

    seen = pick(visible_length[0], chapter)
    base = seen + pick(start_offsets[0], chapter)
    segments = lax.dynamic_slice_in_dim(token_segments[0], chapter * LEN, LEN)
    ranks = lax.dynamic_slice_in_dim(order_ranks[0], chapter * LEN, LEN)
    reversed_segments = jnp.flip(segments.reshape(-1, TQ), 1).reshape(-1)
    qinfo = jnp.stack([segments, ranks, reversed_segments, segments], axis=1)
    key_segments = jnp.concatenate([prompt_segments[0], segments])
    hidden_keys = (jnp.arange(keys, dtype=jnp.int32) < prompt_total) & (
        jnp.arange(keys, dtype=jnp.int32) >= seen
    )
    kinfo = jnp.stack([key_segments, hidden_keys.astype(jnp.int32)], axis=1)
    place = jnp.stack([shard, member])

    frequency = jnp.asarray(np.power(10000.0, -2.0 * np.arange(D // 2) / D).astype(np.float32))
    starts = jnp.concatenate(
        [
            base + LEN - 1 - 64 * jnp.arange((LEN + prompt_total) // 64, dtype=jnp.int32),
            LEN - 1 - 64 * jnp.arange(2 * LEN // 64, dtype=jnp.int32),
        ]
    )
    coarse = starts.astype(jnp.float32)[:, None] * frequency
    coarse = jnp.stack([jnp.sin(coarse), jnp.cos(coarse)])
    fine = jnp.arange(64, dtype=jnp.float32)[:, None] * frequency
    fine = jnp.stack([jnp.sin(fine), jnp.cos(fine)])

    first_full, rt, positions, vectors, inner_full, head_bias = project_table(
        place, first_pieces, small_pieces, coarse, fine
    )
    q, k, v, states = project_states(
        place,
        [content[m] for m in range(members)],
        [query[m] for m in range(members)],
        prompt_all,
        first_full,
    )
    p, a, mixture, kaug, vaug, table_rows = attend_forward(
        q, k, v, rt, head_bias, qinfo, kinfo, ranks[None], tokens
    )
    mixture = lax.all_to_all(mixture, GROUP, 0, 0, tiled=True)

    (
        out_content, out_query, kept_grads, sent_grads, residual_grad, grad_out, token_sums,
        inner_bias_grad,
    ) = layer(
        place, shards, mixture, content_rows, query_rows, content_upstream[0], query_upstream[0],
        vectors, inner_full, output_full, hidden_full, return_full,
    )
    grad_out, attention_full = lax.optimization_barrier((grad_out, attention_full))
    grad_out = lax.all_to_all(grad_out, GROUP, 0, 0, tiled=True)

    bits = jnp.stack([shard >> 1, lax.axis_index("head"), lax.axis_index("half")])
    parts = part(bits, kept_grads, swap(sent_grads, SHARD, 1))
    stage_y, stage_x, stage_z = (SHARD, 1), (("head",), 0), (("half",), 0)
    cont_stage = stages_of(("cont",))
    orders = (
        (stage_y, stage_x, stage_z),
        (stage_x, stage_z, stage_y),
        (stage_z, stage_y, stage_x),
    )
    chains = [
        (kept, swap(out, order[0][0], 1 << order[0][1]))
        for kept, out, order in zip(parts[::2], parts[1::2], orders)
    ]

    def next_stage(chain, stage):
        axes, bit = stage
        x = add_low(*chain)
        axis = 0 if axes == SHARD else 1
        x = split_axis(x, axis)
        own = flat_index(axes) >> bit & 1
        return pick(x, own, axis), swap(pick(x, 1 - own, axis), axes, 1 << bit)

    small_grads = (token_sums, inner_bias_grad)

    def attend_back(h, grad_out):
        return attend_backward(h, q, head_bias, qinfo, kaug, vaug, table_rows, p, a, grad_out)

    last = local_heads - 1
    grad_out, parts = tie((grad_out, parts))
    backward = [attend_back(0, grad_out)]
    grad_out, chains = tie((grad_out, chains))
    chains = [next_stage(x, order[1]) for x, order in zip(chains, orders)]
    backward += [attend_back(h, grad_out) for h in range(1, last)]
    backward, chains = tie((backward, chains))
    chains = [next_stage(x, order[2]) for x, order in zip(chains, orders)]
    dq, dkv, dt, _ = zip(*backward)
    x = head_grads(place, shards, states, positions, dq, dkv, dt)
    x, chains, dq, dkv = tie((x, chains, dq, dkv))
    chains = [add_low(*x) for x in chains]

    def shard_stage(x, bit):
        return half_sum(x.reshape((-1, 2) + x.shape[1:]), SHARD, bit, 1)

    def row_parts(heads):
        parts = []
        for h in heads:
            prompts = dkv[h][:prompt_total].reshape(chapters, members, prompt_part, -1)
            prompts = jnp.transpose(prompts, (1, 0, 2, 3)).reshape(members, -1, dq[h].shape[2])
            own = dkv[h][prompt_total:].reshape(dq[h].shape)
            parts.append(jnp.concatenate([dq[h], own, prompts], axis=1))
        return lax.all_to_all(jnp.stack(parts, axis=1), GROUP, 0, 0, tiled=True)

    first = shard_stage(x, 0)
    grad_out, chains, first = tie((grad_out, chains, first))
    early = full_sum(jnp.concatenate(chains[:2]), cont_stage)
    first = shard_stage(first, 1)
    rows_early = row_parts(range(last))
    backward.append(attend_back(last, grad_out))
    backward[last], late, first, early, rows_early = tie(
        (backward[last], chains[2], first, early, rows_early)
    )
    late = full_sum(late, cont_stage)
    first = full_sum(first[0], cont_stage)
    early_x = swap(early, GROUP, 1)
    early_dq, early_dkv = dq, dkv
    dq, dkv, dt, sums = zip(*backward)
    dq, dkv = early_dq + dq[last:], early_dkv + dkv[last:]
    rows_late = row_parts([last])
    x = head_grads(
        place, shards, states, positions, dq[-1:], dkv[-1:], dt[-1:], small_grads + sums
    )
    x, late, rows_late, first, early_x, early = tie((x, late, rows_late, first, early_x, early))
    early_pieces = [early, early_x] + [swap(early, GROUP, m) for m in range(2, members)]
    late_pieces = group_pieces(late, GROUP)
    prompt_back = jnp.concatenate([rows_early[:, :, 2 * tokens :], rows_late[:, :, 2 * tokens :]], 1)
    prompt_back = prompt_back.reshape(prompt_back.shape[:2] + (chapters, prompt_part, -1))
    prompt_back = jnp.transpose(prompt_back, (2, 0, 1, 3, 4))
    second = shard_stage(shard_stage(x, 0), 1)[0]
    first = group_pieces(first, GROUP)
    for axes, bit in reversed(cont_stage):
        halves = split_axis(prompt_back, 0)
        own = flat_index(axes) >> bit & 1
        sent = pick(halves, 1 - own).reshape(2, -1, prompt_back.shape[-1])
        sent = jnp.concatenate([second, jnp.concatenate([sent[0], sent[1]], axis=1)])
        sent = swap(sent, axes, 1 << bit)
        rows = second.shape[0]
        second = add_low(second, sent[:rows])
        half = sent.shape[1] // 2
        other = jnp.stack([sent[rows:, :half], sent[rows:, half:]])
        prompt_back = add_low(pick(halves, own), other.reshape(halves.shape[1:]))
    second, early_pieces, late_pieces[:3] = tie((second, early_pieces, late_pieces[:3]))
    head_pieces = [first, group_pieces(second, GROUP)]

    hidden_total, return_total, output_total = unpack_tokens(
        place, rows_w, lax.axis_size("head"), early_pieces, late_pieces
    )
    query_grad, key_grad, value_grad, relative_grad, small_total = unpack(
        place, rows_w, *head_pieces
    )
    vector_total = small_total[:10, :rows_w]
    inner_total = small_total[10:14, :rows_w].reshape(-1)
    content_grad, queries_grad, prompt_grad = finish(
        rows_early, rows_late, prompt_back[0], residual_grad, attention_full
    )
    return (
        out_content[None],
        out_query[None],
        prompt_grad[None],
        content_grad[None],
        queries_grad[None],
        query_grad,
        key_grad,
        value_grad,
        output_total,
        relative_grad,
        vector_total[5],
        vector_total[6],
        vector_total[7],
        vector_total[8:10],
        vector_total[0],
        vector_total[1],
        hidden_total,
        inner_total,
        return_total,
        vector_total[2],
        vector_total[3],
        vector_total[4],
    )


def solution(mesh):
    rows = P("wshard", JOB, None)
    job = P("wshard", None)
    matrix = P("wshard", None)
    vector = P("wshard")
    pair = P(None, "wshard")
    in_specs = (
        (rows,) * 3 + (job,) * 5 + (matrix,) * 5 + (vector,) * 3 + (pair,)
        + (vector, vector, matrix, vector, matrix, vector, vector, vector, rows, rows)
    )
    out_specs = (
        (rows,) * 5 + (matrix,) * 5 + (vector,) * 3 + (pair,)
        + (vector, vector, matrix, vector, matrix, vector, vector, vector)
    )

    def run(*arguments):
        seq_count, head_count, shard_count = mesh.devices.shape
        tokens = arguments[1].shape[1] // (seq_count * head_count)
        halves = LEN // (tokens * head_count)
        split = Mesh(
            mesh.devices.reshape(seq_count // halves, halves, head_count, shard_count),
            ("cont", "half", "head", "wshard"),
        )
        return jax.shard_map(
            per_device, mesh=split, in_specs=in_specs, out_specs=out_specs, check_vma=False
        )(*arguments)

    return run
```
